32 devices in a mesh: sens: 4 (over x, core), src: 8 (over z, y).
Axes of the slice: x: 2, y: 2, z: 4, core: 2. Of those that a mesh axis runs over, the one named last changes fastest.
Arguments:
- operator: bfloat16 [128, 2, 512, 1024], P(None, None, 'sens', 'src'), may hold values from -0.375 to 0.375
- right_side: float32 [128, 2, 32, 1024], P('sens', None, None, 'src'), may hold values from -6 to 6
- noise_weights: float32 [128, 512], P('src', 'sens'), may hold values from 0.25 to 4
- damping: float32 [128], P('sens'), may hold values from 1 to 16
Outputs:
- solution: float32 [128, 2, 32, 1024], P('sens', None, None, 'src')
- residual: float32 [128, 2, 32, 1024], P('sens', None, None, 'src')
The draws below stay inside these ranges and needn't reach their ends.
All inputs are finite; a program needn't handle non-finite values.
Results may differ from the reference program's by a relative error of at most 0.025.
Values may be sent and summed in bfloat16 or wider, within the bound.
No kernel may reach another device: no remote copies, remote signals or barrier semaphores. Data moves between devices by JAX's collectives and lax.ppermute only.
A program may use at most 128 MiB of HBM per device.

```python
import math
import jax
import jax.numpy as jnp
from jax import lax

FREQS = 128
SENS_DEV = 128
DATASETS = 32
ITERS = 2
SENSORS = 512
SOURCES = 1024
N_SENS = 4


def spiked(values, key, source, target, parts, factor):
    owner, partner = [(jnp.arange(values.shape[dim]) // (values.shape[dim] // parts)).reshape([-1 if axis == dim else 1 for axis in range(values.ndim)]) for dim in (source, target)]
    chosen = jax.random.permutation(key, parts)[partner]
    strong = (owner == chosen) | (owner == (partner + parts // 2) % parts)
    return jnp.where(strong, factor * values, values)


def steps_of(own_key, extent, shards, low, top_value):
    level, own = 1.0, jax.random.fold_in(own_key, 6)
    for dim, shards_of in shards:
        draws = jnp.exp(jax.random.uniform(jax.random.fold_in(own, dim), (shards_of,), jnp.float32, low / len(shards), top_value / len(shards)))
        level = level * jnp.repeat(draws, extent[dim] // shards_of).reshape([-1 if axis == dim else 1 for axis in range(len(extent))])
    return level


def normal_values(own_key, shape, deviation, most, shards=(), dtype=jnp.bfloat16):
    entries = jax.random.normal(own_key, shape, jnp.float32) * deviation
    if len(shards) > 0:
        entries = steps_of(own_key, shape, shards, -0.22, 0.18) * entries
    return jnp.clip(entries, min=-most, max=most).astype(dtype)


def bell_draw_with(key, shape, spread, most, split, heavy, held_as=jnp.bfloat16):
    array = spread * jax.random.normal(key, shape, jnp.float32)
    if split:
        array = array * steps_of(key, shape, split, -0.22, 0.18)
    return jnp.clip(spiked(array, jax.random.fold_in(key, 3), *heavy), -most, most).astype(held_as)


def setup_inputs(seed: int = 0) -> dict:
    splits = jax.random.split(jax.random.key(seed), 5)
    operator = bell_draw_with(splits[0], (FREQS, 2, SENSORS, SOURCES), SENSORS ** -0.5, 0.375, ((2, 4), (3, 8)), (3, 0, 8, 2.0))
    right_side = normal_values(splits[1], (FREQS, 2, DATASETS, SOURCES), 1.0, 6.0, ((0, 4), (3, 8)), jnp.float32)
    noise_weights = jnp.clip(jnp.exp(math.log(4.0) - 2.7725887 * jax.random.uniform(splits[2], (FREQS, SENSORS), jnp.float32) ** steps_of(splits[2], (FREQS, SENSORS), ((0, 8), (1, 4)), -0.2, 0.2)), 0.25, 4.0)
    damping = jnp.clip(jnp.exp(math.log(16.0) - 2.7725887 * jax.random.uniform(splits[3], (FREQS,), jnp.float32) ** steps_of(splits[3], (FREQS,), ((0, 4),), -0.2, 0.2)), 1.0, 16.0)
    return dict(operator=operator, right_side=right_side, noise_weights=noise_weights, damping=damping)


def forward(gmat, vector):
    dims = (((1,), (1,)), ((), ()))

    def multiply(left, right):
        return lax.dot_general(left, right, dims, preferred_element_type=jnp.float32)

    real_part = multiply(vector[0], gmat[0]) - multiply(vector[1], gmat[1])
    imag_part = multiply(vector[1], gmat[0]) + multiply(vector[0], gmat[1])
    return jnp.stack([real_part, imag_part])


def adjoint(gmat, field):
    total = jnp.zeros((2, field.shape[1], gmat.shape[2]), jnp.float32)
    for group in range(N_SENS):
        lower = group * SENS_DEV
        block = gmat[:, lower:lower + SENS_DEV]
        piece = field[:, :, lower:lower + SENS_DEV]
        real_part = jnp.dot(piece[0], block[0], preferred_element_type=jnp.float32) + jnp.dot(piece[1], block[1], preferred_element_type=jnp.float32)
        imag_part = jnp.dot(piece[1], block[0], preferred_element_type=jnp.float32) - jnp.dot(piece[0], block[1], preferred_element_type=jnp.float32)
        partial_sum = lax.optimization_barrier(jnp.stack([real_part, imag_part]).astype(jnp.bfloat16))
        total = total + partial_sum.astype(jnp.float32)
    return total


def hessian(operator, noise_weights, damping, vector):
    rounded = vector.astype(jnp.bfloat16)
    sensor_field = lax.map(lambda pair: forward(pair[0], pair[1]), (operator, rounded))
    weighted = (noise_weights[:, None, None, :] * sensor_field).astype(jnp.bfloat16)
    back = lax.map(lambda pair: adjoint(pair[0], pair[1]), (operator, weighted))
    return back + damping[:, None, None, None] * vector


def reference(operator, right_side, noise_weights, damping):
    solution = jnp.zeros_like(right_side)
    residual = right_side
    direction = right_side
    norm_now = jnp.sum(residual * residual)
    for step in range(ITERS):
        image = hessian(operator, noise_weights, damping, direction)
        alpha = norm_now / jnp.sum(direction * image)
        solution = solution + alpha * direction
        residual = residual - alpha * image
        norm_next = jnp.sum(residual * residual)
        direction = residual + (norm_next / norm_now) * direction
        norm_now = norm_next
    return solution, residual
```

```python
import functools

import jax
import jax.numpy as jnp
from jax import lax
from jax.experimental import pallas as pl
from jax.experimental.pallas import tpu as pltpu
from jax.sharding import PartitionSpec as P

CHUNKS = 2
F32 = jnp.float32
BF16 = jnp.bfloat16
NT = (((1,), (1,)), ((), ()))
NN = (((1,), (0,)), ((), ()))


def largest_divisor(extent, most):
    return next(size for size in range(min(extent, most), 0, -1) if extent % size == 0)


def turned(block, sign):
    half = block.shape[0] // 2
    upper, lower = block[:half], block[half:]
    return jnp.concatenate([-lower, upper] if sign < 0 else [lower, -upper], axis=0)


def forward_rows(vector, near, far):
    left = jnp.concatenate([vector, turned(vector, -1)], axis=1)

    def apply(part):
        right = jnp.concatenate([part[0], part[1]], axis=1)
        return lax.dot_general(left, right, NT, preferred_element_type=F32)

    return jnp.concatenate([apply(near), apply(far)], axis=1)


def adjoint_rows(field, near, far):
    sensors = near.shape[1]
    total = None
    for part, piece in ((near, field[:, :sensors]), (far, field[:, sensors:])):
        left = jnp.concatenate([piece, turned(piece, 1)], axis=1)
        right = part.reshape(2 * sensors, part.shape[2])
        term = lax.dot_general(left, right, NN, preferred_element_type=F32)
        total = term if total is None else total + term
    return total


def cost(flops, moved):
    return pl.CostEstimate(flops=flops, bytes_accessed=moved, transcendentals=0)


class Plan:
    def __init__(self, operator, right_side, n_sens, n_src, chunks):
        self.freqs, _, self.sensors, self.sources = operator.shape
        self.block = right_side.shape[0]
        self.rows = right_side.shape[1] * right_side.shape[2]
        self.pairs = n_sens // 2
        self.groups = n_src // 2
        self.chunks = chunks
        self.part = self.block // chunks
        self.step = largest_divisor(self.part, 4)
        self.steps = self.part // self.step
        self.flops = 16 * self.part * self.rows * self.sensors * self.sources * 2
        self.piece = self.part * self.rows // self.groups


def near_spec(plan, chunk, blk_of):
    return pl.BlockSpec(
        (None, None, plan.step, 2, plan.sensors, plan.sources),
        lambda p, t, m: (m[0] ^ blk_of(p, m), m[1], chunk * plan.steps + t, 0, 0, 0),
    )


def far_spec(plan, blk_of):
    return pl.BlockSpec(
        (None, plan.step, 2, plan.sensors, plan.sources),
        lambda p, t, m: (m[0] ^ blk_of(p, m), t, 0, 0, 0),
    )


def forward_call(plan, chunk, meta, near, far, first, vectors):
    blk_of = lambda p, m: 1 - (m[2] ^ p)
    step, steps = plan.step, plan.steps

    def kernel(m, near_ref, far_ref, one_ref, two_ref, send_ref, keep_ref):
        phase = pl.program_id(0)
        blk = blk_of(phase, m)

        def run(pick, out_ref):
            for f in range(step):
                out_ref[f] = forward_rows(pick(f), near_ref[f], far_ref[f]).astype(out_ref.dtype)

        def both(pick):
            @pl.when(phase == 0)
            def _():
                run(pick, send_ref)

            @pl.when(phase == 1)
            def _():
                run(pick, keep_ref)

        if first:
            def pick(f):
                own = one_ref[f].astype(BF16)
                return jnp.where(blk == 0, own, two_ref[f])

            both(pick)
        else:
            both(lambda f: (one_ref[f].astype(F32) + two_ref[f].astype(F32)).astype(BF16))

    size = (step, plan.rows, plan.sources)
    if first:
        vec_specs = [
            pl.BlockSpec(size, lambda p, t, m: (chunk * steps + t, 0, 0)),
            pl.BlockSpec(size, lambda p, t, m: (t, 0, 0)),
        ]
    else:
        vec_specs = [
            pl.BlockSpec((None,) + size, lambda p, t, m: (blk_of(p, m), t, 0, 0)),
            pl.BlockSpec((None,) + size, lambda p, t, m: (1 - blk_of(p, m), t, 0, 0)),
        ]
    out = (step, plan.rows, 2 * plan.sensors)
    shape = (plan.part, plan.rows, 2 * plan.sensors)
    return pl.pallas_call(
        kernel,
        grid_spec=pltpu.PrefetchScalarGridSpec(
            num_scalar_prefetch=1,
            grid=(2, steps),
            in_specs=[near_spec(plan, chunk, blk_of), far_spec(plan, blk_of)] + vec_specs,
            out_specs=[
                pl.BlockSpec(out, lambda p, t, m: (jnp.where(p == 0, t, steps - 1), 0, 0)),
                pl.BlockSpec(out, lambda p, t, m: (jnp.where(p == 0, 0, t), 0, 0)),
            ],
        ),
        out_shape=[jax.ShapeDtypeStruct(shape, BF16), jax.ShapeDtypeStruct(shape, F32)],
        cost_estimate=cost(plan.flops, 16 * plan.part * plan.sensors * plan.sources),
        name="forward",
    )(meta, near, far, *vectors)


def adjoint_call(plan, chunk, meta, near, far, halves, last):
    blk_of = lambda p, m: 1 - p
    step, steps = plan.step, plan.steps

    def kernel(m, near_ref, far_ref, own_ref, got_ref, *outs):
        phase = pl.program_id(0)
        mine = blk_of(phase, m) == m[2]

        def run(out_ref):
            for f in range(step):
                field = jnp.where(mine, own_ref[f], got_ref[f])
                out_ref[f] = adjoint_rows(field, near_ref[f], far_ref[f]).astype(out_ref.dtype)

        if last:
            @pl.when(phase == 0)
            def _():
                run(outs[0])

            @pl.when(phase == 1)
            def _():
                run(outs[1])
        else:
            run(outs[0])

    size = (step, plan.rows, 2 * plan.sensors)
    out = (step, plan.rows, plan.sources)
    shape = (plan.part, plan.rows, plan.sources)
    if last:
        out_specs = [
            pl.BlockSpec(out, lambda p, t, m: (jnp.where(p == 0, t, steps - 1), 0, 0)),
            pl.BlockSpec(out, lambda p, t, m: (jnp.where(p == 0, 0, t), 0, 0)),
        ]
        out_shape = [jax.ShapeDtypeStruct(shape, BF16), jax.ShapeDtypeStruct(shape, F32)]
    else:
        out_specs = pl.BlockSpec((None,) + out, lambda p, t, m: (blk_of(p, m), t, 0, 0))
        out_shape = jax.ShapeDtypeStruct((2,) + shape, BF16)
    return pl.pallas_call(
        kernel,
        grid_spec=pltpu.PrefetchScalarGridSpec(
            num_scalar_prefetch=1,
            grid=(2, steps),
            in_specs=[
                near_spec(plan, chunk, blk_of),
                far_spec(plan, blk_of),
                pl.BlockSpec(size, lambda p, t, m: (t, 0, 0)),
                pl.BlockSpec(size, lambda p, t, m: (t, 0, 0)),
            ],
            out_specs=out_specs,
        ),
        out_shape=out_shape,
        cost_estimate=cost(plan.flops, 16 * plan.part * plan.sensors * plan.sources),
        name="adjoint",
    )(meta, near, far, *halves)


def split_call(plan, meta, keep, got):
    piece, groups = plan.piece, plan.groups
    width = keep.shape[-1]

    def kernel(m, keep_ref, got_ref, mine_ref, *sends):
        for d in range(groups):
            place = pl.ds(pl.multiple_of((m[3] ^ d) * piece, piece), piece)
            total = keep_ref[place] + got_ref[place].astype(F32)
            if d == 0:
                mine_ref[...] = total
            else:
                sends[d - 1][...] = total.astype(BF16)

    whole = pl.BlockSpec(memory_space=pltpu.VMEM)
    return pl.pallas_call(
        kernel,
        in_specs=[pl.BlockSpec(memory_space=pltpu.SMEM), whole, whole],
        out_specs=[whole] * groups,
        out_shape=[jax.ShapeDtypeStruct((piece, width), F32)]
        + [jax.ShapeDtypeStruct((piece, width), BF16)] * (groups - 1),
        cost_estimate=cost(groups * piece * width, groups * piece * width * 8),
        name="split",
    )(meta, keep.reshape(-1, width), got.reshape(-1, width))


def place_call(plan, meta, pieces):
    piece, groups = plan.piece, plan.groups
    width = pieces[0].shape[-1]

    def kernel(m, *refs):
        for d in range(groups):
            place = pl.ds(pl.multiple_of((m[3] ^ d) * piece, piece), piece)
            refs[groups][place] = refs[d][...]

    whole = pl.BlockSpec(memory_space=pltpu.VMEM)
    out = pl.pallas_call(
        kernel,
        in_specs=[pl.BlockSpec(memory_space=pltpu.SMEM)] + [whole] * groups,
        out_specs=whole,
        out_shape=jax.ShapeDtypeStruct((groups * piece, width), BF16),
        cost_estimate=cost(0, groups * piece * width * 4),
        name="place",
    )(meta, *pieces)
    return out.reshape(plan.part, plan.rows, width)


def body(n_sens, n_src, operator, right_side, noise_weights, damping):
    plan = Plan(operator, right_side, n_sens, n_src, CHUNKS)
    sens, src = lax.axis_index("sens"), lax.axis_index("src")
    pair, core = sens // 2, sens % 2
    half, group = src % 2, src // 2
    meta = jnp.stack([pair, core, half, group]).astype(jnp.int32)
    part, rows, block = plan.part, plan.rows, plan.block

    def to_core(array):
        return lax.ppermute(array, "sens", [(i, i ^ 1) for i in range(n_sens)])

    def to_pair(array):
        return lax.ppermute(array, "sens", [(i, i ^ 2) for i in range(n_sens)])

    def to_half(array):
        return lax.ppermute(array, "src", [(j, j ^ 1) for j in range(n_src)])

    def to_group(array, d):
        return lax.ppermute(array, "src", [(j, j ^ (2 * d)) for j in range(n_src)])

    def total(values):
        values = jnp.stack(values)
        padded = jnp.zeros((1, 128), F32).at[0, : values.shape[0]].set(values)
        gathered = lax.all_gather(padded, ("sens", "src"), axis=0, tiled=True)
        return jnp.sum(gathered, axis=0)

    near = operator.reshape(plan.pairs, 2, block, 2, plan.sensors, plan.sources)
    start = right_side.reshape(block, rows, plan.sources)
    chunks = range(plan.chunks)

    got_b = [to_pair(start[k * part:(k + 1) * part].astype(BF16)) for k in chunks]
    far = []
    for k in chunks:
        sent = lax.dynamic_slice(
            near,
            (0, 1 - core, k * part, 0, 0, 0),
            (plan.pairs, 1, part, 2, plan.sensors, plan.sources),
        )
        far.append(to_core(sent.reshape(plan.pairs, part, 2, plan.sensors, plan.sources)))

    weights = lax.all_gather(noise_weights, "src", axis=0, tiled=True)
    weights = weights.reshape(plan.pairs, 2, block, plan.sensors)
    weights_near = lax.dynamic_index_in_dim(weights, core, 1, keepdims=False)
    weights_far = to_core(lax.dynamic_index_in_dim(weights, 1 - core, 1, keepdims=False))
    weights = jnp.concatenate([weights_near, weights_far], axis=-1)
    weights = lax.dynamic_index_in_dim(weights, pair ^ half, 0, keepdims=False)
    damping_row = jnp.where(half == 0, damping, to_pair(damping))
    count = max(1, plan.piece // rows)

    def piece_of(k, table):
        place = k * part + group * plan.piece // rows
        cut = lax.dynamic_slice_in_dim(table, place, count, 0)
        return cut.reshape(count, 1, -1)

    def reduce_field(send, keep):
        mine, *sends = split_call(plan, meta, keep, to_half(send))
        for d, piece in enumerate(sends):
            mine = mine + to_group(piece, d + 1).astype(F32)
        return mine.reshape(count, plan.piece // count, -1)

    def gather_field(weighted):
        weighted = weighted.astype(BF16).reshape(plan.piece, -1)
        pieces = [weighted] + [to_group(weighted, d) for d in range(1, plan.groups)]
        own = place_call(plan, meta, pieces)
        return own, to_half(own)

    field, products = [], []
    for k in chunks:
        send, keep = forward_call(plan, k, meta, near, far[k], True, (start, got_b[k]))
        field.append(reduce_field(send, keep))
    scaled = [piece_of(k, weights) * field[k] for k in chunks]
    for k in chunks:
        back = adjoint_call(plan, k, meta, near, far[k], gather_field(scaled[k]), False)
        products.append((back, to_pair(back)))
    damp = damping[:, None, None]
    norm, curve = jnp.sum(start * start), jnp.sum(damp * start * start)
    for k in chunks:
        curve = curve + jnp.sum(scaled[k] * field[k])
    sums = total([norm, curve])
    norm_0, curve_0 = sums[0], sums[1]
    alpha_0 = norm_0 / curve_0

    image_0 = jnp.concatenate([mine[0].astype(F32) + got[1].astype(F32) for mine, got in products])
    image_0 = image_0 + damp * start
    residual = start - alpha_0 * image_0
    values = [
        jnp.sum(residual * residual),
        jnp.sum(damp * residual * residual),
        jnp.sum(damp * residual * start),
    ]

    square = cross = 0.0
    final = []
    for k in chunks:
        send, keep = forward_call(plan, k, meta, near, far[k], False, products[k])
        factor = 1.0 - alpha_0 * piece_of(k, damping_row)
        new_field = factor * field[k] - alpha_0 * reduce_field(send, keep)
        new_scaled = piece_of(k, weights) * new_field
        square = square + jnp.sum(new_scaled * new_field)
        cross = cross + jnp.sum(new_scaled * field[k])
        other, own = adjoint_call(plan, k, meta, near, far[k], gather_field(new_scaled), True)
        final.append(own + to_pair(other).astype(F32))
    sums = total(values + [square, cross])
    norm_1 = sums[0]
    beta = norm_1 / norm_0
    curve_1 = (sums[1] + sums[3]) + 2.0 * beta * (sums[2] + sums[4]) + beta * beta * curve_0
    alpha_1 = norm_1 / curve_1

    image_1 = jnp.concatenate(final) + damp * residual + beta * image_0
    solution = alpha_0 * start + alpha_1 * (residual + beta * start)
    residual = residual - alpha_1 * image_1
    return solution.reshape(right_side.shape), residual.reshape(right_side.shape)


def solution(mesh):
    in_specs = (
        P(None, None, "sens", "src"),
        P("sens", None, None, "src"),
        P("src", "sens"),
        P("sens"),
    )
    out_specs = (P("sens", None, None, "src"), P("sens", None, None, "src"))
    shard = functools.partial(body, mesh.shape["sens"], mesh.shape["src"])
    return jax.shard_map(shard, mesh=mesh, in_specs=in_specs, out_specs=out_specs, check_vma=False)
```

```python
import functools

import jax
import jax.numpy as jnp
from jax import lax
from jax.experimental import pallas as pl
from jax.experimental.pallas import tpu as pltpu
from jax.sharding import PartitionSpec as P

CHUNKS = 2
KERNEL_BYTES = 16 * 2 ** 20
F32 = jnp.float32
BF16 = jnp.bfloat16
NT = (((1,), (1,)), ((), ()))
NN = (((1,), (0,)), ((), ()))


def largest_divisor(extent, most):
    return next(size for size in range(min(extent, most), 0, -1) if extent % size == 0)


def turned(block, sign):
    half = block.shape[0] // 2
    upper, lower = block[:half], block[half:]
    return jnp.concatenate([-lower, upper] if sign < 0 else [lower, -upper], axis=0)


def forward_rows(vector, near, far):
    left = jnp.concatenate([vector, turned(vector, -1)], axis=1)
    right = jnp.concatenate(
        [jnp.concatenate([part[0], part[1]], axis=1) for part in (near, far)], axis=0
    )
    return lax.dot_general(left, right, NT, preferred_element_type=F32)


def adjoint_rows(field, near, far):
    sensors = near.shape[1]
    total = None
    for part, piece in ((near, field[:, :sensors]), (far, field[:, sensors:])):
        left = jnp.concatenate([piece, turned(piece, 1)], axis=1)
        right = part.reshape(2 * sensors, part.shape[2])
        term = lax.dot_general(left, right, NN, preferred_element_type=F32)
        total = term if total is None else total + term
    return total


def cost(flops, moved):
    return pl.CostEstimate(flops=flops, bytes_accessed=moved, transcendentals=0)


class Plan:
    def __init__(self, operator, right_side, n_sens, n_src, chunks):
        self.freqs, _, self.sensors, self.sources = operator.shape
        self.block = right_side.shape[0]
        self.rows = right_side.shape[1] * right_side.shape[2]
        self.pairs = n_sens // 2
        self.groups = n_src // 2
        self.chunks = chunks
        self.part = self.block // chunks
        self.step = largest_divisor(self.part, 8)
        self.steps = self.part // self.step
        self.flops = 16 * self.part * self.rows * self.sensors * self.sources * 2
        self.piece = self.part * self.rows // self.groups


def near_spec(plan, chunk, blk_of):
    return pl.BlockSpec(
        (None, None, plan.step, 2, plan.sensors, plan.sources),
        lambda p, t, m: (m[0] ^ blk_of(p, m), m[1], chunk * plan.steps + t, 0, 0, 0),
    )


def far_spec(plan, blk_of):
    return pl.BlockSpec(
        (None, plan.step, 2, plan.sensors, plan.sources),
        lambda p, t, m: (m[0] ^ blk_of(p, m), t, 0, 0, 0),
    )


def forward_call(plan, chunk, meta, near, far, first, vectors):
    blk_of = lambda p, m: 1 - (m[2] ^ p)
    step, steps = plan.step, plan.steps

    def kernel(m, near_ref, far_ref, one_ref, two_ref, send_ref, keep_ref):
        phase = pl.program_id(0)
        blk = blk_of(phase, m)

        def run(pick, out_ref):
            for f in range(step):
                out_ref[f] = forward_rows(pick(f), near_ref[f], far_ref[f]).astype(out_ref.dtype)

        def both(pick):
            @pl.when(phase == 0)
            def _():
                run(pick, send_ref)

            @pl.when(phase == 1)
            def _():
                run(pick, keep_ref)

        if first:
            def pick(f):
                own = one_ref[f].astype(BF16)
                return jnp.where(blk == 0, own, two_ref[f])

            both(pick)
        else:
            both(lambda f: (one_ref[f].astype(F32) + two_ref[f].astype(F32)).astype(BF16))

    size = (step, plan.rows, plan.sources)
    if first:
        vec_specs = [
            pl.BlockSpec(size, lambda p, t, m: (chunk * steps + t, 0, 0)),
            pl.BlockSpec(size, lambda p, t, m: (t, 0, 0)),
        ]
    else:
        vec_specs = [
            pl.BlockSpec((None,) + size, lambda p, t, m: (blk_of(p, m), t, 0, 0)),
            pl.BlockSpec((None,) + size, lambda p, t, m: (1 - blk_of(p, m), t, 0, 0)),
        ]
    out = (step, plan.rows, 2 * plan.sensors)
    shape = (plan.part, plan.rows, 2 * plan.sensors)
    return pl.pallas_call(
        kernel,
        grid_spec=pltpu.PrefetchScalarGridSpec(
            num_scalar_prefetch=1,
            grid=(2, steps),
            in_specs=[near_spec(plan, chunk, blk_of), far_spec(plan, blk_of)] + vec_specs,
            out_specs=[
                pl.BlockSpec(out, lambda p, t, m: (jnp.where(p == 0, t, steps - 1), 0, 0)),
                pl.BlockSpec(out, lambda p, t, m: (jnp.where(p == 0, 0, t), 0, 0)),
            ],
        ),
        out_shape=[jax.ShapeDtypeStruct(shape, BF16), jax.ShapeDtypeStruct(shape, F32)],
        cost_estimate=cost(plan.flops, 16 * plan.part * plan.sensors * plan.sources),
        compiler_params=pltpu.CompilerParams(vmem_limit_bytes=KERNEL_BYTES),
        name="forward",
    )(meta, near, far, *vectors)


def adjoint_call(plan, chunk, meta, near, far, halves, last):
    blk_of = lambda p, m: 1 - p
    step, steps = plan.step, plan.steps

    def kernel(m, near_ref, far_ref, own_ref, got_ref, *outs):
        phase = pl.program_id(0)
        mine = blk_of(phase, m) == m[2]

        def run(out_ref):
            for f in range(step):
                field = jnp.where(mine, own_ref[f], got_ref[f])
                out_ref[f] = adjoint_rows(field, near_ref[f], far_ref[f]).astype(out_ref.dtype)

        if last:
            @pl.when(phase == 0)
            def _():
                run(outs[0])

            @pl.when(phase == 1)
            def _():
                run(outs[1])
        else:
            run(outs[0])

    size = (step, plan.rows, 2 * plan.sensors)
    out = (step, plan.rows, plan.sources)
    shape = (plan.part, plan.rows, plan.sources)
    if last:
        out_specs = [
            pl.BlockSpec(out, lambda p, t, m: (jnp.where(p == 0, t, steps - 1), 0, 0)),
            pl.BlockSpec(out, lambda p, t, m: (jnp.where(p == 0, 0, t), 0, 0)),
        ]
        out_shape = [jax.ShapeDtypeStruct(shape, BF16), jax.ShapeDtypeStruct(shape, F32)]
    else:
        out_specs = pl.BlockSpec((None,) + out, lambda p, t, m: (blk_of(p, m), t, 0, 0))
        out_shape = jax.ShapeDtypeStruct((2,) + shape, BF16)
    return pl.pallas_call(
        kernel,
        grid_spec=pltpu.PrefetchScalarGridSpec(
            num_scalar_prefetch=1,
            grid=(2, steps),
            in_specs=[
                near_spec(plan, chunk, blk_of),
                far_spec(plan, blk_of),
                pl.BlockSpec(size, lambda p, t, m: (t, 0, 0)),
                pl.BlockSpec(size, lambda p, t, m: (t, 0, 0)),
            ],
            out_specs=out_specs,
        ),
        out_shape=out_shape,
        cost_estimate=cost(plan.flops, 16 * plan.part * plan.sensors * plan.sources),
        compiler_params=pltpu.CompilerParams(vmem_limit_bytes=KERNEL_BYTES),
        name="adjoint",
    )(meta, near, far, *halves)


def body(n_sens, n_src, operator, right_side, noise_weights, damping):
    plan = Plan(operator, right_side, n_sens, n_src, CHUNKS)
    sens, src = lax.axis_index("sens"), lax.axis_index("src")
    pair, core = sens // 2, sens % 2
    half, group = src % 2, src // 2
    meta = jnp.stack([pair, core, half, group]).astype(jnp.int32)
    part, rows, block = plan.part, plan.rows, plan.block

    def to_core(array):
        return lax.ppermute(array, "sens", [(i, i ^ 1) for i in range(n_sens)])

    def to_pair(array):
        return lax.ppermute(array, "sens", [(i, i ^ 2) for i in range(n_sens)])

    def to_half(array):
        return lax.ppermute(array, "src", [(j, j ^ 1) for j in range(n_src)])

    columns = [list(range(0, n_src, 2)), list(range(1, n_src, 2))]

    def src_bits():
        return [2 ** bit for bit in range(n_src.bit_length() - 1)]

    def total(values):
        sums = jnp.zeros((1, 128), F32).at[0, : len(values)].set(jnp.stack(values))
        sums = sums + to_core(sums)
        for bit in src_bits():
            sums = sums + lax.ppermute(sums, "src", [(j, j ^ bit) for j in range(n_src)])
        return (sums + to_pair(sums))[0]

    def all_weights(table):
        for bit in src_bits():
            other = lax.ppermute(table, "src", [(j, j ^ bit) for j in range(n_src)])
            low = (src // bit) % 2 == 0
            table = jnp.concatenate(
                [jnp.where(low, table, other), jnp.where(low, other, table)], axis=0
            )
        return table

    near = operator.reshape(plan.pairs, 2, block, 2, plan.sensors, plan.sources)
    start = right_side.reshape(block, rows, plan.sources)
    chunks = range(plan.chunks)

    got_b = [to_pair(start[k * part:(k + 1) * part].astype(BF16)) for k in chunks]
    far = []
    for k in chunks:
        sent = lax.dynamic_slice(
            near,
            (0, 1 - core, k * part, 0, 0, 0),
            (plan.pairs, 1, part, 2, plan.sensors, plan.sources),
        )
        far.append(to_core(sent.reshape(plan.pairs, part, 2, plan.sensors, plan.sources)))

    weights = all_weights(noise_weights)
    weights = weights.reshape(plan.pairs, 2, block, plan.sensors)
    weights_near = lax.dynamic_index_in_dim(weights, core, 1, keepdims=False)
    weights_far = to_core(lax.dynamic_index_in_dim(weights, 1 - core, 1, keepdims=False))
    weights = jnp.concatenate([weights_near, weights_far], axis=-1)
    weights = lax.dynamic_index_in_dim(weights, pair ^ half, 0, keepdims=False)
    damping_row = jnp.where(half == 0, damping, to_pair(damping))
    count = max(1, plan.piece // rows)

    def piece_of(k, table):
        place = k * part + group * plan.piece // rows
        cut = lax.dynamic_slice_in_dim(table, place, count, 0)
        return cut.reshape(count, 1, -1)

    def reduce_field(send, keep):
        both = (keep + to_half(send).astype(F32)).astype(BF16).reshape(part * rows, -1)
        mine = lax.psum_scatter(
            both, "src", scatter_dimension=0, axis_index_groups=columns, tiled=True
        )
        return mine.astype(F32).reshape(count, plan.piece // count, -1)

    def gather_field(weighted):
        weighted = weighted.astype(BF16).reshape(plan.piece, -1)
        own = lax.all_gather(weighted, "src", axis=0, axis_index_groups=columns, tiled=True)
        own = own.reshape(part, rows, -1)
        return own, to_half(own)

    field, products = [], []
    for k in chunks:
        send, keep = forward_call(plan, k, meta, near, far[k], True, (start, got_b[k]))
        field.append(reduce_field(send, keep))
    scaled = [piece_of(k, weights) * field[k] for k in chunks]
    for k in chunks:
        back = adjoint_call(plan, k, meta, near, far[k], gather_field(scaled[k]), False)
        products.append((back, to_pair(back)))
    damp = damping[:, None, None]
    norm, curve = jnp.sum(start * start), jnp.sum(damp * start * start)
    for k in chunks:
        curve = curve + jnp.sum(scaled[k] * field[k])
    sums = total([norm, curve])
    norm_0, curve_0 = sums[0], sums[1]
    alpha_0 = norm_0 / curve_0

    image_0 = jnp.concatenate([mine[0].astype(F32) + got[1].astype(F32) for mine, got in products])
    image_0 = image_0 + damp * start
    residual = start - alpha_0 * image_0
    values = [
        jnp.sum(residual * residual),
        jnp.sum(damp * residual * residual),
        jnp.sum(damp * residual * start),
    ]

    square = cross = 0.0
    final = []
    for k in chunks:
        send, keep = forward_call(plan, k, meta, near, far[k], False, products[k])
        factor = 1.0 - alpha_0 * piece_of(k, damping_row)
        new_field = factor * field[k] - alpha_0 * reduce_field(send, keep)
        new_scaled = piece_of(k, weights) * new_field
        square = square + jnp.sum(new_scaled * new_field)
        cross = cross + jnp.sum(new_scaled * field[k])
        other, own = adjoint_call(plan, k, meta, near, far[k], gather_field(new_scaled), True)
        final.append(own + to_pair(other).astype(F32))
    sums = total(values + [square, cross])
    norm_1 = sums[0]
    beta = norm_1 / norm_0
    curve_1 = (sums[1] + sums[3]) + 2.0 * beta * (sums[2] + sums[4]) + beta * beta * curve_0
    alpha_1 = norm_1 / curve_1

    image_1 = jnp.concatenate(final) + damp * residual + beta * image_0
    solution = alpha_0 * start + alpha_1 * (residual + beta * start)
    residual = residual - alpha_1 * image_1
    return solution.reshape(right_side.shape), residual.reshape(right_side.shape)


def solution(mesh):
    in_specs = (
        P(None, None, "sens", "src"),
        P("sens", None, None, "src"),
        P("src", "sens"),
        P("sens"),
    )
    out_specs = (P("sens", None, None, "src"), P("sens", None, None, "src"))
    shard = functools.partial(body, mesh.shape["sens"], mesh.shape["src"])
    return jax.shard_map(shard, mesh=mesh, in_specs=in_specs, out_specs=out_specs, check_vma=False)
```

```python
import functools

import jax
import jax.numpy as jnp
from jax import lax
from jax.experimental import pallas as pl
from jax.experimental.pallas import tpu as pltpu
from jax.sharding import PartitionSpec as P

CHUNKS = 2
KERNEL_BYTES = 16 * 2 ** 20
F32 = jnp.float32
BF16 = jnp.bfloat16
NT = (((1,), (1,)), ((), ()))
NN = (((1,), (0,)), ((), ()))


def largest_divisor(extent, most):
    return next(size for size in range(min(extent, most), 0, -1) if extent % size == 0)


def turned(block, sign):
    half = block.shape[0] // 2
    upper, lower = block[:half], block[half:]
    return jnp.concatenate([-lower, upper] if sign < 0 else [lower, -upper], axis=0)


def forward_rows(vector, near, far):
    left = jnp.concatenate([vector, turned(vector, -1)], axis=1)
    right = jnp.concatenate(
        [jnp.concatenate([part[0], part[1]], axis=1) for part in (near, far)], axis=0
    )
    return lax.dot_general(left, right, NT, preferred_element_type=F32)


def adjoint_rows(field, near, far):
    sensors = near.shape[1]
    total = None
    for part, piece in ((near, field[:, :sensors]), (far, field[:, sensors:])):
        left = jnp.concatenate([piece, turned(piece, 1)], axis=1)
        right = part.reshape(2 * sensors, part.shape[2])
        term = lax.dot_general(left, right, NN, preferred_element_type=F32)
        total = term if total is None else total + term
    return total


def cost(flops, moved):
    return pl.CostEstimate(flops=flops, bytes_accessed=moved, transcendentals=0)


class Plan:
    def __init__(self, operator, right_side, n_sens, n_src, chunks):
        self.freqs, _, self.sensors, self.sources = operator.shape
        self.block = right_side.shape[0]
        self.rows = right_side.shape[1] * right_side.shape[2]
        self.pairs = n_sens // 2
        self.groups = n_src // 2
        self.chunks = chunks
        self.part = self.block // chunks
        self.step = largest_divisor(self.part, 8)
        self.steps = self.part // self.step
        self.flops = 16 * self.part * self.rows * self.sensors * self.sources * 2
        self.piece = self.part * self.rows // self.groups


def part_spec(plan, blk_of):
    return pl.BlockSpec(
        (None, plan.step, 2, plan.sensors, plan.sources),
        lambda p, t, m: (m[0] ^ blk_of(p, m), t, 0, 0, 0),
    )


def forward_call(plan, chunk, meta, near, far, first, vectors):
    blk_of = lambda p, m: 1 - (m[2] ^ p)
    step, steps = plan.step, plan.steps

    def kernel(m, near_ref, far_ref, one_ref, two_ref, send_ref, keep_ref):
        phase = pl.program_id(0)
        blk = blk_of(phase, m)

        def run(pick, out_ref):
            for f in range(step):
                out_ref[f] = forward_rows(pick(f), near_ref[f], far_ref[f]).astype(out_ref.dtype)

        def both(pick):
            @pl.when(phase == 0)
            def _():
                run(pick, send_ref)

            @pl.when(phase == 1)
            def _():
                run(pick, keep_ref)

        if first:
            def pick(f):
                own = one_ref[f].astype(BF16)
                return jnp.where(blk == 0, own, two_ref[f])

            both(pick)
        else:
            both(lambda f: (one_ref[f].astype(F32) + two_ref[f].astype(F32)).astype(BF16))

    size = (step, plan.rows, plan.sources)
    if first:
        vec_specs = [
            pl.BlockSpec(size, lambda p, t, m: (chunk * steps + t, 0, 0)),
            pl.BlockSpec(size, lambda p, t, m: (t, 0, 0)),
        ]
    else:
        vec_specs = [
            pl.BlockSpec((None,) + size, lambda p, t, m: (blk_of(p, m), t, 0, 0)),
            pl.BlockSpec((None,) + size, lambda p, t, m: (1 - blk_of(p, m), t, 0, 0)),
        ]
    out = (step, plan.rows, 2 * plan.sensors)
    shape = (plan.part, plan.rows, 2 * plan.sensors)
    return pl.pallas_call(
        kernel,
        grid_spec=pltpu.PrefetchScalarGridSpec(
            num_scalar_prefetch=1,
            grid=(2, steps),
            in_specs=[part_spec(plan, blk_of)] * 2 + vec_specs,
            out_specs=[
                pl.BlockSpec(out, lambda p, t, m: (jnp.where(p == 0, t, steps - 1), 0, 0)),
                pl.BlockSpec(out, lambda p, t, m: (jnp.where(p == 0, 0, t), 0, 0)),
            ],
        ),
        out_shape=[jax.ShapeDtypeStruct(shape, BF16), jax.ShapeDtypeStruct(shape, F32)],
        cost_estimate=cost(plan.flops, 16 * plan.part * plan.sensors * plan.sources),
        compiler_params=pltpu.CompilerParams(vmem_limit_bytes=KERNEL_BYTES),
        name="forward",
    )(meta, near, far, *vectors)


def adjoint_call(plan, meta, near, far, halves, last):
    blk_of = lambda p, m: 1 - p
    step, steps = plan.step, plan.steps

    def kernel(m, near_ref, far_ref, own_ref, got_ref, *outs):
        phase = pl.program_id(0)
        mine = blk_of(phase, m) == m[2]

        def run(out_ref):
            for f in range(step):
                field = jnp.where(mine, own_ref[f], got_ref[f])
                out_ref[f] = adjoint_rows(field, near_ref[f], far_ref[f]).astype(out_ref.dtype)

        if last:
            @pl.when(phase == 0)
            def _():
                run(outs[0])

            @pl.when(phase == 1)
            def _():
                run(outs[1])
        else:
            run(outs[0])

    size = (step, plan.rows, 2 * plan.sensors)
    out = (step, plan.rows, plan.sources)
    shape = (plan.part, plan.rows, plan.sources)
    if last:
        out_specs = [
            pl.BlockSpec(out, lambda p, t, m: (jnp.where(p == 0, t, steps - 1), 0, 0)),
            pl.BlockSpec(out, lambda p, t, m: (jnp.where(p == 0, 0, t), 0, 0)),
        ]
        out_shape = [jax.ShapeDtypeStruct(shape, BF16), jax.ShapeDtypeStruct(shape, F32)]
    else:
        out_specs = pl.BlockSpec((None,) + out, lambda p, t, m: (blk_of(p, m), t, 0, 0))
        out_shape = jax.ShapeDtypeStruct((2,) + shape, BF16)
    return pl.pallas_call(
        kernel,
        grid_spec=pltpu.PrefetchScalarGridSpec(
            num_scalar_prefetch=1,
            grid=(2, steps),
            in_specs=[
                part_spec(plan, blk_of),
                part_spec(plan, blk_of),
                pl.BlockSpec(size, lambda p, t, m: (t, 0, 0)),
                pl.BlockSpec(size, lambda p, t, m: (t, 0, 0)),
            ],
            out_specs=out_specs,
        ),
        out_shape=out_shape,
        cost_estimate=cost(plan.flops, 16 * plan.part * plan.sensors * plan.sources),
        compiler_params=pltpu.CompilerParams(vmem_limit_bytes=KERNEL_BYTES),
        name="adjoint",
    )(meta, near, far, *halves)


def split_call(plan, meta, keep, got):
    piece, groups = plan.piece, plan.groups
    width = keep.shape[-1]

    def kernel(m, keep_ref, got_ref, mine_ref, *sends):
        for d in range(groups):
            place = pl.ds(pl.multiple_of((m[3] ^ d) * piece, piece), piece)
            total = keep_ref[place] + got_ref[place].astype(F32)
            if d == 0:
                mine_ref[...] = total
            else:
                sends[d - 1][...] = total.astype(BF16)

    whole = pl.BlockSpec(memory_space=pltpu.VMEM)
    return pl.pallas_call(
        kernel,
        in_specs=[pl.BlockSpec(memory_space=pltpu.SMEM), whole, whole],
        out_specs=[whole] * groups,
        out_shape=[jax.ShapeDtypeStruct((piece, width), F32)]
        + [jax.ShapeDtypeStruct((piece, width), BF16)] * (groups - 1),
        cost_estimate=cost(groups * piece * width, groups * piece * width * 8),
        compiler_params=pltpu.CompilerParams(vmem_limit_bytes=KERNEL_BYTES),
        name="split",
    )(meta, keep.reshape(-1, width), got.reshape(-1, width))


def place_call(plan, meta, pieces):
    piece, groups = plan.piece, plan.groups
    width = pieces[0].shape[-1]

    def kernel(m, *refs):
        for d in range(groups):
            place = pl.ds(pl.multiple_of((m[3] ^ d) * piece, piece), piece)
            refs[groups][place] = refs[d][...]

    whole = pl.BlockSpec(memory_space=pltpu.VMEM)
    out = pl.pallas_call(
        kernel,
        in_specs=[pl.BlockSpec(memory_space=pltpu.SMEM)] + [whole] * groups,
        out_specs=whole,
        out_shape=jax.ShapeDtypeStruct((groups * piece, width), BF16),
        cost_estimate=cost(0, groups * piece * width * 4),
        compiler_params=pltpu.CompilerParams(vmem_limit_bytes=KERNEL_BYTES),
        name="place",
    )(meta, *pieces)
    return out.reshape(plan.part, plan.rows, width)


def body(n_sens, n_src, operator, right_side, noise_weights, damping):
    plan = Plan(operator, right_side, n_sens, n_src, CHUNKS)
    sens, src = lax.axis_index("sens"), lax.axis_index("src")
    pair, core = sens // 2, sens % 2
    half, group = src % 2, src // 2
    meta = jnp.stack([pair, core, half, group]).astype(jnp.int32)
    part, rows, block = plan.part, plan.rows, plan.block

    def to_core(array):
        return lax.ppermute(array, "sens", [(i, i ^ 1) for i in range(n_sens)])

    def to_pair(array):
        return lax.ppermute(array, "sens", [(i, i ^ 2) for i in range(n_sens)])

    def to_half(array):
        return lax.ppermute(array, "src", [(j, j ^ 1) for j in range(n_src)])

    def to_group(array, d):
        return lax.ppermute(array, "src", [(j, j ^ (2 * d)) for j in range(n_src)])

    def src_bits():
        return [2 ** bit for bit in range(n_src.bit_length() - 1)]

    def total(values):
        sums = jnp.zeros((1, 128), F32).at[0, : len(values)].set(jnp.stack(values))
        sums = sums + to_core(sums)
        for bit in src_bits():
            sums = sums + lax.ppermute(sums, "src", [(j, j ^ bit) for j in range(n_src)])
        return (sums + to_pair(sums))[0]

    def all_weights(table):
        for bit in src_bits():
            other = lax.ppermute(table, "src", [(j, j ^ bit) for j in range(n_src)])
            low = (src // bit) % 2 == 0
            table = jnp.concatenate(
                [jnp.where(low, table, other), jnp.where(low, other, table)], axis=0
            )
        return table

    whole = operator.reshape(plan.pairs, 2, block, 2, plan.sensors, plan.sources)
    start = right_side.reshape(block, rows, plan.sources)
    chunks = range(plan.chunks)

    sent_b = [start[k * part:(k + 1) * part].astype(BF16) for k in chunks]
    got_b = [to_pair(sent) for sent in sent_b]
    core, *_ = lax.optimization_barrier((core, *sent_b))

    def half_of(k, which):
        size = (plan.pairs, 1, part, 2, plan.sensors, plan.sources)
        cut = lax.dynamic_slice(whole, (0, which, k * part, 0, 0, 0), size)
        return cut.reshape(plan.pairs, part, 2, plan.sensors, plan.sources)

    near, far = [], []
    for k in chunks:
        far.append(to_core(half_of(k, 1 - core)))
        near.append(half_of(k, core))

    weights = all_weights(noise_weights)
    weights = weights.reshape(plan.pairs, 2, block, plan.sensors)
    weights_near = lax.dynamic_index_in_dim(weights, core, 1, keepdims=False)
    weights_far = to_core(lax.dynamic_index_in_dim(weights, 1 - core, 1, keepdims=False))
    weights = jnp.concatenate([weights_near, weights_far], axis=-1)
    weights = lax.dynamic_index_in_dim(weights, pair ^ half, 0, keepdims=False)
    damping_row = jnp.where(half == 0, damping, to_pair(damping))
    count = max(1, plan.piece // rows)

    def piece_of(k, table):
        place = k * part + group * plan.piece // rows
        cut = lax.dynamic_slice_in_dim(table, place, count, 0)
        return cut.reshape(count, 1, -1)

    def reduce_field(send, keep):
        mine, *sends = split_call(plan, meta, keep, to_half(send))
        for d, piece in enumerate(sends):
            mine = mine + to_group(piece, d + 1).astype(F32)
        return mine.reshape(count, plan.piece // count, -1)

    def gather_field(weighted):
        weighted = weighted.astype(BF16).reshape(plan.piece, -1)
        pieces = [weighted] + [to_group(weighted, d) for d in range(1, plan.groups)]
        own = place_call(plan, meta, pieces)
        return own, to_half(own)

    field, products = [], []
    for k in chunks:
        send, keep = forward_call(plan, k, meta, near[k], far[k], True, (start, got_b[k]))
        field.append(reduce_field(send, keep))
    scaled = [piece_of(k, weights) * field[k] for k in chunks]
    for k in chunks:
        back = adjoint_call(plan, meta, near[k], far[k], gather_field(scaled[k]), False)
        products.append((back, to_pair(back)))
    damp = damping[:, None, None]
    norm, curve = jnp.sum(start * start), jnp.sum(damp * start * start)
    for k in chunks:
        curve = curve + jnp.sum(scaled[k] * field[k])
    sums = total([norm, curve])
    norm_0, curve_0 = sums[0], sums[1]
    alpha_0 = norm_0 / curve_0

    image_0 = jnp.concatenate([mine[0].astype(F32) + got[1].astype(F32) for mine, got in products])
    image_0 = image_0 + damp * start
    residual = start - alpha_0 * image_0
    values = [
        jnp.sum(residual * residual),
        jnp.sum(damp * residual * residual),
        jnp.sum(damp * residual * start),
    ]

    square = cross = 0.0
    final = []
    for k in chunks:
        send, keep = forward_call(plan, k, meta, near[k], far[k], False, products[k])
        factor = 1.0 - alpha_0 * piece_of(k, damping_row)
        new_field = factor * field[k] - alpha_0 * reduce_field(send, keep)
        new_scaled = piece_of(k, weights) * new_field
        square = square + jnp.sum(new_scaled * new_field)
        cross = cross + jnp.sum(new_scaled * field[k])
        other, own = adjoint_call(plan, meta, near[k], far[k], gather_field(new_scaled), True)
        final.append(own + to_pair(other).astype(F32))
    sums = total(values + [square, cross])
    norm_1 = sums[0]
    beta = norm_1 / norm_0
    curve_1 = (sums[1] + sums[3]) + 2.0 * beta * (sums[2] + sums[4]) + beta * beta * curve_0
    alpha_1 = norm_1 / curve_1

    image_1 = jnp.concatenate(final) + damp * residual + beta * image_0
    solution = alpha_0 * start + alpha_1 * (residual + beta * start)
    residual = residual - alpha_1 * image_1
    return solution.reshape(right_side.shape), residual.reshape(right_side.shape)


def solution(mesh):
    in_specs = (
        P(None, None, "sens", "src"),
        P("sens", None, None, "src"),
        P("src", "sens"),
        P("sens"),
    )
    out_specs = (P("sens", None, None, "src"), P("sens", None, None, "src"))
    shard = functools.partial(body, mesh.shape["sens"], mesh.shape["src"])
    return jax.shard_map(shard, mesh=mesh, in_specs=in_specs, out_specs=out_specs, check_vma=False)
```

```python
import functools

import jax
import jax.numpy as jnp
from jax import lax
from jax.experimental import pallas as pl
from jax.experimental.pallas import tpu as pltpu
from jax.sharding import PartitionSpec as P

CHUNKS = 2
KERNEL_BYTES = 16 * 2 ** 20
F32 = jnp.float32
BF16 = jnp.bfloat16
NT = (((1,), (1,)), ((), ()))
NN = (((1,), (0,)), ((), ()))


def largest_divisor(extent, most):
    return next(size for size in range(min(extent, most), 0, -1) if extent % size == 0)


def turned(block, sign):
    half = block.shape[0] // 2
    upper, lower = block[:half], block[half:]
    return jnp.concatenate([-lower, upper] if sign < 0 else [lower, -upper], axis=0)


def forward_rows(vector, near, far):
    left = jnp.concatenate([vector, turned(vector, -1)], axis=1)
    right = jnp.concatenate(
        [jnp.concatenate([part[0], part[1]], axis=1) for part in (near, far)], axis=0
    )
    return lax.dot_general(left, right, NT, preferred_element_type=F32)


def adjoint_rows(field, near, far):
    sensors = near.shape[1]
    total = None
    for part, piece in ((near, field[:, :sensors]), (far, field[:, sensors:])):
        left = jnp.concatenate([piece, turned(piece, 1)], axis=1)
        right = part.reshape(2 * sensors, part.shape[2])
        term = lax.dot_general(left, right, NN, preferred_element_type=F32)
        total = term if total is None else total + term
    return total


def cost(flops, moved):
    return pl.CostEstimate(flops=flops, bytes_accessed=moved, transcendentals=0)


class Plan:
    def __init__(self, operator, right_side, n_sens, n_src, chunks):
        self.freqs, _, self.sensors, self.sources = operator.shape
        self.block = right_side.shape[0]
        self.rows = right_side.shape[1] * right_side.shape[2]
        self.pairs = n_sens // 2
        self.groups = n_src // 2
        self.chunks = chunks
        self.part = self.block // chunks
        self.step = largest_divisor(self.part, 8)
        self.steps = self.part // self.step
        self.flops = 16 * self.part * self.rows * self.sensors * self.sources * 2
        self.piece = self.part * self.rows // self.groups


def part_spec(plan, blk_of):
    return pl.BlockSpec(
        (None, plan.step, 2, plan.sensors, plan.sources),
        lambda p, t, m: (m[0] ^ blk_of(p, m), t, 0, 0, 0),
    )


def forward_call(plan, chunk, meta, near, far, first, vectors):
    blk_of = lambda p, m: 1 - (m[2] ^ p)
    step, steps = plan.step, plan.steps

    def kernel(m, near_ref, far_ref, one_ref, two_ref, send_ref, keep_ref):
        phase = pl.program_id(0)
        blk = blk_of(phase, m)

        def run(pick, out_ref):
            for f in range(step):
                out_ref[f] = forward_rows(pick(f), near_ref[f], far_ref[f]).astype(out_ref.dtype)

        def both(pick):
            @pl.when(phase == 0)
            def _():
                run(pick, send_ref)

            @pl.when(phase == 1)
            def _():
                run(pick, keep_ref)

        if first:
            def pick(f):
                own = one_ref[f].astype(BF16)
                return jnp.where(blk == 0, own, two_ref[f])

            both(pick)
        else:
            both(lambda f: (one_ref[f].astype(F32) + two_ref[f].astype(F32)).astype(BF16))

    size = (step, plan.rows, plan.sources)
    if first:
        vec_specs = [
            pl.BlockSpec(size, lambda p, t, m: (chunk * steps + t, 0, 0)),
            pl.BlockSpec(size, lambda p, t, m: (t, 0, 0)),
        ]
    else:
        vec_specs = [
            pl.BlockSpec((None,) + size, lambda p, t, m: (blk_of(p, m), t, 0, 0)),
            pl.BlockSpec((None,) + size, lambda p, t, m: (1 - blk_of(p, m), t, 0, 0)),
        ]
    out = (step, plan.rows, 2 * plan.sensors)
    shape = (plan.part, plan.rows, 2 * plan.sensors)
    return pl.pallas_call(
        kernel,
        grid_spec=pltpu.PrefetchScalarGridSpec(
            num_scalar_prefetch=1,
            grid=(2, steps),
            in_specs=[part_spec(plan, blk_of)] * 2 + vec_specs,
            out_specs=[
                pl.BlockSpec(out, lambda p, t, m: (jnp.where(p == 0, t, steps - 1), 0, 0)),
                pl.BlockSpec(out, lambda p, t, m: (jnp.where(p == 0, 0, t), 0, 0)),
            ],
        ),
        out_shape=[jax.ShapeDtypeStruct(shape, BF16)] * 2,
        cost_estimate=cost(plan.flops, 16 * plan.part * plan.sensors * plan.sources),
        compiler_params=pltpu.CompilerParams(vmem_limit_bytes=KERNEL_BYTES),
        name="forward",
    )(meta, near, far, *vectors)


def adjoint_call(plan, meta, near, far, halves, last):
    blk_of = lambda p, m: 1 - p
    step, steps = plan.step, plan.steps

    def kernel(m, near_ref, far_ref, own_ref, got_ref, *outs):
        phase = pl.program_id(0)
        mine = blk_of(phase, m) == m[2]

        def run(out_ref):
            for f in range(step):
                field = jnp.where(mine, own_ref[f], got_ref[f])
                out_ref[f] = adjoint_rows(field, near_ref[f], far_ref[f]).astype(out_ref.dtype)

        if last:
            @pl.when(phase == 0)
            def _():
                run(outs[0])

            @pl.when(phase == 1)
            def _():
                run(outs[1])
        else:
            run(outs[0])

    size = (step, plan.rows, 2 * plan.sensors)
    out = (step, plan.rows, plan.sources)
    shape = (plan.part, plan.rows, plan.sources)
    if last:
        out_specs = [
            pl.BlockSpec(out, lambda p, t, m: (jnp.where(p == 0, t, steps - 1), 0, 0)),
            pl.BlockSpec(out, lambda p, t, m: (jnp.where(p == 0, 0, t), 0, 0)),
        ]
        out_shape = [jax.ShapeDtypeStruct(shape, BF16), jax.ShapeDtypeStruct(shape, F32)]
    else:
        out_specs = pl.BlockSpec((None,) + out, lambda p, t, m: (blk_of(p, m), t, 0, 0))
        out_shape = jax.ShapeDtypeStruct((2,) + shape, BF16)
    return pl.pallas_call(
        kernel,
        grid_spec=pltpu.PrefetchScalarGridSpec(
            num_scalar_prefetch=1,
            grid=(2, steps),
            in_specs=[
                part_spec(plan, blk_of),
                part_spec(plan, blk_of),
                pl.BlockSpec(size, lambda p, t, m: (t, 0, 0)),
                pl.BlockSpec(size, lambda p, t, m: (t, 0, 0)),
            ],
            out_specs=out_specs,
        ),
        out_shape=out_shape,
        cost_estimate=cost(plan.flops, 16 * plan.part * plan.sensors * plan.sources),
        compiler_params=pltpu.CompilerParams(vmem_limit_bytes=KERNEL_BYTES),
        name="adjoint",
    )(meta, near, far, *halves)


def fold_call(plan, level, meta, keep, got):
    height, width = keep.shape
    cut = height // 2

    def kernel(m, keep_ref, got_ref, send_ref, own_ref):
        bit = (m[3] >> level) & 1
        for out_ref, side in ((send_ref, 1 - bit), (own_ref, bit)):
            place = pl.ds(pl.multiple_of(side * cut, cut), cut)
            out_ref[...] = (keep_ref[place].astype(F32) + got_ref[place].astype(F32)).astype(BF16)

    whole = pl.BlockSpec(memory_space=pltpu.VMEM)
    return pl.pallas_call(
        kernel,
        in_specs=[pl.BlockSpec(memory_space=pltpu.SMEM), whole, whole],
        out_specs=[whole] * 2,
        out_shape=[jax.ShapeDtypeStruct((cut, width), BF16)] * 2,
        cost_estimate=cost(height * width, height * width * 6),
        compiler_params=pltpu.CompilerParams(vmem_limit_bytes=KERNEL_BYTES),
        name="fold",
    )(meta, keep, got)


def join_call(plan, level, meta, own, got):
    height, width = own.shape

    def kernel(m, own_ref, got_ref, out_ref):
        bit = (m[3] >> level) & 1
        for ref, side in ((own_ref, bit), (got_ref, 1 - bit)):
            out_ref[pl.ds(pl.multiple_of(side * height, height), height)] = ref[...]

    whole = pl.BlockSpec(memory_space=pltpu.VMEM)
    return pl.pallas_call(
        kernel,
        in_specs=[pl.BlockSpec(memory_space=pltpu.SMEM), whole, whole],
        out_specs=whole,
        out_shape=jax.ShapeDtypeStruct((2 * height, width), BF16),
        cost_estimate=cost(0, height * width * 8),
        compiler_params=pltpu.CompilerParams(vmem_limit_bytes=KERNEL_BYTES),
        name="join",
    )(meta, own, got)


def body(n_sens, n_src, operator, right_side, noise_weights, damping):
    plan = Plan(operator, right_side, n_sens, n_src, CHUNKS)
    sens, src = lax.axis_index("sens"), lax.axis_index("src")
    pair, core, half = sens // 2, sens % 2, src % 2
    meta = jnp.stack([pair, core, half, src]).astype(jnp.int32)
    part, rows, block = plan.part, plan.rows, plan.block
    levels = range(n_src.bit_length() - 1)
    chunks = range(plan.chunks)

    def to_core(array):
        return lax.ppermute(array, "sens", [(i, i ^ 1) for i in range(n_sens)])

    def to_pair(array):
        return lax.ppermute(array, "sens", [(i, i ^ 2) for i in range(n_sens)])

    def to_src(array, level):
        return lax.ppermute(array, "src", [(j, j ^ (1 << level)) for j in range(n_src)])

    def lanes(array):
        array = jnp.sum(array.reshape(-1, 8, array.shape[-1]), axis=0)
        return jnp.sum(array.reshape(8, -1, 128), axis=1)

    def total(values):
        sums = jnp.concatenate(values, axis=0)
        for level in levels:
            sums = sums + to_src(sums, level)
        sums = sums + to_pair(sums)
        sums = sums + to_core(sums)
        return jnp.sum(sums.reshape(len(values), -1), axis=1)

    def double(table, level):
        other = to_src(table, level)
        low = (src >> level) % 2 == 0
        return jnp.concatenate([jnp.where(low, table, other), jnp.where(low, other, table)], axis=0)

    whole = operator.reshape(plan.pairs, 2, block, 2, plan.sensors, plan.sources)
    start = right_side.reshape(block, rows, plan.sources)

    def half_of(k, which):
        size = (plan.pairs, 1, part, 2, plan.sensors, plan.sources)
        cut = lax.dynamic_slice(whole, (0, which, k * part, 0, 0, 0), size)
        return cut.reshape(plan.pairs, part, 2, plan.sensors, plan.sources)

    sent_b = [start[k * part:(k + 1) * part].astype(BF16) for k in chunks]
    got_b = [to_pair(sent) for sent in sent_b]
    other, *_ = lax.optimization_barrier((1 - core, *sent_b))
    far = [to_core(half_of(k, other)) for k in chunks]
    weights = double(noise_weights, 0)
    core_late, _ = lax.optimization_barrier((core, weights))
    near = [half_of(k, core_late) for k in chunks]

    for level in levels[1:]:
        weights = double(weights, level)
    weights = weights.reshape(plan.pairs, 2, block, plan.sensors)
    weights_near = lax.dynamic_index_in_dim(weights, core, 1, keepdims=False)
    weights_far = to_core(lax.dynamic_index_in_dim(weights, 1 - core, 1, keepdims=False))
    weights = jnp.concatenate([weights_near, weights_far], axis=-1)
    weights = lax.dynamic_index_in_dim(weights, pair ^ half, 0, keepdims=False)
    damping_row = jnp.where(half == 0, damping, to_pair(damping))
    first_row = sum(((src >> level) & 1) * ((part * rows) >> level) for level in levels[1:])
    count = max(1, plan.piece // rows)

    def piece_of(k, table):
        cut = lax.dynamic_slice_in_dim(table, k * part + first_row // rows, count, 0)
        return cut.reshape(count, 1, -1)

    def reduce_field(send, keep):
        keep, got = keep.reshape(part * rows, -1), to_src(send, 0).reshape(part * rows, -1)
        for level in levels[1:]:
            send, keep = fold_call(plan, level, meta, keep, got)
            got = to_src(send, level)
        mine = keep.astype(F32) + got.astype(F32)
        return mine.reshape(count, plan.piece // count, -1)

    def gather_field(weighted):
        own = weighted.astype(BF16).reshape(plan.piece, -1)
        for level in reversed(levels[1:]):
            own = join_call(plan, level, meta, own, to_src(own, level))
        own = own.reshape(part, rows, -1)
        return own, to_src(own, 0)

    field, products = [], []
    for k in chunks:
        send, keep = forward_call(plan, k, meta, near[k], far[k], True, (start, got_b[k]))
        field.append(reduce_field(send, keep))
    scaled = [piece_of(k, weights) * field[k] for k in chunks]
    damp = damping[:, None, None]
    start_late, _ = lax.optimization_barrier((start, got_b[-1]))
    sums = total([
        lanes(start_late * start_late),
        lanes(damp * start_late * start_late) + sum(lanes(scaled[k] * field[k]) for k in chunks),
    ])
    norm_0, curve_0 = sums[0], sums[1]
    alpha_0 = norm_0 / curve_0
    for k in chunks:
        back = adjoint_call(plan, meta, near[k], far[k], gather_field(scaled[k]), False)
        products.append((back, to_pair(back)))
    alpha_0, products[0] = lax.optimization_barrier((alpha_0, products[0]))

    image_0 = jnp.concatenate([mine[0].astype(F32) + got[1].astype(F32) for mine, got in products])
    image_0 = image_0 + damp * start
    residual = start - alpha_0 * image_0

    new_scaled, square, cross = [], 0.0, 0.0
    for k in chunks:
        send, keep = forward_call(plan, k, meta, near[k], far[k], False, products[k])
        factor = 1.0 - alpha_0 * piece_of(k, damping_row)
        new_field = factor * field[k] - alpha_0 * reduce_field(send, keep)
        new_scaled.append(piece_of(k, weights) * new_field)
        square = square + lanes(new_scaled[k] * new_field)
        cross = cross + lanes(new_scaled[k] * field[k])
    damped = damp * residual
    sums = total([
        lanes(residual * residual),
        lanes(damped * residual) + square,
        lanes(damped * start) + cross,
    ])
    norm_1 = sums[0]
    beta = norm_1 / norm_0
    curve_1 = sums[1] + 2.0 * beta * sums[2] + beta * beta * curve_0
    alpha_1 = norm_1 / curve_1

    final = []
    for k in chunks:
        halves = gather_field(new_scaled[k])
        if k == plan.chunks - 1:
            alpha_1, halves = lax.optimization_barrier((alpha_1, halves))
        sent, own = adjoint_call(plan, meta, near[k], far[k], halves, True)
        final.append(own + to_pair(sent).astype(F32))
    image_1 = jnp.concatenate(final) + damp * residual + beta * image_0
    solution = alpha_0 * start + alpha_1 * (residual + beta * start)
    residual = residual - alpha_1 * image_1
    return solution.reshape(right_side.shape), residual.reshape(right_side.shape)


def solution(mesh):
    in_specs = (
        P(None, None, "sens", "src"),
        P("sens", None, None, "src"),
        P("src", "sens"),
        P("sens"),
    )
    out_specs = (P("sens", None, None, "src"), P("sens", None, None, "src"))
    shard = functools.partial(body, mesh.shape["sens"], mesh.shape["src"])
    return jax.shard_map(shard, mesh=mesh, in_specs=in_specs, out_specs=out_specs, check_vma=False)
```

```python
import functools

import jax
import jax.numpy as jnp
from jax import lax
from jax.experimental import pallas as pl
from jax.experimental.pallas import tpu as pltpu
from jax.sharding import PartitionSpec as P

CHUNKS = 2
KERNEL_BYTES = 16 * 2 ** 20
F32 = jnp.float32
BF16 = jnp.bfloat16
ANYWHERE = pl.BlockSpec(memory_space=pl.ANY)
NT = (((1,), (1,)), ((), ()))
NN = (((1,), (0,)), ((), ()))


def largest_divisor(extent, most):
    return next(size for size in range(min(extent, most), 0, -1) if extent % size == 0)


def turned(block, sign):
    half = block.shape[0] // 2
    upper, lower = block[:half], block[half:]
    return jnp.concatenate([-lower, upper] if sign < 0 else [lower, -upper], axis=0)


def forward_rows(vector, near, far):
    left = jnp.concatenate([vector, turned(vector, -1)], axis=1)
    right = jnp.concatenate(
        [jnp.concatenate([part[0], part[1]], axis=1) for part in (near, far)], axis=0
    )
    return lax.dot_general(left, right, NT, preferred_element_type=F32)


def adjoint_rows(field, near, far):
    sensors = near.shape[1]
    total = None
    for part, piece in ((near, field[:, :sensors]), (far, field[:, sensors:])):
        left = jnp.concatenate([piece, turned(piece, 1)], axis=1)
        right = part.reshape(2 * sensors, part.shape[2])
        term = lax.dot_general(left, right, NN, preferred_element_type=F32)
        total = term if total is None else total + term
    return total


def cost(flops, moved):
    return pl.CostEstimate(flops=flops, bytes_accessed=moved, transcendentals=0)


class Plan:
    def __init__(self, operator, right_side, n_sens, n_src, chunks):
        self.freqs, _, self.sensors, self.sources = operator.shape
        self.block = right_side.shape[0]
        self.rows = right_side.shape[1] * right_side.shape[2]
        self.pairs = n_sens // 2
        self.groups = n_src // 2
        self.chunks = chunks
        self.part = self.block // chunks
        self.step = largest_divisor(self.part, 8)
        self.steps = self.part // self.step
        self.flops = 16 * self.part * self.rows * self.sensors * self.sources * 2
        self.piece = self.part * self.rows // self.groups


def part_spec(plan, blk_of):
    return pl.BlockSpec(
        (None, plan.step, 2, plan.sensors, plan.sources),
        lambda p, t, m: (m[0] ^ blk_of(p, m), t, 0, 0, 0),
    )


def forward_call(plan, chunk, meta, near, far, first, vectors, wait=()):
    blk_of = lambda p, m: 1 - (m[2] ^ p)
    step, steps = plan.step, plan.steps

    def kernel(m, near_ref, far_ref, one_ref, two_ref, *refs):
        send_ref, keep_ref = refs[len(wait):]
        phase = pl.program_id(0)
        blk = blk_of(phase, m)

        def run(pick, out_ref):
            for f in range(step):
                out_ref[f] = forward_rows(pick(f), near_ref[f], far_ref[f]).astype(out_ref.dtype)

        def both(pick):
            @pl.when(phase == 0)
            def _():
                run(pick, send_ref)

            @pl.when(phase == 1)
            def _():
                run(pick, keep_ref)

        if first:
            def pick(f):
                own = one_ref[f].astype(BF16)
                return jnp.where(blk == 0, own, two_ref[f])

            both(pick)
        else:
            both(lambda f: (one_ref[f].astype(F32) + two_ref[f].astype(F32)).astype(BF16))

    size = (step, plan.rows, plan.sources)
    if first:
        vec_specs = [
            pl.BlockSpec(size, lambda p, t, m: (chunk * steps + t, 0, 0)),
            pl.BlockSpec(size, lambda p, t, m: (t, 0, 0)),
        ]
    else:
        vec_specs = [
            pl.BlockSpec((None,) + size, lambda p, t, m: (blk_of(p, m), t, 0, 0)),
            pl.BlockSpec((None,) + size, lambda p, t, m: (1 - blk_of(p, m), t, 0, 0)),
        ]
    out = (step, plan.rows, 2 * plan.sensors)
    shape = (plan.part, plan.rows, 2 * plan.sensors)
    return pl.pallas_call(
        kernel,
        grid_spec=pltpu.PrefetchScalarGridSpec(
            num_scalar_prefetch=1,
            grid=(2, steps),
            in_specs=[part_spec(plan, blk_of)] * 2 + vec_specs + [ANYWHERE] * len(wait),
            out_specs=[
                pl.BlockSpec(out, lambda p, t, m: (jnp.where(p == 0, t, steps - 1), 0, 0)),
                pl.BlockSpec(out, lambda p, t, m: (jnp.where(p == 0, 0, t), 0, 0)),
            ],
        ),
        out_shape=[jax.ShapeDtypeStruct(shape, BF16)] * 2,
        cost_estimate=cost(plan.flops, 16 * plan.part * plan.sensors * plan.sources),
        compiler_params=pltpu.CompilerParams(vmem_limit_bytes=KERNEL_BYTES),
        name="forward",
    )(meta, near, far, *vectors, *wait)


def adjoint_call(plan, meta, near, far, halves, last, wait=()):
    blk_of = lambda p, m: 1 - p
    step, steps = plan.step, plan.steps

    def kernel(m, near_ref, far_ref, own_ref, got_ref, *outs):
        outs = outs[len(wait):]
        phase = pl.program_id(0)
        mine = blk_of(phase, m) == m[2]

        def run(out_ref):
            for f in range(step):
                field = jnp.where(mine, own_ref[f], got_ref[f])
                out_ref[f] = adjoint_rows(field, near_ref[f], far_ref[f]).astype(out_ref.dtype)

        if last:
            @pl.when(phase == 0)
            def _():
                run(outs[0])

            @pl.when(phase == 1)
            def _():
                run(outs[1])
        else:
            run(outs[0])

    size = (step, plan.rows, 2 * plan.sensors)
    out = (step, plan.rows, plan.sources)
    shape = (plan.part, plan.rows, plan.sources)
    if last:
        out_specs = [
            pl.BlockSpec(out, lambda p, t, m: (jnp.where(p == 0, t, steps - 1), 0, 0)),
            pl.BlockSpec(out, lambda p, t, m: (jnp.where(p == 0, 0, t), 0, 0)),
        ]
        out_shape = [jax.ShapeDtypeStruct(shape, BF16), jax.ShapeDtypeStruct(shape, F32)]
    else:
        out_specs = pl.BlockSpec((None,) + out, lambda p, t, m: (blk_of(p, m), t, 0, 0))
        out_shape = jax.ShapeDtypeStruct((2,) + shape, BF16)
    return pl.pallas_call(
        kernel,
        grid_spec=pltpu.PrefetchScalarGridSpec(
            num_scalar_prefetch=1,
            grid=(2, steps),
            in_specs=[
                part_spec(plan, blk_of),
                part_spec(plan, blk_of),
                pl.BlockSpec(size, lambda p, t, m: (t, 0, 0)),
                pl.BlockSpec(size, lambda p, t, m: (t, 0, 0)),
            ] + [ANYWHERE] * len(wait),
            out_specs=out_specs,
        ),
        out_shape=out_shape,
        cost_estimate=cost(plan.flops, 16 * plan.part * plan.sensors * plan.sources),
        compiler_params=pltpu.CompilerParams(vmem_limit_bytes=KERNEL_BYTES),
        name="adjoint",
    )(meta, near, far, *halves, *wait)


def split_call(plan, meta, keep, got):
    piece, groups = plan.piece, plan.groups
    width = keep.shape[-1]

    def kernel(m, keep_ref, got_ref, mine_ref, *sends):
        for d in range(groups):
            place = pl.ds(pl.multiple_of((m[3] ^ d) * piece, piece), piece)
            total = keep_ref[place].astype(F32) + got_ref[place].astype(F32)
            if d == 0:
                mine_ref[...] = total
            else:
                sends[d - 1][...] = total.astype(BF16)

    whole = pl.BlockSpec(memory_space=pltpu.VMEM)
    return pl.pallas_call(
        kernel,
        in_specs=[pl.BlockSpec(memory_space=pltpu.SMEM), whole, whole],
        out_specs=[whole] * groups,
        out_shape=[jax.ShapeDtypeStruct((piece, width), F32)]
        + [jax.ShapeDtypeStruct((piece, width), BF16)] * (groups - 1),
        cost_estimate=cost(groups * piece * width, groups * piece * width * 8),
        compiler_params=pltpu.CompilerParams(vmem_limit_bytes=KERNEL_BYTES),
        name="split",
    )(meta, keep.reshape(-1, width), got.reshape(-1, width))


def place_call(plan, meta, pieces):
    piece, groups = plan.piece, plan.groups
    width = pieces[0].shape[-1]

    def kernel(m, *refs):
        for d in range(groups):
            place = pl.ds(pl.multiple_of((m[3] ^ d) * piece, piece), piece)
            refs[groups][place] = refs[d][...]

    whole = pl.BlockSpec(memory_space=pltpu.VMEM)
    out = pl.pallas_call(
        kernel,
        in_specs=[pl.BlockSpec(memory_space=pltpu.SMEM)] + [whole] * groups,
        out_specs=whole,
        out_shape=jax.ShapeDtypeStruct((groups * piece, width), BF16),
        cost_estimate=cost(0, groups * piece * width * 4),
        compiler_params=pltpu.CompilerParams(vmem_limit_bytes=KERNEL_BYTES),
        name="place",
    )(meta, *pieces)
    return out.reshape(plan.part, plan.rows, width)


def ordered(array, *earlier):
    def kernel(*refs):
        del refs

    return pl.pallas_call(
        kernel,
        in_specs=[ANYWHERE] * (1 + len(earlier)),
        out_specs=ANYWHERE,
        out_shape=jax.ShapeDtypeStruct(array.shape, array.dtype),
        input_output_aliases={0: 0},
        cost_estimate=cost(0, 0),
        compiler_params=pltpu.CompilerParams(vmem_limit_bytes=KERNEL_BYTES),
        name="ordered",
    )(array, *earlier)


def lanes(array):
    total = jnp.sum(array.reshape(-1, 8, array.shape[-1]), axis=0)
    return sum(total[:, i:i + 128] for i in range(0, array.shape[-1], 128))


def sensor_call(plan, chunk, meta, weights, pieces, alpha=None, damping=None, old=None):
    piece, rows, groups = plan.piece, plan.rows, plan.groups
    width = pieces[0].shape[-1]
    count = max(1, piece // rows)
    high = piece // count
    second = old is not None

    def kernel(m, *refs):
        if second:
            alpha_ref, damp_ref, old_ref, *refs = refs
        weights_ref, *refs = refs
        ins, (out_ref, *more) = refs[:groups], refs[groups:]
        stats_ref = more[-1]
        square = cross = jnp.zeros((8, 128), F32)
        for c in range(count):
            at = pl.ds(c * high, high)
            freq = chunk * plan.part + (m[3] * piece + c * high) // rows
            field = ins[0][at]
            for ref in ins[1:]:
                field = field + ref[at].astype(F32)
            if second:
                factor = 1.0 - alpha_ref[0] * damp_ref[freq]
                field = factor * old_ref[at] - alpha_ref[0] * field
            scaled = weights_ref[pl.ds(freq, 1)] * field
            out_ref[at] = scaled.astype(BF16)
            square = square + lanes(scaled * field)
            if second:
                cross = cross + lanes(scaled * old_ref[at])
            else:
                more[0][at] = field
        stats_ref[0:8] = square
        stats_ref[8:16] = cross

    whole = pl.BlockSpec(memory_space=pltpu.VMEM)
    scalars = pl.BlockSpec(memory_space=pltpu.SMEM)
    first_out = [] if second else [jax.ShapeDtypeStruct((piece, width), F32)]
    extra = (alpha, damping, old) if second else ()
    out_shape = [jax.ShapeDtypeStruct((piece, width), BF16)] + first_out
    out_shape = out_shape + [jax.ShapeDtypeStruct((16, 128), F32)]
    return pl.pallas_call(
        kernel,
        in_specs=[scalars] + ([scalars] * 2 + [whole] if second else []) + [whole] * (1 + groups),
        out_specs=[whole] * len(out_shape),
        out_shape=out_shape,
        cost_estimate=cost(8 * piece * width, 16 * piece * width),
        compiler_params=pltpu.CompilerParams(vmem_limit_bytes=KERNEL_BYTES),
        name="sensor",
    )(meta, *extra, weights, *pieces)


def norms_call(plan, damping, start):
    def kernel(damp_ref, start_ref, stats_ref):
        plain = damped = jnp.zeros((8, 128), F32)
        for f in range(plan.block):
            term = lanes(start_ref[f] * start_ref[f])
            plain = plain + term
            damped = damped + damp_ref[f] * term
        stats_ref[0:8] = plain
        stats_ref[8:16] = damped

    whole = pl.BlockSpec(memory_space=pltpu.VMEM)
    return pl.pallas_call(
        kernel,
        in_specs=[pl.BlockSpec(memory_space=pltpu.SMEM), whole],
        out_specs=whole,
        out_shape=jax.ShapeDtypeStruct((16, 128), F32),
        cost_estimate=cost(2 * start.size, 4 * start.size),
        compiler_params=pltpu.CompilerParams(vmem_limit_bytes=KERNEL_BYTES),
        name="norms",
    )(damping, start)


def residual_call(plan, chunk, alpha, damping, start, mine, got):
    part, rows, sources = plan.part, plan.rows, plan.sources

    def kernel(alpha_ref, damp_ref, start_ref, mine_ref, got_ref, image_ref, out_ref, stats_ref):
        plain = damped = mixed = jnp.zeros((8, 128), F32)
        for f in range(part):
            damp = damp_ref[chunk * part + f]
            begin = start_ref[f]
            image = mine_ref[f].astype(F32) + got_ref[f].astype(F32) + damp * begin
            residual = begin - alpha_ref[0] * image
            image_ref[f] = image
            out_ref[f] = residual
            term = lanes(residual * residual)
            plain = plain + term
            damped = damped + damp * term
            mixed = mixed + damp * lanes(residual * begin)
        stats_ref[0:8] = plain
        stats_ref[8:16] = damped
        stats_ref[16:24] = mixed

    block = (part, rows, sources)
    scalars = pl.BlockSpec(memory_space=pltpu.SMEM)
    out = jax.ShapeDtypeStruct(block, F32)
    return pl.pallas_call(
        kernel,
        grid=(1,),
        in_specs=[
            scalars,
            scalars,
            pl.BlockSpec(block, lambda i: (chunk, 0, 0)),
            pl.BlockSpec((None,) + block, lambda i: (0, 0, 0, 0)),
            pl.BlockSpec((None,) + block, lambda i: (1, 0, 0, 0)),
        ],
        out_specs=[
            pl.BlockSpec(block, lambda i: (0, 0, 0)),
            pl.BlockSpec(block, lambda i: (0, 0, 0)),
            pl.BlockSpec((24, 128), lambda i: (0, 0)),
        ],
        out_shape=[out, out, jax.ShapeDtypeStruct((24, 128), F32)],
        cost_estimate=cost(8 * part * rows * sources, 16 * part * rows * sources),
        compiler_params=pltpu.CompilerParams(vmem_limit_bytes=KERNEL_BYTES),
        name="residual",
    )(alpha, damping, start, mine, got)


def body(n_sens, n_src, operator, right_side, noise_weights, damping):
    plan = Plan(operator, right_side, n_sens, n_src, CHUNKS)
    sens, src = lax.axis_index("sens"), lax.axis_index("src")
    pair, core, half, group = sens // 2, sens % 2, src % 2, src // 2
    meta = jnp.stack([pair, core, half, group]).astype(jnp.int32)
    part, rows, block = plan.part, plan.rows, plan.block
    levels = range(n_src.bit_length() - 1)
    chunks = range(plan.chunks)

    def to_core(array):
        return lax.ppermute(array, "sens", [(i, i ^ 1) for i in range(n_sens)])

    def to_pair(array):
        return lax.ppermute(array, "sens", [(i, i ^ 2) for i in range(n_sens)])

    def to_src(array, step):
        return lax.ppermute(array, "src", [(j, j ^ step) for j in range(n_src)])

    def in_turn(arrays, move):
        moved = []
        for k, array in enumerate(arrays):
            if k > 0:
                array = arrays[k] = ordered(array, moved[-1])
            moved.append(move(array))
        return moved

    def total(sums):
        steps = [sums]
        for level in levels:
            steps.append(steps[-1] + to_src(steps[-1], 1 << level))
        steps.append(steps[-1] + to_pair(steps[-1]))
        steps.append(steps[-1] + to_core(steps[-1]))
        return jnp.sum(steps[-1].reshape(-1, 8 * 128), axis=1), steps

    def double(table, level):
        other = to_src(table, 1 << level)
        low = (src >> level) % 2 == 0
        return jnp.concatenate([jnp.where(low, table, other), jnp.where(low, other, table)], axis=0)

    whole = operator.reshape(plan.pairs, 2, block, 2, plan.sensors, plan.sources)
    start = right_side.reshape(block, rows, plan.sources)

    def half_of(k, which):
        size = (plan.pairs, 1, part, 2, plan.sensors, plan.sources)
        cut = lax.dynamic_slice(whole, (0, which, k * part, 0, 0, 0), size)
        return cut.reshape(plan.pairs, part, 2, plan.sensors, plan.sources)

    sent_b = [start[k * part:(k + 1) * part].astype(BF16) for k in chunks]
    got_b = [to_pair(sent) for sent in sent_b]
    now = ordered(meta, *sent_b)[1]
    weights = double(noise_weights, 0)

    for level in levels[1:]:
        weights = double(weights, level)
    weights = weights.reshape(plan.pairs, 2, block, plan.sensors)
    weights_near = lax.dynamic_index_in_dim(weights, core, 1, keepdims=False)
    weights_far = to_core(lax.dynamic_index_in_dim(weights, 1 - core, 1, keepdims=False))
    weights = jnp.concatenate([weights_near, weights_far], axis=-1)
    weights = lax.dynamic_index_in_dim(weights, pair ^ half, 0, keepdims=False)
    damping_row = jnp.where(half == 0, damping, to_pair(damping))
    steps = [2 * d for d in range(1, plan.groups)]

    def reduce_field(keep, got):
        mine, *sends = split_call(plan, meta, keep, got)
        return [mine] + [to_src(piece, step) for piece, step in zip(sends, steps)]

    def gather_field(weighted):
        return place_call(plan, meta, [weighted] + [to_src(weighted, step) for step in steps])

    def to_half(array):
        return to_src(array, 1)

    near, far, pairs = [], [], []
    for k in chunks:
        far.append(to_core(half_of(k, 1 - now)))
        near.append(half_of(k, now))
        pairs.append(forward_call(plan, k, meta, near[k], far[k], True, (start, got_b[k])))
        now = ordered(meta, pairs[k][0])[1]
    got = in_turn([send for send, _ in pairs], to_half)
    pieces = [reduce_field(pairs[k][1], got[k]) for k in chunks]
    scaled, field, stats = zip(*[sensor_call(plan, k, meta, weights, pieces[k]) for k in chunks])
    norms = norms_call(plan, damping, start)
    sums, steps_0 = total(norms + jnp.pad(sum(one[0:8] for one in stats), ((8, 0), (0, 0))))
    norm_0, curve_0 = sums[0], sums[1]
    alpha_0 = (norm_0 / curve_0)[None]

    own = [gather_field(scaled[k]) for k in chunks]
    got = in_turn(own, to_half)
    back = []
    for k in chunks:
        wait = (steps_0[3],) if k == 0 else (steps_0[-1],)
        back.append(adjoint_call(plan, meta, near[k], far[k], (own[k], got[k]), False, wait))
    got_back = in_turn(back, to_pair)

    pairs = [
        forward_call(plan, k, meta, near[k], far[k], False, (back[k], got_back[k])) for k in chunks
    ]
    got = in_turn([send for send, _ in pairs], to_half)
    image_0, residual, norms = zip(*[
        residual_call(plan, k, alpha_0, damping, start, back[k], got_back[k]) for k in chunks
    ])
    pieces = [reduce_field(pairs[k][1], got[k]) for k in chunks]
    scaled, stats = zip(*[
        sensor_call(plan, k, meta, weights, pieces[k], alpha_0, damping_row, field[k])
        for k in chunks
    ])
    sums, steps_1 = total(sum(norms) + jnp.pad(sum(stats), ((8, 0), (0, 0))))
    norm_1 = sums[0]
    beta = norm_1 / norm_0
    curve_1 = sums[1] + 2.0 * beta * sums[2] + beta * beta * curve_0
    alpha_1 = norm_1 / curve_1

    own = [gather_field(scaled[k]) for k in chunks]
    got = in_turn(own, to_half)
    final = []
    for k in chunks:
        wait = (steps_1[3],) if k == 0 else (steps_1[-1],)
        sent, mine = adjoint_call(plan, meta, near[k], far[k], (own[k], got[k]), True, wait)
        final.append(mine + to_pair(sent).astype(F32))
    residual, image_0 = jnp.concatenate(residual), jnp.concatenate(image_0)
    image_1 = jnp.concatenate(final) + damping[:, None, None] * residual + beta * image_0
    solution = alpha_0 * start + alpha_1 * (residual + beta * start)
    residual = residual - alpha_1 * image_1
    return solution.reshape(right_side.shape), residual.reshape(right_side.shape)


def solution(mesh):
    in_specs = (
        P(None, None, "sens", "src"),
        P("sens", None, None, "src"),
        P("src", "sens"),
        P("sens"),
    )
    out_specs = (P("sens", None, None, "src"), P("sens", None, None, "src"))
    shard = functools.partial(body, mesh.shape["sens"], mesh.shape["src"])
    return jax.shard_map(shard, mesh=mesh, in_specs=in_specs, out_specs=out_specs, check_vma=False)
```

```python
import functools

import jax
import jax.numpy as jnp
from jax import lax
from jax.experimental import pallas as pl
from jax.experimental.pallas import tpu as pltpu
from jax.sharding import PartitionSpec as P

CHUNKS = 2
KERNEL_BYTES = 16 * 2 ** 20
F32 = jnp.float32
BF16 = jnp.bfloat16
ANYWHERE = pl.BlockSpec(memory_space=pl.ANY)
NT = (((1,), (1,)), ((), ()))
NN = (((1,), (0,)), ((), ()))


def largest_divisor(extent, most):
    return next(size for size in range(min(extent, most), 0, -1) if extent % size == 0)


def turned(block, sign):
    half = block.shape[0] // 2
    upper, lower = block[:half], block[half:]
    return jnp.concatenate([-lower, upper] if sign < 0 else [lower, -upper], axis=0)


def forward_rows(vector, near, far):
    left = jnp.concatenate([vector, turned(vector, -1)], axis=1)
    right = jnp.concatenate(
        [jnp.concatenate([part[0], part[1]], axis=1) for part in (near, far)], axis=0
    )
    return lax.dot_general(left, right, NT, preferred_element_type=F32)


def adjoint_rows(field, near, far):
    sensors = near[0].shape[0]
    total = None
    for part, piece in ((near, field[:, :sensors]), (far, field[:, sensors:])):
        left = jnp.concatenate([piece, turned(piece, 1)], axis=1)
        right = jnp.concatenate(part, axis=0)
        term = lax.dot_general(left, right, NN, preferred_element_type=F32)
        total = term if total is None else total + term
    return total


def cost(flops, moved):
    return pl.CostEstimate(flops=flops // 1000, bytes_accessed=moved // 1000, transcendentals=0)


class Plan:
    def __init__(self, operator, right_side, n_sens, n_src, chunks):
        self.freqs, _, self.sensors, self.sources = operator.shape
        self.block = right_side.shape[0]
        self.rows = right_side.shape[1] * right_side.shape[2]
        self.pairs = n_sens // 2
        self.groups = n_src // 2
        self.chunks = chunks
        self.part = self.block // chunks
        self.step = largest_divisor(self.part, 8)
        self.steps = self.part // self.step
        self.flops = 16 * self.part * self.rows * self.sensors * self.sources * 2
        self.piece = self.part * self.rows // self.groups


def part_specs(plan, blk_of):
    def spec(component):
        return pl.BlockSpec(
            (None, plan.step, None, plan.sensors, plan.sources),
            lambda p, t, m: (m[0] ^ blk_of(p, m), t, component, 0, 0),
        )

    return [spec(0), spec(1), spec(0), spec(1)]


def cut_call(plan, chunk, meta, whole, wait):
    block = (None, plan.step, 2, plan.sensors, plan.sources)
    base = chunk * plan.steps

    def kernel(m, one_ref, two_ref, *refs):
        far_ref, near_ref = refs[len(wait):]
        far_ref[...] = one_ref[...]
        near_ref[...] = two_ref[...]

    def source(core):
        return pl.BlockSpec(
            (None,) + block,
            lambda p, t, m: (p, core(m), base + t, 0, 0, 0),
            )

    out = jax.ShapeDtypeStruct((plan.pairs, plan.part, 2, plan.sensors, plan.sources), BF16)
    return pl.pallas_call(
        kernel,
        grid_spec=pltpu.PrefetchScalarGridSpec(
            num_scalar_prefetch=1,
            grid=(plan.pairs, plan.steps),
            in_specs=[source(lambda m: 1 - m[1]), source(lambda m: m[1])] + [ANYWHERE] * len(wait),
            out_specs=[pl.BlockSpec(block, lambda p, t, m: (p, t, 0, 0, 0))] * 2,
        ),
        out_shape=[out] * 2,
        cost_estimate=cost(0, 8 * plan.part * plan.sensors * plan.sources),
        compiler_params=pltpu.CompilerParams(vmem_limit_bytes=KERNEL_BYTES),
        name="cut",
    )(meta, whole, whole, *wait)


def forward_call(plan, chunk, meta, near, far, first, vectors, wait=()):
    blk_of = lambda p, m: 1 - (m[2] ^ p)
    step, steps = plan.step, plan.steps

    def kernel(m, near_0, near_1, far_0, far_1, one_ref, two_ref, *refs):
        send_ref, keep_ref = refs[len(wait):]
        phase = pl.program_id(0)
        blk = blk_of(phase, m)

        def run(pick, out_ref):
            for f in range(step):
                out_ref[f] = forward_rows(pick(f), (near_0[f], near_1[f]), (far_0[f], far_1[f])).astype(out_ref.dtype)

        def both(pick):
            @pl.when(phase == 0)
            def _():
                run(pick, send_ref)

            @pl.when(phase == 1)
            def _():
                run(pick, keep_ref)

        if first:
            def pick(f):
                own = one_ref[f].astype(BF16)
                return jnp.where(blk == 0, own, two_ref[f])

            both(pick)
        else:
            both(lambda f: (one_ref[f].astype(F32) + two_ref[f].astype(F32)).astype(BF16))

    size = (step, plan.rows, plan.sources)
    if first:
        vec_specs = [
            pl.BlockSpec(size, lambda p, t, m: (chunk * steps + t, 0, 0)),
            pl.BlockSpec(size, lambda p, t, m: (t, 0, 0)),
        ]
    else:
        vec_specs = [
            pl.BlockSpec((None,) + size, lambda p, t, m: (blk_of(p, m), t, 0, 0)),
            pl.BlockSpec((None,) + size, lambda p, t, m: (1 - blk_of(p, m), t, 0, 0)),
        ]
    out = (step, plan.rows, 2 * plan.sensors)
    shape = (plan.part, plan.rows, 2 * plan.sensors)
    return pl.pallas_call(
        kernel,
        grid_spec=pltpu.PrefetchScalarGridSpec(
            num_scalar_prefetch=1,
            grid=(2, steps),
            in_specs=part_specs(plan, blk_of) + vec_specs + [ANYWHERE] * len(wait),
            out_specs=[
                pl.BlockSpec(out, lambda p, t, m: (jnp.where(p == 0, t, steps - 1), 0, 0)),
                pl.BlockSpec(out, lambda p, t, m: (jnp.where(p == 0, 0, t), 0, 0)),
            ],
        ),
        out_shape=[jax.ShapeDtypeStruct(shape, BF16)] * 2,
        cost_estimate=cost(plan.flops, 16 * plan.part * plan.sensors * plan.sources),
        compiler_params=pltpu.CompilerParams(vmem_limit_bytes=KERNEL_BYTES),
        name="forward",
    )(meta, near, near, far, far, *vectors, *wait)


def adjoint_call(plan, meta, near, far, halves, last, wait=()):
    blk_of = lambda p, m: 1 - p
    step, steps = plan.step, plan.steps

    def kernel(m, near_0, near_1, far_0, far_1, own_ref, got_ref, *outs):
        outs = outs[len(wait):]
        phase = pl.program_id(0)
        mine = blk_of(phase, m) == m[2]

        def run(out_ref):
            for f in range(step):
                field = jnp.where(mine, own_ref[f], got_ref[f])
                out_ref[f] = adjoint_rows(field, (near_0[f], near_1[f]), (far_0[f], far_1[f])).astype(out_ref.dtype)

        if last:
            @pl.when(phase == 0)
            def _():
                run(outs[0])

            @pl.when(phase == 1)
            def _():
                run(outs[1])
        else:
            run(outs[0])

    size = (step, plan.rows, 2 * plan.sensors)
    out = (step, plan.rows, plan.sources)
    shape = (plan.part, plan.rows, plan.sources)
    if last:
        out_specs = [
            pl.BlockSpec(out, lambda p, t, m: (jnp.where(p == 0, t, steps - 1), 0, 0)),
            pl.BlockSpec(out, lambda p, t, m: (jnp.where(p == 0, 0, t), 0, 0)),
        ]
        out_shape = [jax.ShapeDtypeStruct(shape, BF16), jax.ShapeDtypeStruct(shape, F32)]
    else:
        out_specs = pl.BlockSpec((None,) + out, lambda p, t, m: (blk_of(p, m), t, 0, 0))
        out_shape = jax.ShapeDtypeStruct((2,) + shape, BF16)
    return pl.pallas_call(
        kernel,
        grid_spec=pltpu.PrefetchScalarGridSpec(
            num_scalar_prefetch=1,
            grid=(2, steps),
            in_specs=part_specs(plan, blk_of) + [
                pl.BlockSpec(size, lambda p, t, m: (t, 0, 0)),
                pl.BlockSpec(size, lambda p, t, m: (t, 0, 0)),
            ] + [ANYWHERE] * len(wait),
            out_specs=out_specs,
        ),
        out_shape=out_shape,
        cost_estimate=cost(plan.flops, 16 * plan.part * plan.sensors * plan.sources),
        compiler_params=pltpu.CompilerParams(vmem_limit_bytes=KERNEL_BYTES),
        name="adjoint",
    )(meta, near, near, far, far, *halves, *wait)


def split_call(plan, meta, keep, got):
    piece, groups = plan.piece, plan.groups
    width = keep.shape[-1]

    def kernel(m, keep_ref, got_ref, mine_ref, *sends):
        for d in range(groups):
            place = pl.ds(pl.multiple_of((m[3] ^ d) * piece, piece), piece)
            total = keep_ref[place].astype(F32) + got_ref[place].astype(F32)
            if d == 0:
                mine_ref[...] = total
            else:
                sends[d - 1][...] = total.astype(BF16)

    whole = pl.BlockSpec(memory_space=pltpu.VMEM)
    return pl.pallas_call(
        kernel,
        in_specs=[pl.BlockSpec(memory_space=pltpu.SMEM), whole, whole],
        out_specs=[whole] * groups,
        out_shape=[jax.ShapeDtypeStruct((piece, width), F32)]
        + [jax.ShapeDtypeStruct((piece, width), BF16)] * (groups - 1),
        cost_estimate=cost(groups * piece * width, groups * piece * width * 8),
        compiler_params=pltpu.CompilerParams(vmem_limit_bytes=KERNEL_BYTES),
        name="split",
    )(meta, keep.reshape(-1, width), got.reshape(-1, width))


def place_call(plan, meta, pieces):
    piece, groups = plan.piece, plan.groups
    width = pieces[0].shape[-1]

    def kernel(m, *refs):
        for d in range(groups):
            place = pl.ds(pl.multiple_of((m[3] ^ d) * piece, piece), piece)
            refs[groups][place] = refs[d][...]

    whole = pl.BlockSpec(memory_space=pltpu.VMEM)
    out = pl.pallas_call(
        kernel,
        in_specs=[pl.BlockSpec(memory_space=pltpu.SMEM)] + [whole] * groups,
        out_specs=whole,
        out_shape=jax.ShapeDtypeStruct((groups * piece, width), BF16),
        cost_estimate=cost(0, groups * piece * width * 4),
        compiler_params=pltpu.CompilerParams(vmem_limit_bytes=KERNEL_BYTES),
        name="place",
    )(meta, *pieces)
    return out.reshape(plan.part, plan.rows, width)


def ordered(array, *earlier):
    def kernel(*refs):
        del refs

    return pl.pallas_call(
        kernel,
        in_specs=[ANYWHERE] * (1 + len(earlier)),
        out_specs=ANYWHERE,
        out_shape=jax.ShapeDtypeStruct(array.shape, array.dtype),
        input_output_aliases={0: 0},
        cost_estimate=cost(0, 0),
        compiler_params=pltpu.CompilerParams(vmem_limit_bytes=KERNEL_BYTES),
        name="ordered",
    )(array, *earlier)


def lanes(array):
    total = jnp.sum(array.reshape(-1, 8, array.shape[-1]), axis=0)
    return sum(total[:, i:i + 128] for i in range(0, array.shape[-1], 128))


def sensor_call(plan, chunk, meta, weights, pieces, norms, alpha=None, damping=None, old=None):
    piece, rows, groups = plan.piece, plan.rows, plan.groups
    width = pieces[0].shape[-1]
    count = max(1, piece // rows)
    high = piece // count
    second = old is not None

    def kernel(m, *refs):
        if second:
            alpha_ref, damp_ref, old_ref, *refs = refs
        weights_ref, norms_ref, *refs = refs
        ins, (out_ref, *more) = refs[:groups], refs[groups:]
        stats_ref = more[-1]
        square = cross = jnp.zeros((8, 128), F32)
        for c in range(count):
            at = pl.ds(c * high, high)
            freq = chunk * plan.part + (m[3] * piece + c * high) // rows
            field = ins[0][at]
            for ref in ins[1:]:
                field = field + ref[at].astype(F32)
            if second:
                factor = 1.0 - alpha_ref[0] * damp_ref[freq]
                field = factor * old_ref[at] - alpha_ref[0] * field
            scaled = weights_ref[pl.ds(freq, 1)] * field
            out_ref[at] = scaled.astype(BF16)
            square = square + lanes(scaled * field)
            if second:
                cross = cross + lanes(scaled * old_ref[at])
            else:
                more[0][at] = field
        stats_ref[0:8] = norms_ref[0:8]
        stats_ref[8:16] = norms_ref[8:16] + square
        stats_ref[16:24] = norms_ref[16:24] + cross

    whole = pl.BlockSpec(memory_space=pltpu.VMEM)
    scalars = pl.BlockSpec(memory_space=pltpu.SMEM)
    first_out = [] if second else [jax.ShapeDtypeStruct((piece, width), F32)]
    extra = (alpha, damping, old) if second else ()
    out_shape = [jax.ShapeDtypeStruct((piece, width), BF16)] + first_out
    out_shape = out_shape + [jax.ShapeDtypeStruct((24, 128), F32)]
    return pl.pallas_call(
        kernel,
        in_specs=[scalars] + ([scalars] * 2 + [whole] if second else []) + [whole] * (2 + groups),
        out_specs=[whole] * len(out_shape),
        out_shape=out_shape,
        cost_estimate=cost(8 * piece * width, 16 * piece * width),
        compiler_params=pltpu.CompilerParams(vmem_limit_bytes=KERNEL_BYTES),
        name="sensor",
    )(meta, *extra, weights, norms, *pieces)


def norms_call(plan, chunk, damping, start):
    block = (plan.part, plan.rows, plan.sources)

    def kernel(damp_ref, start_ref, stats_ref):
        plain = damped = jnp.zeros((8, 128), F32)
        for f in range(plan.part):
            term = lanes(start_ref[f] * start_ref[f])
            plain = plain + term
            damped = damped + damp_ref[chunk * plan.part + f] * term
        stats_ref[0:8] = plain
        stats_ref[8:16] = damped
        stats_ref[16:24] = jnp.zeros((8, 128), F32)

    return pl.pallas_call(
        kernel,
        grid=(1,),
        in_specs=[
            pl.BlockSpec(memory_space=pltpu.SMEM),
            pl.BlockSpec(block, lambda i: (chunk, 0, 0)),
        ],
        out_specs=pl.BlockSpec((24, 128), lambda i: (0, 0)),
        out_shape=jax.ShapeDtypeStruct((24, 128), F32),
        cost_estimate=cost(2 * start.size, 4 * start.size),
        compiler_params=pltpu.CompilerParams(vmem_limit_bytes=KERNEL_BYTES),
        name="norms",
    )(damping, start)


def residual_call(plan, chunk, alpha, damping, start, mine, got):
    part, rows, sources = plan.part, plan.rows, plan.sources

    def kernel(alpha_ref, damp_ref, start_ref, mine_ref, got_ref, image_ref, out_ref, stats_ref):
        plain = damped = mixed = jnp.zeros((8, 128), F32)
        for f in range(part):
            damp = damp_ref[chunk * part + f]
            begin = start_ref[f]
            image = mine_ref[f].astype(F32) + got_ref[f].astype(F32) + damp * begin
            residual = begin - alpha_ref[0] * image
            image_ref[f] = image
            out_ref[f] = residual
            term = lanes(residual * residual)
            plain = plain + term
            damped = damped + damp * term
            mixed = mixed + damp * lanes(residual * begin)
        stats_ref[0:8] = plain
        stats_ref[8:16] = damped
        stats_ref[16:24] = mixed

    block = (part, rows, sources)
    scalars = pl.BlockSpec(memory_space=pltpu.SMEM)
    out = jax.ShapeDtypeStruct(block, F32)
    return pl.pallas_call(
        kernel,
        grid=(1,),
        in_specs=[
            scalars,
            scalars,
            pl.BlockSpec(block, lambda i: (chunk, 0, 0)),
            pl.BlockSpec((None,) + block, lambda i: (0, 0, 0, 0)),
            pl.BlockSpec((None,) + block, lambda i: (1, 0, 0, 0)),
        ],
        out_specs=[
            pl.BlockSpec(block, lambda i: (0, 0, 0)),
            pl.BlockSpec(block, lambda i: (0, 0, 0)),
            pl.BlockSpec((24, 128), lambda i: (0, 0)),
        ],
        out_shape=[out, out, jax.ShapeDtypeStruct((24, 128), F32)],
        cost_estimate=cost(8 * part * rows * sources, 16 * part * rows * sources),
        compiler_params=pltpu.CompilerParams(vmem_limit_bytes=KERNEL_BYTES),
        name="residual",
    )(alpha, damping, start, mine, got)


def body(n_sens, n_src, operator, right_side, noise_weights, damping):
    plan = Plan(operator, right_side, n_sens, n_src, CHUNKS)
    sens, src = lax.axis_index("sens"), lax.axis_index("src")
    pair, core, half, group = sens // 2, sens % 2, src % 2, src // 2
    meta = jnp.stack([pair, core, half, group]).astype(jnp.int32)
    part, rows, block = plan.part, plan.rows, plan.block
    levels = range(n_src.bit_length() - 1)
    chunks = range(plan.chunks)

    def to_core(array):
        return lax.ppermute(array, "sens", [(i, i ^ 1) for i in range(n_sens)])

    def to_pair(array):
        return lax.ppermute(array, "sens", [(i, i ^ 2) for i in range(n_sens)])

    def to_src(array, step):
        return lax.ppermute(array, "src", [(j, j ^ step) for j in range(n_src)])

    def in_turn(arrays, move):
        moved = []
        for k, array in enumerate(arrays):
            if k > 0:
                array = arrays[k] = ordered(array, moved[-1])
            moved.append(move(array))
        return moved

    def total(sums):
        steps = [sums]
        steps.append(steps[-1] + to_core(steps[-1]))
        steps.append(steps[-1] + to_pair(steps[-1]))
        for level in reversed(levels):
            steps.append(steps[-1] + to_src(steps[-1], 1 << level))
        return jnp.sum(steps[-1].reshape(-1, 8 * 128), axis=1), steps

    def double(table, level):
        other = to_src(table, 1 << level)
        low = (src >> level) % 2 == 0
        return jnp.concatenate([jnp.where(low, table, other), jnp.where(low, other, table)], axis=0)

    whole = operator.reshape(plan.pairs, 2, block, 2, plan.sensors, plan.sources)
    start = right_side.reshape(block, rows, plan.sources)

    sent_b = [start[k * part:(k + 1) * part].astype(BF16) for k in chunks]
    got_b = in_turn(list(sent_b), to_pair)
    near, far, wait, weights = [], [], tuple(sent_b), noise_weights
    for k in chunks:
        sent, mine = cut_call(plan, k, meta, whole, wait)
        near.append(mine)
        far.append(to_core(sent))
        if k == 0:
            weights = double(ordered(weights, sent), 0)
        wait = (weights,)

    for level in levels[1:]:
        weights = double(weights, level)
    weights = weights.reshape(plan.pairs, 2, block, plan.sensors)
    weights_near = lax.dynamic_index_in_dim(weights, core, 1, keepdims=False)
    weights_far = to_core(lax.dynamic_index_in_dim(weights, 1 - core, 1, keepdims=False))
    weights = jnp.concatenate([weights_near, weights_far], axis=-1)
    weights = lax.dynamic_index_in_dim(weights, pair ^ half, 0, keepdims=False)
    damping_row = jnp.where(half == 0, damping, to_pair(damping))
    steps = [2 * d for d in range(1, plan.groups)]

    def reduce_field(keep, got):
        mine, *sends = split_call(plan, meta, keep, got)
        return [mine] + [to_src(piece, step) for piece, step in zip(sends, steps)]

    def gather_field(weighted):
        return place_call(plan, meta, [weighted] + [to_src(weighted, step) for step in steps])

    def to_half(array):
        return to_src(array, 1)

    pairs = [
        forward_call(plan, k, meta, near[k], far[k], True, (start, got_b[k])) for k in chunks
    ]
    got = in_turn([send for send, _ in pairs], to_half)
    pieces = [reduce_field(pairs[k][1], got[k]) for k in chunks]
    scaled, field, stats = zip(*[
        sensor_call(plan, k, meta, weights, pieces[k], norms_call(plan, k, damping, start))
        for k in chunks
    ])
    sums, steps_0 = total(sum(stats))
    norm_0, curve_0 = sums[0], sums[1]
    alpha_0 = (norm_0 / curve_0)[None]

    own = [gather_field(scaled[k]) for k in chunks]
    got = in_turn(own, to_half)
    back = []
    for k in chunks:
        wait = () if k == 0 else (steps_0[3],)
        back.append(adjoint_call(plan, meta, near[k], far[k], (own[k], got[k]), False, wait))
    got_back = in_turn(back, to_pair)

    pairs = [
        forward_call(
            plan, k, meta, near[k], far[k], False, (back[k], got_back[k]), (alpha_0,) if k > 0 else ()
        )
        for k in chunks
    ]
    got = in_turn([send for send, _ in pairs], to_half)
    image_0, residual, norms = zip(*[
        residual_call(plan, k, alpha_0, damping, start, back[k], got_back[k]) for k in chunks
    ])
    pieces = [reduce_field(pairs[k][1], got[k]) for k in chunks]
    scaled, stats = zip(*[
        sensor_call(plan, k, meta, weights, pieces[k], norms[k], alpha_0, damping_row, field[k])
        for k in chunks
    ])
    sums, steps_1 = total(sum(stats))
    norm_1 = sums[0]
    beta = norm_1 / norm_0
    curve_1 = sums[1] + 2.0 * beta * sums[2] + beta * beta * curve_0
    alpha_1 = norm_1 / curve_1

    own = [gather_field(scaled[k]) for k in chunks]
    got = in_turn(own, to_half)
    final = []
    for k in chunks:
        wait = () if k == 0 else (steps_1[3],)
        sent, mine = adjoint_call(plan, meta, near[k], far[k], (own[k], got[k]), True, wait)
        final.append(mine + to_pair(sent).astype(F32))
    residual, image_0 = jnp.concatenate(residual), jnp.concatenate(image_0)
    image_1 = jnp.concatenate(final) + damping[:, None, None] * residual + beta * image_0
    solution = alpha_0 * start + alpha_1 * (residual + beta * start)
    residual = residual - alpha_1 * image_1
    return solution.reshape(right_side.shape), residual.reshape(right_side.shape)


def solution(mesh):
    in_specs = (
        P(None, None, "sens", "src"),
        P("sens", None, None, "src"),
        P("src", "sens"),
        P("sens"),
    )
    out_specs = (P("sens", None, None, "src"), P("sens", None, None, "src"))
    shard = functools.partial(body, mesh.shape["sens"], mesh.shape["src"])
    return jax.shard_map(shard, mesh=mesh, in_specs=in_specs, out_specs=out_specs, check_vma=False)
```

```python
import functools

import jax
import jax.numpy as jnp
from jax import lax
from jax.experimental import pallas as pl
from jax.experimental.pallas import tpu as pltpu
from jax.sharding import PartitionSpec as P

CHUNKS = 2
KERNEL_BYTES = 16 * 2 ** 20
CUT_BYTES = 56 * 2 ** 20
F32 = jnp.float32
BF16 = jnp.bfloat16
ANYWHERE = pl.BlockSpec(memory_space=pl.ANY)
NT = (((1,), (1,)), ((), ()))
NN = (((1,), (0,)), ((), ()))


def largest_divisor(extent, most):
    return next(size for size in range(min(extent, most), 0, -1) if extent % size == 0)


def turned(block, sign):
    half = block.shape[0] // 2
    upper, lower = block[:half], block[half:]
    return jnp.concatenate([-lower, upper] if sign < 0 else [lower, -upper], axis=0)


def forward_rows(vector, near, far):
    left = jnp.concatenate([vector, turned(vector, -1)], axis=1)
    right = jnp.concatenate(
        [jnp.concatenate([part[0], part[1]], axis=1) for part in (near, far)], axis=0
    )
    return lax.dot_general(left, right, NT, preferred_element_type=F32)


def adjoint_rows(field, near, far):
    sensors = near[0].shape[0]
    total = None
    for part, piece in ((near, field[:, :sensors]), (far, field[:, sensors:])):
        left = jnp.concatenate([piece, turned(piece, 1)], axis=1)
        right = jnp.concatenate(part, axis=0)
        term = lax.dot_general(left, right, NN, preferred_element_type=F32)
        total = term if total is None else total + term
    return total


def cost(flops, moved):
    return pl.CostEstimate(flops=flops // 1000, bytes_accessed=moved // 1000, transcendentals=0)


class Plan:
    def __init__(self, operator, right_side, n_sens, n_src, chunks):
        self.freqs, _, self.sensors, self.sources = operator.shape
        self.block = right_side.shape[0]
        self.rows = right_side.shape[1] * right_side.shape[2]
        self.pairs = n_sens // 2
        self.groups = n_src // 2
        self.chunks = chunks
        self.part = self.block // chunks
        self.step = largest_divisor(self.part, 8)
        self.steps = self.part // self.step
        self.flops = 16 * self.part * self.rows * self.sensors * self.sources * 2
        self.piece = self.part * self.rows // self.groups


class Parts:
    def __init__(self, plan, m, blk_of, refs):
        (near, far), (near_buf, far_buf, sems) = refs
        self.buffers, self.copies = (near_buf, far_buf), {}
        for phase in range(2):
            for t in range(plan.steps):
                slot = phase * plan.steps + t
                self.copies[phase, t] = [
                    pltpu.make_async_copy(
                        ref.at[m[0] ^ blk_of(phase, m), pl.ds(t * plan.step, plan.step)],
                        buffer.at[slot],
                        sems.at[slot, place],
                    )
                    for place, (ref, buffer) in enumerate(((near, near_buf), (far, far_buf)))
                ]
        for copies in self.copies.values():
            for copy in copies:
                copy.start()

    def get(self, plan, phase, t):
        for copy in self.copies[phase, t]:
            copy.wait()
        slot = phase * plan.steps + t
        return [
            tuple(tuple(buffer[slot, f, c] for c in range(2)) for buffer in self.buffers)
            for f in range(plan.step)
        ]

    @staticmethod
    def scratch(plan):
        buffer = pltpu.VMEM((2 * plan.steps, plan.step, 2, plan.sensors, plan.sources), BF16)
        return [buffer, buffer, pltpu.SemaphoreType.DMA((2 * plan.steps, 2))]


def cut_call(plan, chunk, meta, whole, wait):
    block = (None, plan.step, 2, plan.sensors, plan.sources)
    base = chunk * plan.steps

    def kernel(m, one_ref, two_ref, *refs):
        far_ref, near_ref = refs[len(wait):]
        far_ref[...] = one_ref[...]
        near_ref[...] = two_ref[...]

    def source(core):
        return pl.BlockSpec(
            (None,) + block,
            lambda p, t, m: (p, core(m), base + t, 0, 0, 0),
            )

    out = jax.ShapeDtypeStruct((plan.pairs, plan.part, 2, plan.sensors, plan.sources), BF16)
    return pl.pallas_call(
        kernel,
        grid_spec=pltpu.PrefetchScalarGridSpec(
            num_scalar_prefetch=1,
            grid=(plan.pairs, plan.steps),
            in_specs=[source(lambda m: 1 - m[1]), source(lambda m: m[1])] + [ANYWHERE] * len(wait),
            out_specs=[pl.BlockSpec(block, lambda p, t, m: (p, t, 0, 0, 0))] * 2,
        ),
        out_shape=[out] * 2,
        cost_estimate=cost(0, 8 * plan.part * plan.sensors * plan.sources),
        compiler_params=pltpu.CompilerParams(vmem_limit_bytes=CUT_BYTES),
        name="cut",
    )(meta, whole, whole, *wait)


def cast_call(plan, chunk, start, wait=()):
    block = (plan.part, plan.rows, plan.sources)

    def kernel(start_ref, *refs):
        refs[-1][...] = start_ref[...].astype(BF16)

    return pl.pallas_call(
        kernel,
        grid=(1,),
        in_specs=[pl.BlockSpec(block, lambda i: (chunk, 0, 0))] + [ANYWHERE] * len(wait),
        out_specs=pl.BlockSpec(block, lambda i: (0, 0, 0)),
        out_shape=jax.ShapeDtypeStruct(block, BF16),
        cost_estimate=cost(0, 6 * plan.part * plan.rows * plan.sources),
        compiler_params=pltpu.CompilerParams(vmem_limit_bytes=KERNEL_BYTES),
        name="cast",
    )(start, *wait)


def forward_call(plan, chunk, meta, near, far, first, vectors, wait=()):
    blk_of = lambda p, m: 1 - (m[2] ^ p)

    def kernel(m, near, far, one_ref, two_ref, *refs):
        outs, scratch = refs[len(wait):len(wait) + 2], refs[len(wait) + 2:]
        parts = Parts(plan, m, blk_of, ((near, far), scratch))
        for phase in range(2):
            blk = blk_of(phase, m)
            for t in range(plan.steps):
                for i, (near_part, far_part) in enumerate(parts.get(plan, phase, t)):
                    f = t * plan.step + i
                    if first:
                        vector = jnp.where(blk == 0, one_ref[f].astype(BF16), two_ref[f])
                    else:
                        vector = one_ref[blk, f].astype(F32) + two_ref[1 - blk, f].astype(F32)
                    outs[phase][f] = forward_rows(vector.astype(BF16), near_part, far_part).astype(BF16)

    size = (plan.part, plan.rows, plan.sources)
    if first:
        vec_specs = [
            pl.BlockSpec(size, lambda i: (chunk, 0, 0)),
            pl.BlockSpec(size, lambda i: (0, 0, 0)),
        ]
    else:
        vec_specs = [pl.BlockSpec((2,) + size, lambda i: (0, 0, 0, 0))] * 2
    shape = (plan.part, plan.rows, 2 * plan.sensors)
    return pl.pallas_call(
        kernel,
        grid=(1,),
        in_specs=[pl.BlockSpec(memory_space=pltpu.SMEM)] + [ANYWHERE] * 2 + vec_specs
        + [ANYWHERE] * len(wait),
        out_specs=[pl.BlockSpec(shape, lambda i: (0, 0, 0))] * 2,
        out_shape=[jax.ShapeDtypeStruct(shape, BF16)] * 2,
        scratch_shapes=Parts.scratch(plan),
        cost_estimate=cost(plan.flops, 16 * plan.part * plan.sensors * plan.sources),
        compiler_params=pltpu.CompilerParams(vmem_limit_bytes=KERNEL_BYTES),
        name="forward",
    )(meta, near, far, *vectors, *wait)


def adjoint_call(plan, meta, near, far, halves, last, wait=()):
    blk_of = lambda p, m: 1 - p
    n_out = 2 if last else 1

    def kernel(m, near, far, own_ref, got_ref, *refs):
        outs, scratch = refs[len(wait):len(wait) + n_out], refs[len(wait) + n_out:]
        parts = Parts(plan, m, blk_of, ((near, far), scratch))
        for phase in range(2):
            blk = blk_of(phase, m)
            for t in range(plan.steps):
                for i, (near_part, far_part) in enumerate(parts.get(plan, phase, t)):
                    f = t * plan.step + i
                    field = jnp.where(blk == m[2], own_ref[f], got_ref[f])
                    back = adjoint_rows(field, near_part, far_part)
                    if last:
                        outs[phase][f] = back.astype(outs[phase].dtype)
                    else:
                        outs[0][blk, f] = back.astype(BF16)

    size = (plan.part, plan.rows, 2 * plan.sensors)
    shape = (plan.part, plan.rows, plan.sources)
    if last:
        out_specs = [pl.BlockSpec(shape, lambda i: (0, 0, 0))] * 2
        out_shape = [jax.ShapeDtypeStruct(shape, BF16), jax.ShapeDtypeStruct(shape, F32)]
    else:
        out_specs = pl.BlockSpec((2,) + shape, lambda i: (0, 0, 0, 0))
        out_shape = jax.ShapeDtypeStruct((2,) + shape, BF16)
    return pl.pallas_call(
        kernel,
        grid=(1,),
        in_specs=[pl.BlockSpec(memory_space=pltpu.SMEM)] + [ANYWHERE] * 2
        + [pl.BlockSpec(size, lambda i: (0, 0, 0))] * 2 + [ANYWHERE] * len(wait),
        out_specs=out_specs,
        out_shape=out_shape,
        scratch_shapes=Parts.scratch(plan),
        cost_estimate=cost(plan.flops, 16 * plan.part * plan.sensors * plan.sources),
        compiler_params=pltpu.CompilerParams(vmem_limit_bytes=KERNEL_BYTES),
        name="adjoint",
    )(meta, near, far, *halves, *wait)


def split_call(plan, meta, keep, got, wait=()):
    piece, groups = plan.piece, plan.groups
    width = keep.shape[-1]

    def kernel(m, keep_ref, got_ref, *refs):
        mine_ref, *sends = refs[len(wait):]
        for d in range(groups):
            place = pl.ds(pl.multiple_of((m[3] ^ d) * piece, piece), piece)
            total = keep_ref[place].astype(F32) + got_ref[place].astype(F32)
            if d == 0:
                mine_ref[...] = total
            else:
                sends[d - 1][...] = total.astype(BF16)

    whole = pl.BlockSpec(memory_space=pltpu.VMEM)
    return pl.pallas_call(
        kernel,
        in_specs=[pl.BlockSpec(memory_space=pltpu.SMEM), whole, whole] + [ANYWHERE] * len(wait),
        out_specs=[whole] * groups,
        out_shape=[jax.ShapeDtypeStruct((piece, width), F32)]
        + [jax.ShapeDtypeStruct((piece, width), BF16)] * (groups - 1),
        cost_estimate=cost(groups * piece * width, groups * piece * width * 8),
        compiler_params=pltpu.CompilerParams(vmem_limit_bytes=KERNEL_BYTES),
        name="split",
    )(meta, keep.reshape(-1, width), got.reshape(-1, width), *wait)


def place_call(plan, meta, pieces, wait=()):
    piece, groups = plan.piece, plan.groups
    width = pieces[0].shape[-1]

    def kernel(m, *refs):
        for d in range(groups):
            place = pl.ds(pl.multiple_of((m[3] ^ d) * piece, piece), piece)
            refs[-1][place] = refs[d][...]

    whole = pl.BlockSpec(memory_space=pltpu.VMEM)
    out = pl.pallas_call(
        kernel,
        in_specs=[pl.BlockSpec(memory_space=pltpu.SMEM)] + [whole] * groups
        + [ANYWHERE] * len(wait),
        out_specs=whole,
        out_shape=jax.ShapeDtypeStruct((groups * piece, width), BF16),
        cost_estimate=cost(0, groups * piece * width * 4),
        compiler_params=pltpu.CompilerParams(vmem_limit_bytes=KERNEL_BYTES),
        name="place",
    )(meta, *pieces, *wait)
    return out.reshape(plan.part, plan.rows, width)


def ordered(array, *earlier):
    def kernel(*refs):
        del refs

    return pl.pallas_call(
        kernel,
        in_specs=[ANYWHERE] * (1 + len(earlier)),
        out_specs=ANYWHERE,
        out_shape=jax.ShapeDtypeStruct(array.shape, array.dtype),
        input_output_aliases={0: 0},
        cost_estimate=cost(0, 0),
        compiler_params=pltpu.CompilerParams(vmem_limit_bytes=KERNEL_BYTES),
        name="ordered",
    )(array, *earlier)


def lanes(array):
    total = jnp.sum(array.reshape(-1, 8, array.shape[-1]), axis=0)
    return sum(total[:, i:i + 128] for i in range(0, array.shape[-1], 128))


def sensor_call(plan, chunk, meta, weights, pieces, norms, alpha=None, damping=None, old=None):
    piece, rows, groups = plan.piece, plan.rows, plan.groups
    width = pieces[0].shape[-1]
    count = max(1, piece // rows)
    high = piece // count
    second = old is not None

    def kernel(m, *refs):
        if second:
            alpha_ref, damp_ref, old_ref, *refs = refs
        weights_ref, norms_ref, *refs = refs
        ins, (out_ref, *more) = refs[:groups], refs[groups:]
        stats_ref = more[-1]
        square = cross = jnp.zeros((8, 128), F32)
        for c in range(count):
            at = pl.ds(c * high, high)
            freq = chunk * plan.part + (m[3] * piece + c * high) // rows
            field = ins[0][at]
            for ref in ins[1:]:
                field = field + ref[at].astype(F32)
            if second:
                factor = 1.0 - alpha_ref[0] * damp_ref[freq]
                field = factor * old_ref[at] - alpha_ref[0] * field
            scaled = weights_ref[pl.ds(freq, 1)] * field
            out_ref[at] = scaled.astype(BF16)
            square = square + lanes(scaled * field)
            if second:
                cross = cross + lanes(scaled * old_ref[at])
            else:
                more[0][at] = field
        stats_ref[0:8] = norms_ref[0:8]
        stats_ref[8:16] = norms_ref[8:16] + square
        stats_ref[16:24] = norms_ref[16:24] + cross

    whole = pl.BlockSpec(memory_space=pltpu.VMEM)
    scalars = pl.BlockSpec(memory_space=pltpu.SMEM)
    first_out = [] if second else [jax.ShapeDtypeStruct((piece, width), F32)]
    extra = (alpha, damping, old) if second else ()
    out_shape = [jax.ShapeDtypeStruct((piece, width), BF16)] + first_out
    out_shape = out_shape + [jax.ShapeDtypeStruct((24, 128), F32)]
    return pl.pallas_call(
        kernel,
        in_specs=[scalars] + ([scalars] * 2 + [whole] if second else []) + [whole] * (2 + groups),
        out_specs=[whole] * len(out_shape),
        out_shape=out_shape,
        cost_estimate=cost(8 * piece * width, 16 * piece * width),
        compiler_params=pltpu.CompilerParams(vmem_limit_bytes=KERNEL_BYTES),
        name="sensor",
    )(meta, *extra, weights, norms, *pieces)


def norms_call(plan, chunk, damping, start):
    block = (plan.part, plan.rows, plan.sources)

    def kernel(damp_ref, start_ref, stats_ref):
        plain = damped = jnp.zeros((8, 128), F32)
        for f in range(plan.part):
            term = lanes(start_ref[f] * start_ref[f])
            plain = plain + term
            damped = damped + damp_ref[chunk * plan.part + f] * term
        stats_ref[0:8] = plain
        stats_ref[8:16] = damped
        stats_ref[16:24] = jnp.zeros((8, 128), F32)

    return pl.pallas_call(
        kernel,
        grid=(1,),
        in_specs=[
            pl.BlockSpec(memory_space=pltpu.SMEM),
            pl.BlockSpec(block, lambda i: (chunk, 0, 0)),
        ],
        out_specs=pl.BlockSpec((24, 128), lambda i: (0, 0)),
        out_shape=jax.ShapeDtypeStruct((24, 128), F32),
        cost_estimate=cost(2 * start.size, 4 * start.size),
        compiler_params=pltpu.CompilerParams(vmem_limit_bytes=KERNEL_BYTES),
        name="norms",
    )(damping, start)


def residual_call(plan, chunk, alpha, damping, start, mine, got):
    part, rows, sources = plan.part, plan.rows, plan.sources

    def kernel(alpha_ref, damp_ref, start_ref, mine_ref, got_ref, image_ref, out_ref, stats_ref):
        plain = damped = mixed = jnp.zeros((8, 128), F32)
        for f in range(part):
            damp = damp_ref[chunk * part + f]
            begin = start_ref[f]
            image = mine_ref[f].astype(F32) + got_ref[f].astype(F32) + damp * begin
            residual = begin - alpha_ref[0] * image
            image_ref[f] = image
            out_ref[f] = residual
            term = lanes(residual * residual)
            plain = plain + term
            damped = damped + damp * term
            mixed = mixed + damp * lanes(residual * begin)
        stats_ref[0:8] = plain
        stats_ref[8:16] = damped
        stats_ref[16:24] = mixed

    block = (part, rows, sources)
    scalars = pl.BlockSpec(memory_space=pltpu.SMEM)
    out = jax.ShapeDtypeStruct(block, F32)
    return pl.pallas_call(
        kernel,
        grid=(1,),
        in_specs=[
            scalars,
            scalars,
            pl.BlockSpec(block, lambda i: (chunk, 0, 0)),
            pl.BlockSpec((None,) + block, lambda i: (0, 0, 0, 0)),
            pl.BlockSpec((None,) + block, lambda i: (1, 0, 0, 0)),
        ],
        out_specs=[
            pl.BlockSpec(block, lambda i: (0, 0, 0)),
            pl.BlockSpec(block, lambda i: (0, 0, 0)),
            pl.BlockSpec((24, 128), lambda i: (0, 0)),
        ],
        out_shape=[out, out, jax.ShapeDtypeStruct((24, 128), F32)],
        cost_estimate=cost(8 * part * rows * sources, 16 * part * rows * sources),
        compiler_params=pltpu.CompilerParams(vmem_limit_bytes=KERNEL_BYTES),
        name="residual",
    )(alpha, damping, start, mine, got)


def body(n_sens, n_src, operator, right_side, noise_weights, damping):
    plan = Plan(operator, right_side, n_sens, n_src, CHUNKS)
    sens, src = lax.axis_index("sens"), lax.axis_index("src")
    pair, core, half, group = sens // 2, sens % 2, src % 2, src // 2
    meta = jnp.stack([pair, core, half, group]).astype(jnp.int32)
    part, rows, block = plan.part, plan.rows, plan.block
    levels = range(n_src.bit_length() - 1)
    chunks = range(plan.chunks)

    def to_core(array):
        return lax.ppermute(array, "sens", [(i, i ^ 1) for i in range(n_sens)])

    def to_pair(array):
        return lax.ppermute(array, "sens", [(i, i ^ 2) for i in range(n_sens)])

    def to_src(array, step):
        return lax.ppermute(array, "src", [(j, j ^ step) for j in range(n_src)])

    def in_turn(arrays, move):
        moved = []
        for k, array in enumerate(arrays):
            if k > 0:
                array = arrays[k] = ordered(array, moved[-1])
            moved.append(move(array))
        return moved

    def total(sums):
        steps = [sums]
        steps.append(steps[-1] + to_core(steps[-1]))
        steps.append(steps[-1] + to_pair(steps[-1]))
        for level in levels:
            steps.append(steps[-1] + to_src(steps[-1], 1 << level))
        return jnp.sum(steps[-1].reshape(-1, 8 * 128), axis=1), steps

    def double(table, level):
        other = to_src(table, 1 << level)
        low = (src >> level) % 2 == 0
        return jnp.concatenate([jnp.where(low, table, other), jnp.where(low, other, table)], axis=0)

    whole = operator.reshape(plan.pairs, 2, block, 2, plan.sensors, plan.sources)
    start = right_side.reshape(block, rows, plan.sources)

    got_b, near, far, wait = [], [], [], ()
    for k in chunks:
        sent_b = cast_call(plan, k, start, wait)
        got_b.append(to_pair(sent_b))
        sent, mine = cut_call(plan, k, meta, whole, wait + (sent_b,))
        near.append(mine)
        far.append(to_core(sent))
        wait = (got_b[k],)
    weights = double(noise_weights, 0)

    for level in levels[1:]:
        weights = double(weights, level)
    weights = weights.reshape(plan.pairs, 2, block, plan.sensors)
    weights_near = lax.dynamic_index_in_dim(weights, core, 1, keepdims=False)
    weights_far = to_core(lax.dynamic_index_in_dim(weights, 1 - core, 1, keepdims=False))
    weights = jnp.concatenate([weights_near, weights_far], axis=-1)
    weights = lax.dynamic_index_in_dim(weights, pair ^ half, 0, keepdims=False)
    damping_row = jnp.where(half == 0, damping, to_pair(damping))
    steps = [2 * d for d in range(1, plan.groups)]

    def reduce_field(keep, got, wait=()):
        mine, *sends = split_call(plan, meta, keep, got, wait)
        return [mine] + [to_src(piece, step) for piece, step in zip(sends, steps)]

    def to_half(array):
        return to_src(array, 1)

    def both_products(scaled, scalar_steps, last, then):
        outs, wait = [], ()
        for k in chunks:
            pieces = [scaled[k]] + [to_src(scaled[k], step) for step in steps]
            own = place_call(plan, meta, pieces, wait)
            halves = (own, to_half(own))
            wait = () if k == 0 else (outs[k - 1][1][0], scalar_steps[-1])
            out = adjoint_call(plan, meta, near[k], far[k], halves, last, wait)
            outs.append((out, then(k, out)))
            wait = (out[0] if last else out, scalar_steps[3])
        return outs

    pairs = [
        forward_call(plan, k, meta, near[k], far[k], True, (start, got_b[k])) for k in chunks
    ]
    sends = [send for send, _ in pairs]
    got = in_turn(sends, to_half)
    pieces = [reduce_field(pairs[k][1], got[k], tuple(sends[k + 1:k + 2])) for k in chunks]
    scaled, field, stats = zip(*[
        sensor_call(plan, k, meta, weights, pieces[k], norms_call(plan, k, damping, start))
        for k in chunks
    ])
    sums, steps_0 = total(sum(stats))
    norm_0, curve_0 = sums[0], sums[1]
    alpha_0 = (norm_0 / curve_0)[None]

    def go_on(k, back):
        got = to_pair(back)
        send, keep = forward_call(plan, k, meta, near[k], far[k], False, (back, got))
        return send, keep, got

    outs = both_products(scaled, steps_0, False, go_on)
    back = [out for out, _ in outs]
    sends, keeps, got_back = zip(*[rest for _, rest in outs])
    got = in_turn(list(sends), to_half)
    image_0, residual, norms = zip(*[
        residual_call(plan, k, alpha_0, damping, start, back[k], got_back[k]) for k in chunks
    ])
    pieces = [reduce_field(keeps[k], got[k]) for k in chunks]
    scaled, stats = zip(*[
        sensor_call(plan, k, meta, weights, pieces[k], norms[k], alpha_0, damping_row, field[k])
        for k in chunks
    ])
    sums, steps_1 = total(sum(stats))
    norm_1 = sums[0]
    beta = norm_1 / norm_0
    curve_1 = sums[1] + 2.0 * beta * sums[2] + beta * beta * curve_0
    alpha_1 = norm_1 / curve_1

    outs = both_products(scaled, steps_1, True, lambda k, out: (to_pair(out[0]),))
    final = [out[1] + rest[0].astype(F32) for out, rest in outs]
    residual, image_0 = jnp.concatenate(residual), jnp.concatenate(image_0)
    image_1 = jnp.concatenate(final) + damping[:, None, None] * residual + beta * image_0
    solution = alpha_0 * start + alpha_1 * (residual + beta * start)
    residual = residual - alpha_1 * image_1
    return solution.reshape(right_side.shape), residual.reshape(right_side.shape)


def solution(mesh):
    in_specs = (
        P(None, None, "sens", "src"),
        P("sens", None, None, "src"),
        P("src", "sens"),
        P("sens"),
    )
    out_specs = (P("sens", None, None, "src"), P("sens", None, None, "src"))
    shard = functools.partial(body, mesh.shape["sens"], mesh.shape["src"])
    return jax.shard_map(shard, mesh=mesh, in_specs=in_specs, out_specs=out_specs, check_vma=False)
```

```python
import functools

import jax
import jax.numpy as jnp
from jax import lax
from jax.experimental import pallas as pl
from jax.experimental.pallas import tpu as pltpu
from jax.sharding import PartitionSpec as P

CHUNKS = 2
KERNEL_BYTES = 16 * 2 ** 20
PRODUCT_BYTES = 56 * 2 ** 20
F32 = jnp.float32
BF16 = jnp.bfloat16
ANYWHERE = pl.BlockSpec(memory_space=pl.ANY)
NT = (((1,), (1,)), ((), ()))
NN = (((1,), (0,)), ((), ()))


def largest_divisor(extent, most):
    return next(size for size in range(min(extent, most), 0, -1) if extent % size == 0)


def turned(block, sign):
    half = block.shape[0] // 2
    upper, lower = block[:half], block[half:]
    return jnp.concatenate([-lower, upper] if sign < 0 else [lower, -upper], axis=0)


def forward_rows(vector, near, far):
    left = jnp.concatenate([vector, turned(vector, -1)], axis=1)
    right = jnp.concatenate(
        [jnp.concatenate([part[0], part[1]], axis=1) for part in (near, far)], axis=0
    )
    return lax.dot_general(left, right, NT, preferred_element_type=F32)


def adjoint_rows(field, near, far):
    sensors = near[0].shape[0]
    total = None
    for part, piece in ((near, field[:, :sensors]), (far, field[:, sensors:])):
        left = jnp.concatenate([piece, turned(piece, 1)], axis=1)
        right = jnp.concatenate(part, axis=0)
        term = lax.dot_general(left, right, NN, preferred_element_type=F32)
        total = term if total is None else total + term
    return total


def cost(flops, moved):
    return pl.CostEstimate(flops=flops // 1000, bytes_accessed=moved // 1000, transcendentals=0)


class Plan:
    def __init__(self, operator, right_side, n_sens, n_src, chunks):
        self.freqs, _, self.sensors, self.sources = operator.shape
        self.block = right_side.shape[0]
        self.rows = right_side.shape[1] * right_side.shape[2]
        self.pairs = n_sens // 2
        self.groups = n_src // 2
        self.chunks = chunks
        self.part = self.block // chunks
        self.step = largest_divisor(self.part, 8)
        self.steps = self.part // self.step
        self.flops = 16 * self.part * self.rows * self.sensors * self.sources * 2
        self.piece = self.part * self.rows // self.groups


class Parts:
    def __init__(self, plan, chunk, m, blk_of, refs):
        (whole, far), (near_buf, far_buf, sems) = refs
        self.buffers, self.copies = (near_buf, far_buf), {}
        for phase in range(2):
            for t in range(plan.steps):
                slot = phase * plan.steps + t
                side = m[0] ^ blk_of(phase, m)
                rows = pl.ds(t * plan.step, plan.step)
                near_rows = pl.ds(chunk * plan.part + t * plan.step, plan.step)
                self.copies[phase, t] = [
                    pltpu.make_async_copy(ref, buffer.at[slot], sems.at[slot, place])
                    for place, (ref, buffer) in enumerate((
                        (whole.at[side, m[1], near_rows], near_buf),
                        (far.at[side, rows], far_buf),
                    ))
                ]
        for copies in self.copies.values():
            for copy in copies:
                copy.start()

    def get(self, plan, phase, t):
        for copy in self.copies[phase, t]:
            copy.wait()
        slot = phase * plan.steps + t
        return [
            tuple(tuple(buffer[slot, f, c] for c in range(2)) for buffer in self.buffers)
            for f in range(plan.step)
        ]

    @staticmethod
    def scratch(plan):
        buffer = pltpu.VMEM((2 * plan.steps, plan.step, 2, plan.sensors, plan.sources), BF16)
        return [buffer, buffer, pltpu.SemaphoreType.DMA((2 * plan.steps, 2))]


def cut_call(plan, chunk, meta, whole, wait=()):
    def kernel(m, whole_ref, *refs):
        out_ref, sems = refs[len(wait):]
        copies = []
        for side in range(plan.pairs):
            for t in range(plan.steps):
                rows = pl.ds(chunk * plan.part + t * plan.step, plan.step)
                copies.append(pltpu.make_async_copy(
                    whole_ref.at[side, 1 - m[1], rows],
                    out_ref.at[side, pl.ds(t * plan.step, plan.step)],
                    sems.at[side * plan.steps + t],
                ))
        for copy in copies:
            copy.start()
        for copy in copies:
            copy.wait()

    shape = (plan.pairs, plan.part, 2, plan.sensors, plan.sources)
    return pl.pallas_call(
        kernel,
        in_specs=[pl.BlockSpec(memory_space=pltpu.SMEM), ANYWHERE] + [ANYWHERE] * len(wait),
        out_specs=ANYWHERE,
        out_shape=jax.ShapeDtypeStruct(shape, BF16),
        scratch_shapes=[pltpu.SemaphoreType.DMA((plan.pairs * plan.steps,))],
        cost_estimate=cost(0, 8 * plan.part * plan.sensors * plan.sources),
        compiler_params=pltpu.CompilerParams(vmem_limit_bytes=PRODUCT_BYTES),
        name="cut",
    )(meta, whole, *wait)


def cast_call(plan, chunk, start, wait=()):
    shape = (plan.part, plan.rows, plan.sources)

    def kernel(start_ref, *refs):
        out_ref, buffer, sem = refs[len(wait):]
        rows = pl.ds(chunk * plan.part, plan.part)
        copy = pltpu.make_async_copy(start_ref.at[rows], buffer, sem)
        copy.start()
        copy.wait()
        out_ref[...] = buffer[...].astype(BF16)

    return pl.pallas_call(
        kernel,
        in_specs=[ANYWHERE] + [ANYWHERE] * len(wait),
        out_specs=pl.BlockSpec(memory_space=pltpu.VMEM),
        out_shape=jax.ShapeDtypeStruct(shape, BF16),
        scratch_shapes=[pltpu.VMEM(shape, F32), pltpu.SemaphoreType.DMA(())],
        cost_estimate=cost(0, 6 * plan.part * plan.rows * plan.sources),
        compiler_params=pltpu.CompilerParams(vmem_limit_bytes=KERNEL_BYTES),
        name="cast",
    )(start, *wait)


def forward_call(plan, chunk, meta, whole, far, first, vectors, wait=()):
    blk_of = lambda p, m: 1 - (m[2] ^ p)

    def kernel(m, whole, far, one_ref, two_ref, *refs):
        outs, scratch = refs[len(wait):len(wait) + 2], refs[len(wait) + 2:]
        parts = Parts(plan, chunk, m, blk_of, ((whole, far), scratch))
        for phase in range(2):
            blk = blk_of(phase, m)
            for t in range(plan.steps):
                for i, (near_part, far_part) in enumerate(parts.get(plan, phase, t)):
                    f = t * plan.step + i
                    if first:
                        vector = jnp.where(blk == 0, one_ref[f].astype(BF16), two_ref[f])
                    else:
                        vector = one_ref[blk, f].astype(F32) + two_ref[1 - blk, f].astype(F32)
                    outs[phase][f] = forward_rows(vector.astype(BF16), near_part, far_part).astype(BF16)

    size = (plan.part, plan.rows, plan.sources)
    if first:
        vec_specs = [
            pl.BlockSpec(size, lambda i: (chunk, 0, 0)),
            pl.BlockSpec(size, lambda i: (0, 0, 0)),
        ]
    else:
        vec_specs = [pl.BlockSpec((2,) + size, lambda i: (0, 0, 0, 0))] * 2
    shape = (plan.part, plan.rows, 2 * plan.sensors)
    return pl.pallas_call(
        kernel,
        grid=(1,),
        in_specs=[pl.BlockSpec(memory_space=pltpu.SMEM)] + [ANYWHERE] * 2 + vec_specs
        + [ANYWHERE] * len(wait),
        out_specs=[pl.BlockSpec(shape, lambda i: (0, 0, 0))] * 2,
        out_shape=[jax.ShapeDtypeStruct(shape, BF16)] * 2,
        scratch_shapes=Parts.scratch(plan),
        cost_estimate=cost(plan.flops, 16 * plan.part * plan.sensors * plan.sources),
        compiler_params=pltpu.CompilerParams(vmem_limit_bytes=PRODUCT_BYTES),
        name="forward",
    )(meta, whole, far, *vectors, *wait)


def adjoint_call(plan, chunk, meta, whole, far, halves, last, wait=()):
    blk_of = lambda p, m: 1 - p
    n_out = 2 if last else 1

    def kernel(m, whole, far, own_ref, got_ref, *refs):
        outs, scratch = refs[len(wait):len(wait) + n_out], refs[len(wait) + n_out:]
        parts = Parts(plan, chunk, m, blk_of, ((whole, far), scratch))
        for phase in range(2):
            blk = blk_of(phase, m)
            for t in range(plan.steps):
                for i, (near_part, far_part) in enumerate(parts.get(plan, phase, t)):
                    f = t * plan.step + i
                    field = jnp.where(blk == m[2], own_ref[f], got_ref[f])
                    back = adjoint_rows(field, near_part, far_part)
                    if last:
                        outs[phase][f] = back.astype(outs[phase].dtype)
                    else:
                        outs[0][blk, f] = back.astype(BF16)

    size = (plan.part, plan.rows, 2 * plan.sensors)
    shape = (plan.part, plan.rows, plan.sources)
    if last:
        out_specs = [pl.BlockSpec(shape, lambda i: (0, 0, 0))] * 2
        out_shape = [jax.ShapeDtypeStruct(shape, BF16), jax.ShapeDtypeStruct(shape, F32)]
    else:
        out_specs = pl.BlockSpec((2,) + shape, lambda i: (0, 0, 0, 0))
        out_shape = jax.ShapeDtypeStruct((2,) + shape, BF16)
    return pl.pallas_call(
        kernel,
        grid=(1,),
        in_specs=[pl.BlockSpec(memory_space=pltpu.SMEM)] + [ANYWHERE] * 2
        + [pl.BlockSpec(size, lambda i: (0, 0, 0))] * 2 + [ANYWHERE] * len(wait),
        out_specs=out_specs,
        out_shape=out_shape,
        scratch_shapes=Parts.scratch(plan),
        cost_estimate=cost(plan.flops, 16 * plan.part * plan.sensors * plan.sources),
        compiler_params=pltpu.CompilerParams(vmem_limit_bytes=PRODUCT_BYTES),
        name="adjoint",
    )(meta, whole, far, *halves, *wait)


def split_call(plan, meta, keep, got, wait=()):
    piece, groups = plan.piece, plan.groups
    width = keep.shape[-1]

    def kernel(m, keep_ref, got_ref, *refs):
        mine_ref, *sends = refs[len(wait):]
        for d in range(groups):
            place = pl.ds(pl.multiple_of((m[3] ^ d) * piece, piece), piece)
            total = keep_ref[place].astype(F32) + got_ref[place].astype(F32)
            if d == 0:
                mine_ref[...] = total
            else:
                sends[d - 1][...] = total.astype(BF16)

    whole = pl.BlockSpec(memory_space=pltpu.VMEM)
    return pl.pallas_call(
        kernel,
        in_specs=[pl.BlockSpec(memory_space=pltpu.SMEM), whole, whole] + [ANYWHERE] * len(wait),
        out_specs=[whole] * groups,
        out_shape=[jax.ShapeDtypeStruct((piece, width), F32)]
        + [jax.ShapeDtypeStruct((piece, width), BF16)] * (groups - 1),
        cost_estimate=cost(groups * piece * width, groups * piece * width * 8),
        compiler_params=pltpu.CompilerParams(vmem_limit_bytes=KERNEL_BYTES),
        name="split",
    )(meta, keep.reshape(-1, width), got.reshape(-1, width), *wait)


def place_call(plan, meta, pieces, wait=()):
    piece, groups = plan.piece, plan.groups
    width = pieces[0].shape[-1]

    def kernel(m, *refs):
        for d in range(groups):
            place = pl.ds(pl.multiple_of((m[3] ^ d) * piece, piece), piece)
            refs[-1][place] = refs[d][...]

    whole = pl.BlockSpec(memory_space=pltpu.VMEM)
    out = pl.pallas_call(
        kernel,
        in_specs=[pl.BlockSpec(memory_space=pltpu.SMEM)] + [whole] * groups
        + [ANYWHERE] * len(wait),
        out_specs=whole,
        out_shape=jax.ShapeDtypeStruct((groups * piece, width), BF16),
        cost_estimate=cost(0, groups * piece * width * 4),
        compiler_params=pltpu.CompilerParams(vmem_limit_bytes=KERNEL_BYTES),
        name="place",
    )(meta, *pieces, *wait)
    return out.reshape(plan.part, plan.rows, width)


def ordered(array, *earlier):
    def kernel(*refs):
        del refs

    return pl.pallas_call(
        kernel,
        in_specs=[ANYWHERE] * (1 + len(earlier)),
        out_specs=ANYWHERE,
        out_shape=jax.ShapeDtypeStruct(array.shape, array.dtype),
        input_output_aliases={0: 0},
        cost_estimate=cost(0, 0),
        compiler_params=pltpu.CompilerParams(vmem_limit_bytes=KERNEL_BYTES),
        name="ordered",
    )(array, *earlier)


def lanes(array):
    total = jnp.sum(array.reshape(-1, 8, array.shape[-1]), axis=0)
    return sum(total[:, i:i + 128] for i in range(0, array.shape[-1], 128))


def sensor_call(plan, chunk, meta, weights, pieces, norms, alpha=None, damping=None, old=None):
    piece, rows, groups = plan.piece, plan.rows, plan.groups
    width = pieces[0].shape[-1]
    count = max(1, piece // rows)
    high = piece // count
    second = old is not None

    def kernel(m, *refs):
        if second:
            alpha_ref, damp_ref, old_ref, *refs = refs
        weights_ref, norms_ref, *refs = refs
        ins, (out_ref, *more) = refs[:groups], refs[groups:]
        stats_ref = more[-1]
        square = cross = jnp.zeros((8, 128), F32)
        for c in range(count):
            at = pl.ds(c * high, high)
            freq = chunk * plan.part + (m[3] * piece + c * high) // rows
            field = ins[0][at]
            for ref in ins[1:]:
                field = field + ref[at].astype(F32)
            if second:
                factor = 1.0 - alpha_ref[0] * damp_ref[freq]
                field = factor * old_ref[at] - alpha_ref[0] * field
            scaled = weights_ref[pl.ds(freq, 1)] * field
            out_ref[at] = scaled.astype(BF16)
            square = square + lanes(scaled * field)
            if second:
                cross = cross + lanes(scaled * old_ref[at])
            else:
                more[0][at] = field
        stats_ref[0:8] = norms_ref[0:8]
        stats_ref[8:16] = norms_ref[8:16] + square
        stats_ref[16:24] = norms_ref[16:24] + cross

    whole = pl.BlockSpec(memory_space=pltpu.VMEM)
    scalars = pl.BlockSpec(memory_space=pltpu.SMEM)
    first_out = [] if second else [jax.ShapeDtypeStruct((piece, width), F32)]
    extra = (alpha, damping, old) if second else ()
    out_shape = [jax.ShapeDtypeStruct((piece, width), BF16)] + first_out
    out_shape = out_shape + [jax.ShapeDtypeStruct((24, 128), F32)]
    return pl.pallas_call(
        kernel,
        in_specs=[scalars] + ([scalars] * 2 + [whole] if second else []) + [whole] * (2 + groups),
        out_specs=[whole] * len(out_shape),
        out_shape=out_shape,
        cost_estimate=cost(8 * piece * width, 16 * piece * width),
        compiler_params=pltpu.CompilerParams(vmem_limit_bytes=KERNEL_BYTES),
        name="sensor",
    )(meta, *extra, weights, norms, *pieces)


def norms_call(plan, chunk, damping, start):
    block = (plan.part, plan.rows, plan.sources)

    def kernel(damp_ref, start_ref, stats_ref):
        plain = damped = jnp.zeros((8, 128), F32)
        for f in range(plan.part):
            term = lanes(start_ref[f] * start_ref[f])
            plain = plain + term
            damped = damped + damp_ref[chunk * plan.part + f] * term
        stats_ref[0:8] = plain
        stats_ref[8:16] = damped
        stats_ref[16:24] = jnp.zeros((8, 128), F32)

    return pl.pallas_call(
        kernel,
        grid=(1,),
        in_specs=[
            pl.BlockSpec(memory_space=pltpu.SMEM),
            pl.BlockSpec(block, lambda i: (chunk, 0, 0)),
        ],
        out_specs=pl.BlockSpec((24, 128), lambda i: (0, 0)),
        out_shape=jax.ShapeDtypeStruct((24, 128), F32),
        cost_estimate=cost(2 * start.size, 4 * start.size),
        compiler_params=pltpu.CompilerParams(vmem_limit_bytes=KERNEL_BYTES),
        name="norms",
    )(damping, start)


def residual_call(plan, chunk, alpha, damping, start, mine, got):
    part, rows, sources = plan.part, plan.rows, plan.sources

    def kernel(alpha_ref, damp_ref, start_ref, mine_ref, got_ref, image_ref, out_ref, stats_ref):
        plain = damped = mixed = jnp.zeros((8, 128), F32)
        for f in range(part):
            damp = damp_ref[chunk * part + f]
            begin = start_ref[f]
            image = mine_ref[f].astype(F32) + got_ref[f].astype(F32) + damp * begin
            residual = begin - alpha_ref[0] * image
            image_ref[f] = image
            out_ref[f] = residual
            term = lanes(residual * residual)
            plain = plain + term
            damped = damped + damp * term
            mixed = mixed + damp * lanes(residual * begin)
        stats_ref[0:8] = plain
        stats_ref[8:16] = damped
        stats_ref[16:24] = mixed

    block = (part, rows, sources)
    scalars = pl.BlockSpec(memory_space=pltpu.SMEM)
    out = jax.ShapeDtypeStruct(block, F32)
    return pl.pallas_call(
        kernel,
        grid=(1,),
        in_specs=[
            scalars,
            scalars,
            pl.BlockSpec(block, lambda i: (chunk, 0, 0)),
            pl.BlockSpec((None,) + block, lambda i: (0, 0, 0, 0)),
            pl.BlockSpec((None,) + block, lambda i: (1, 0, 0, 0)),
        ],
        out_specs=[
            pl.BlockSpec(block, lambda i: (0, 0, 0)),
            pl.BlockSpec(block, lambda i: (0, 0, 0)),
            pl.BlockSpec((24, 128), lambda i: (0, 0)),
        ],
        out_shape=[out, out, jax.ShapeDtypeStruct((24, 128), F32)],
        cost_estimate=cost(8 * part * rows * sources, 16 * part * rows * sources),
        compiler_params=pltpu.CompilerParams(vmem_limit_bytes=KERNEL_BYTES),
        name="residual",
    )(alpha, damping, start, mine, got)


def body(n_sens, n_src, operator, right_side, noise_weights, damping):
    plan = Plan(operator, right_side, n_sens, n_src, CHUNKS)
    sens, src = lax.axis_index("sens"), lax.axis_index("src")
    pair, core, half, group = sens // 2, sens % 2, src % 2, src // 2
    meta = jnp.stack([pair, core, half, group]).astype(jnp.int32)
    part, rows, block = plan.part, plan.rows, plan.block
    levels = range(n_src.bit_length() - 1)
    chunks = range(plan.chunks)

    def to_core(array):
        return lax.ppermute(array, "sens", [(i, i ^ 1) for i in range(n_sens)])

    def to_pair(array):
        return lax.ppermute(array, "sens", [(i, i ^ 2) for i in range(n_sens)])

    def to_src(array, step):
        return lax.ppermute(array, "src", [(j, j ^ step) for j in range(n_src)])

    def in_turn(arrays, move):
        moved = []
        for k, array in enumerate(arrays):
            if k > 0:
                array = arrays[k] = ordered(array, moved[-1])
            moved.append(move(array))
        return moved

    def total(sums):
        steps = [sums]
        steps.append(steps[-1] + to_core(steps[-1]))
        steps.append(steps[-1] + to_pair(steps[-1]))
        for level in levels:
            steps.append(steps[-1] + to_src(steps[-1], 1 << level))
        return jnp.sum(steps[-1].reshape(-1, 8 * 128), axis=1), steps

    def double(table, level):
        other = to_src(table, 1 << level)
        low = (src >> level) % 2 == 0
        return jnp.concatenate([jnp.where(low, table, other), jnp.where(low, other, table)], axis=0)

    whole = operator.reshape(plan.pairs, 2, block, 2, plan.sensors, plan.sources)
    start = right_side.reshape(block, rows, plan.sources)

    far, pairs, wait = [], [], ()
    for k in chunks:
        got_b = to_pair(cast_call(plan, k, start, wait))
        far.append(to_core(cut_call(plan, k, meta, whole, wait)))
        pairs.append(forward_call(plan, k, meta, whole, far[k], True, (start, got_b)))
        wait = (pairs[k][0],)
    weights = double(ordered(noise_weights, pairs[0][0]), 0)

    for level in levels[1:]:
        weights = double(weights, level)
    weights = weights.reshape(plan.pairs, 2, block, plan.sensors)
    weights_near = lax.dynamic_index_in_dim(weights, core, 1, keepdims=False)
    weights_far = to_core(lax.dynamic_index_in_dim(weights, 1 - core, 1, keepdims=False))
    weights = jnp.concatenate([weights_near, weights_far], axis=-1)
    weights = lax.dynamic_index_in_dim(weights, pair ^ half, 0, keepdims=False)
    damping_row = jnp.where(half == 0, damping, to_pair(damping))
    steps = [2 * d for d in range(1, plan.groups)]

    def reduce_field(keep, got, wait=()):
        mine, *sends = split_call(plan, meta, keep, got, wait)
        return [mine] + [to_src(piece, step) for piece, step in zip(sends, steps)]

    def to_half(array):
        return to_src(array, 1)

    def both_products(scaled, scalar_steps, last, then):
        outs, wait = [], ()
        for k in chunks:
            pieces = [scaled[k]] + [to_src(scaled[k], step) for step in steps]
            own = place_call(plan, meta, pieces, wait)
            halves = (own, to_half(own))
            wait = () if k == 0 else (outs[k - 1][1][0], scalar_steps[-1])
            out = adjoint_call(plan, k, meta, whole, far[k], halves, last, wait)
            outs.append((out, then(k, out)))
            wait = (out[0] if last else out, scalar_steps[3])
        return outs

    sends = [send for send, _ in pairs]
    got = in_turn(sends, to_half)
    pieces = [reduce_field(pairs[k][1], got[k], tuple(sends[k + 1:k + 2])) for k in chunks]
    scaled, field, stats = zip(*[
        sensor_call(plan, k, meta, weights, pieces[k], norms_call(plan, k, damping, start))
        for k in chunks
    ])
    sums, steps_0 = total(sum(stats))
    norm_0, curve_0 = sums[0], sums[1]
    alpha_0 = (norm_0 / curve_0)[None]

    def go_on(k, back):
        got = to_pair(back)
        send, keep = forward_call(plan, k, meta, whole, far[k], False, (back, got))
        return send, keep, got

    outs = both_products(scaled, steps_0, False, go_on)
    back = [out for out, _ in outs]
    sends, keeps, got_back = zip(*[rest for _, rest in outs])
    got = in_turn(list(sends), to_half)
    image_0, residual, norms = zip(*[
        residual_call(plan, k, alpha_0, damping, start, back[k], got_back[k]) for k in chunks
    ])
    pieces = [reduce_field(keeps[k], got[k]) for k in chunks]
    scaled, stats = zip(*[
        sensor_call(plan, k, meta, weights, pieces[k], norms[k], alpha_0, damping_row, field[k])
        for k in chunks
    ])
    sums, steps_1 = total(sum(stats))
    norm_1 = sums[0]
    beta = norm_1 / norm_0
    curve_1 = sums[1] + 2.0 * beta * sums[2] + beta * beta * curve_0
    alpha_1 = norm_1 / curve_1

    outs = both_products(scaled, steps_1, True, lambda k, out: (to_pair(out[0]),))
    final = [out[1] + rest[0].astype(F32) for out, rest in outs]
    residual, image_0 = jnp.concatenate(residual), jnp.concatenate(image_0)
    image_1 = jnp.concatenate(final) + damping[:, None, None] * residual + beta * image_0
    solution = alpha_0 * start + alpha_1 * (residual + beta * start)
    residual = residual - alpha_1 * image_1
    return solution.reshape(right_side.shape), residual.reshape(right_side.shape)


def solution(mesh):
    in_specs = (
        P(None, None, "sens", "src"),
        P("sens", None, None, "src"),
        P("src", "sens"),
        P("sens"),
    )
    out_specs = (P("sens", None, None, "src"), P("sens", None, None, "src"))
    shard = functools.partial(body, mesh.shape["sens"], mesh.shape["src"])
    return jax.shard_map(shard, mesh=mesh, in_specs=in_specs, out_specs=out_specs, check_vma=False)
```

```python
import functools

import jax
import jax.numpy as jnp
from jax import lax
from jax.experimental import pallas as pl
from jax.experimental.pallas import tpu as pltpu
from jax.sharding import PartitionSpec as P

CHUNKS = 2
KERNEL_BYTES = 16 * 2 ** 20
PRODUCT_BYTES = 56 * 2 ** 20
F32 = jnp.float32
BF16 = jnp.bfloat16
ANYWHERE = pl.BlockSpec(memory_space=pl.ANY)
NT = (((1,), (1,)), ((), ()))
NN = (((1,), (0,)), ((), ()))


def largest_divisor(extent, most):
    return next(size for size in range(min(extent, most), 0, -1) if extent % size == 0)


def turned(block, sign):
    half = block.shape[0] // 2
    upper, lower = block[:half], block[half:]
    return jnp.concatenate([-lower, upper] if sign < 0 else [lower, -upper], axis=0)


def forward_rows(vector, near, far):
    left = jnp.concatenate([vector, turned(vector, -1)], axis=1)
    right = jnp.concatenate(
        [jnp.concatenate([part[0], part[1]], axis=1) for part in (near, far)], axis=0
    )
    return lax.dot_general(left, right, NT, preferred_element_type=F32)


def adjoint_rows(field, near, far):
    sensors = near[0].shape[0]
    total = None
    for part, piece in ((near, field[:, :sensors]), (far, field[:, sensors:])):
        left = jnp.concatenate([piece, turned(piece, 1)], axis=1)
        right = jnp.concatenate(part, axis=0)
        term = lax.dot_general(left, right, NN, preferred_element_type=F32)
        total = term if total is None else total + term
    return total


def cost(flops, moved):
    return pl.CostEstimate(flops=flops // 1000, bytes_accessed=moved // 1000, transcendentals=0)


class Plan:
    def __init__(self, operator, right_side, n_sens, n_src, chunks):
        self.freqs, _, self.sensors, self.sources = operator.shape
        self.block = right_side.shape[0]
        self.rows = right_side.shape[1] * right_side.shape[2]
        self.pairs = n_sens // 2
        self.groups = n_src // 2
        self.chunks = chunks
        self.part = self.block // chunks
        self.step = largest_divisor(self.part, 8)
        self.steps = self.part // self.step
        self.flops = 16 * self.part * self.rows * self.sensors * self.sources * 2
        self.piece = self.part * self.rows // self.groups


class Parts:
    def __init__(self, plan, chunk, m, blk_of, refs):
        (whole, far), (near_buf, far_buf, sems) = refs
        self.buffers, self.copies = (near_buf, far_buf), {}
        for phase in range(2):
            for t in range(plan.steps):
                slot = phase * plan.steps + t
                side = m[0] ^ blk_of(phase, m)
                rows = pl.ds(t * plan.step, plan.step)
                near_rows = pl.ds(chunk * plan.part + t * plan.step, plan.step)
                self.copies[phase, t] = [
                    pltpu.make_async_copy(ref, buffer.at[slot], sems.at[slot, place])
                    for place, (ref, buffer) in enumerate((
                        (whole.at[side, m[1], near_rows], near_buf),
                        (far.at[side, rows], far_buf),
                    ))
                ]
        for copies in self.copies.values():
            for copy in copies:
                copy.start()

    def get(self, plan, phase, t):
        for copy in self.copies[phase, t]:
            copy.wait()
        slot = phase * plan.steps + t
        return [
            tuple(tuple(buffer[slot, f, c] for c in range(2)) for buffer in self.buffers)
            for f in range(plan.step)
        ]

    @staticmethod
    def scratch(plan):
        buffer = pltpu.VMEM((2 * plan.steps, plan.step, 2, plan.sensors, plan.sources), BF16)
        return [buffer, buffer, pltpu.SemaphoreType.DMA((2 * plan.steps, 2))]


def cut_call(plan, chunk, meta, whole, wait=()):
    def kernel(m, whole_ref, *refs):
        out_ref, buffer, sems = refs[len(wait):]
        slots = [(side, t) for side in range(plan.pairs) for t in range(plan.steps)]
        ins, outs = [], []
        for slot, (side, t) in enumerate(slots):
            rows = pl.ds(chunk * plan.part + t * plan.step, plan.step)
            ins.append(pltpu.make_async_copy(
                whole_ref.at[side, 1 - m[1], rows], buffer.at[slot], sems.at[0, slot]
            ))
            outs.append(pltpu.make_async_copy(
                buffer.at[slot], out_ref.at[side, pl.ds(t * plan.step, plan.step)], sems.at[1, slot]
            ))
        for copy in ins:
            copy.start()
        for slot in range(len(slots)):
            ins[slot].wait()
            outs[slot].start()
        for copy in outs:
            copy.wait()

    shape = (plan.pairs, plan.part, 2, plan.sensors, plan.sources)
    return pl.pallas_call(
        kernel,
        in_specs=[pl.BlockSpec(memory_space=pltpu.SMEM), ANYWHERE] + [ANYWHERE] * len(wait),
        out_specs=ANYWHERE,
        out_shape=jax.ShapeDtypeStruct(shape, BF16),
        scratch_shapes=[
            pltpu.VMEM((plan.pairs * plan.steps, plan.step) + shape[2:], BF16),
            pltpu.SemaphoreType.DMA((2, plan.pairs * plan.steps)),
        ],
        cost_estimate=cost(0, 8 * plan.part * plan.sensors * plan.sources),
        compiler_params=pltpu.CompilerParams(vmem_limit_bytes=PRODUCT_BYTES),
        name="cut",
    )(meta, whole, *wait)


def cast_call(plan, chunk, start, wait=()):
    shape = (plan.part, plan.rows, plan.sources)

    def kernel(start_ref, *refs):
        out_ref, buffer, sem = refs[len(wait):]
        rows = pl.ds(chunk * plan.part, plan.part)
        copy = pltpu.make_async_copy(start_ref.at[rows], buffer, sem)
        copy.start()
        copy.wait()
        out_ref[...] = buffer[...].astype(BF16)

    return pl.pallas_call(
        kernel,
        in_specs=[ANYWHERE] + [ANYWHERE] * len(wait),
        out_specs=pl.BlockSpec(memory_space=pltpu.VMEM),
        out_shape=jax.ShapeDtypeStruct(shape, BF16),
        scratch_shapes=[pltpu.VMEM(shape, F32), pltpu.SemaphoreType.DMA(())],
        cost_estimate=cost(0, 6 * plan.part * plan.rows * plan.sources),
        compiler_params=pltpu.CompilerParams(vmem_limit_bytes=KERNEL_BYTES),
        name="cast",
    )(start, *wait)


def forward_call(plan, chunk, meta, whole, far, first, vectors, wait=()):
    blk_of = lambda p, m: 1 - (m[2] ^ p)

    def kernel(m, whole, far, one_ref, two_ref, *refs):
        outs, scratch = refs[len(wait):len(wait) + 2], refs[len(wait) + 2:]
        parts = Parts(plan, chunk, m, blk_of, ((whole, far), scratch))
        for phase in range(2):
            blk = blk_of(phase, m)
            for t in range(plan.steps):
                for i, (near_part, far_part) in enumerate(parts.get(plan, phase, t)):
                    f = t * plan.step + i
                    if first:
                        vector = jnp.where(blk == 0, one_ref[f].astype(BF16), two_ref[f])
                    else:
                        vector = one_ref[blk, f].astype(F32) + two_ref[1 - blk, f].astype(F32)
                    outs[phase][f] = forward_rows(vector.astype(BF16), near_part, far_part).astype(BF16)

    size = (plan.part, plan.rows, plan.sources)
    if first:
        vec_specs = [
            pl.BlockSpec(size, lambda i: (chunk, 0, 0)),
            pl.BlockSpec(size, lambda i: (0, 0, 0)),
        ]
    else:
        vec_specs = [pl.BlockSpec((2,) + size, lambda i: (0, 0, 0, 0))] * 2
    shape = (plan.part, plan.rows, 2 * plan.sensors)
    return pl.pallas_call(
        kernel,
        grid=(1,),
        in_specs=[pl.BlockSpec(memory_space=pltpu.SMEM)] + [ANYWHERE] * 2 + vec_specs
        + [ANYWHERE] * len(wait),
        out_specs=[pl.BlockSpec(shape, lambda i: (0, 0, 0))] * 2,
        out_shape=[jax.ShapeDtypeStruct(shape, BF16)] * 2,
        scratch_shapes=Parts.scratch(plan),
        cost_estimate=cost(plan.flops, 16 * plan.part * plan.sensors * plan.sources),
        compiler_params=pltpu.CompilerParams(vmem_limit_bytes=PRODUCT_BYTES),
        name="forward",
    )(meta, whole, far, *vectors, *wait)


def adjoint_call(plan, chunk, meta, whole, far, halves, last, wait=()):
    blk_of = lambda p, m: 1 - p
    n_out = 2 if last else 1

    def kernel(m, whole, far, own_ref, got_ref, *refs):
        outs, scratch = refs[len(wait):len(wait) + n_out], refs[len(wait) + n_out:]
        parts = Parts(plan, chunk, m, blk_of, ((whole, far), scratch))
        for phase in range(2):
            blk = blk_of(phase, m)
            for t in range(plan.steps):
                for i, (near_part, far_part) in enumerate(parts.get(plan, phase, t)):
                    f = t * plan.step + i
                    field = jnp.where(blk == m[2], own_ref[f], got_ref[f])
                    back = adjoint_rows(field, near_part, far_part)
                    if last:
                        outs[phase][f] = back.astype(outs[phase].dtype)
                    else:
                        outs[0][blk, f] = back.astype(BF16)

    size = (plan.part, plan.rows, 2 * plan.sensors)
    shape = (plan.part, plan.rows, plan.sources)
    if last:
        out_specs = [pl.BlockSpec(shape, lambda i: (0, 0, 0))] * 2
        out_shape = [jax.ShapeDtypeStruct(shape, BF16), jax.ShapeDtypeStruct(shape, F32)]
    else:
        out_specs = pl.BlockSpec((2,) + shape, lambda i: (0, 0, 0, 0))
        out_shape = jax.ShapeDtypeStruct((2,) + shape, BF16)
    return pl.pallas_call(
        kernel,
        grid=(1,),
        in_specs=[pl.BlockSpec(memory_space=pltpu.SMEM)] + [ANYWHERE] * 2
        + [pl.BlockSpec(size, lambda i: (0, 0, 0))] * 2 + [ANYWHERE] * len(wait),
        out_specs=out_specs,
        out_shape=out_shape,
        scratch_shapes=Parts.scratch(plan),
        cost_estimate=cost(plan.flops, 16 * plan.part * plan.sensors * plan.sources),
        compiler_params=pltpu.CompilerParams(vmem_limit_bytes=PRODUCT_BYTES),
        name="adjoint",
    )(meta, whole, far, *halves, *wait)


def split_call(plan, meta, keep, got, wait=()):
    piece, groups = plan.piece, plan.groups
    width = keep.shape[-1]

    def kernel(m, keep_ref, got_ref, *refs):
        mine_ref, *sends = refs[len(wait):]
        for d in range(groups):
            place = pl.ds(pl.multiple_of((m[3] ^ d) * piece, piece), piece)
            total = keep_ref[place].astype(F32) + got_ref[place].astype(F32)
            if d == 0:
                mine_ref[...] = total
            else:
                sends[d - 1][...] = total.astype(BF16)

    whole = pl.BlockSpec(memory_space=pltpu.VMEM)
    return pl.pallas_call(
        kernel,
        in_specs=[pl.BlockSpec(memory_space=pltpu.SMEM), whole, whole] + [ANYWHERE] * len(wait),
        out_specs=[whole] * groups,
        out_shape=[jax.ShapeDtypeStruct((piece, width), F32)]
        + [jax.ShapeDtypeStruct((piece, width), BF16)] * (groups - 1),
        cost_estimate=cost(groups * piece * width, groups * piece * width * 8),
        compiler_params=pltpu.CompilerParams(vmem_limit_bytes=KERNEL_BYTES),
        name="split",
    )(meta, keep.reshape(-1, width), got.reshape(-1, width), *wait)


def place_call(plan, meta, pieces, wait=()):
    piece, groups = plan.piece, plan.groups
    width = pieces[0].shape[-1]

    def kernel(m, *refs):
        for d in range(groups):
            place = pl.ds(pl.multiple_of((m[3] ^ d) * piece, piece), piece)
            refs[-1][place] = refs[d][...]

    whole = pl.BlockSpec(memory_space=pltpu.VMEM)
    out = pl.pallas_call(
        kernel,
        in_specs=[pl.BlockSpec(memory_space=pltpu.SMEM)] + [whole] * groups
        + [ANYWHERE] * len(wait),
        out_specs=whole,
        out_shape=jax.ShapeDtypeStruct((groups * piece, width), BF16),
        cost_estimate=cost(0, groups * piece * width * 4),
        compiler_params=pltpu.CompilerParams(vmem_limit_bytes=KERNEL_BYTES),
        name="place",
    )(meta, *pieces, *wait)
    return out.reshape(plan.part, plan.rows, width)


def ordered(array, *earlier):
    def kernel(*refs):
        del refs

    return pl.pallas_call(
        kernel,
        in_specs=[ANYWHERE] * (1 + len(earlier)),
        out_specs=ANYWHERE,
        out_shape=jax.ShapeDtypeStruct(array.shape, array.dtype),
        input_output_aliases={0: 0},
        cost_estimate=cost(0, 0),
        compiler_params=pltpu.CompilerParams(vmem_limit_bytes=KERNEL_BYTES),
        name="ordered",
    )(array, *earlier)


def lanes(array):
    total = jnp.sum(array.reshape(-1, 8, array.shape[-1]), axis=0)
    return sum(total[:, i:i + 128] for i in range(0, array.shape[-1], 128))


def sensor_call(plan, chunk, meta, weights, pieces, norms, alpha=None, damping=None, old=None):
    piece, rows, groups = plan.piece, plan.rows, plan.groups
    width = pieces[0].shape[-1]
    count = max(1, piece // rows)
    high = piece // count
    second = old is not None

    def kernel(m, *refs):
        if second:
            alpha_ref, damp_ref, old_ref, *refs = refs
        weights_ref, norms_ref, *refs = refs
        ins, (out_ref, *more) = refs[:groups], refs[groups:]
        stats_ref = more[-1]
        square = cross = jnp.zeros((8, 128), F32)
        for c in range(count):
            at = pl.ds(c * high, high)
            freq = chunk * plan.part + (m[3] * piece + c * high) // rows
            field = ins[0][at]
            for ref in ins[1:]:
                field = field + ref[at].astype(F32)
            if second:
                factor = 1.0 - alpha_ref[0] * damp_ref[freq]
                field = factor * old_ref[at] - alpha_ref[0] * field
            scaled = weights_ref[pl.ds(freq, 1)] * field
            out_ref[at] = scaled.astype(BF16)
            square = square + lanes(scaled * field)
            if second:
                cross = cross + lanes(scaled * old_ref[at])
            else:
                more[0][at] = field
        stats_ref[0:8] = norms_ref[0:8]
        stats_ref[8:16] = norms_ref[8:16] + square
        stats_ref[16:24] = norms_ref[16:24] + cross

    whole = pl.BlockSpec(memory_space=pltpu.VMEM)
    scalars = pl.BlockSpec(memory_space=pltpu.SMEM)
    first_out = [] if second else [jax.ShapeDtypeStruct((piece, width), F32)]
    extra = (alpha, damping, old) if second else ()
    out_shape = [jax.ShapeDtypeStruct((piece, width), BF16)] + first_out
    out_shape = out_shape + [jax.ShapeDtypeStruct((24, 128), F32)]
    return pl.pallas_call(
        kernel,
        in_specs=[scalars] + ([scalars] * 2 + [whole] if second else []) + [whole] * (2 + groups),
        out_specs=[whole] * len(out_shape),
        out_shape=out_shape,
        cost_estimate=cost(8 * piece * width, 16 * piece * width),
        compiler_params=pltpu.CompilerParams(vmem_limit_bytes=KERNEL_BYTES),
        name="sensor",
    )(meta, *extra, weights, norms, *pieces)


def norms_call(plan, chunk, damping, start):
    block = (plan.part, plan.rows, plan.sources)

    def kernel(damp_ref, start_ref, stats_ref):
        plain = damped = jnp.zeros((8, 128), F32)
        for f in range(plan.part):
            term = lanes(start_ref[f] * start_ref[f])
            plain = plain + term
            damped = damped + damp_ref[chunk * plan.part + f] * term
        stats_ref[0:8] = plain
        stats_ref[8:16] = damped
        stats_ref[16:24] = jnp.zeros((8, 128), F32)

    return pl.pallas_call(
        kernel,
        grid=(1,),
        in_specs=[
            pl.BlockSpec(memory_space=pltpu.SMEM),
            pl.BlockSpec(block, lambda i: (chunk, 0, 0)),
        ],
        out_specs=pl.BlockSpec((24, 128), lambda i: (0, 0)),
        out_shape=jax.ShapeDtypeStruct((24, 128), F32),
        cost_estimate=cost(2 * start.size, 4 * start.size),
        compiler_params=pltpu.CompilerParams(vmem_limit_bytes=KERNEL_BYTES),
        name="norms",
    )(damping, start)


def residual_call(plan, chunk, alpha, damping, start, mine, got):
    part, rows, sources = plan.part, plan.rows, plan.sources

    def kernel(alpha_ref, damp_ref, start_ref, mine_ref, got_ref, image_ref, out_ref, stats_ref):
        plain = damped = mixed = jnp.zeros((8, 128), F32)
        for f in range(part):
            damp = damp_ref[chunk * part + f]
            begin = start_ref[f]
            image = mine_ref[f].astype(F32) + got_ref[f].astype(F32) + damp * begin
            residual = begin - alpha_ref[0] * image
            image_ref[f] = image
            out_ref[f] = residual
            term = lanes(residual * residual)
            plain = plain + term
            damped = damped + damp * term
            mixed = mixed + damp * lanes(residual * begin)
        stats_ref[0:8] = plain
        stats_ref[8:16] = damped
        stats_ref[16:24] = mixed

    block = (part, rows, sources)
    scalars = pl.BlockSpec(memory_space=pltpu.SMEM)
    out = jax.ShapeDtypeStruct(block, F32)
    return pl.pallas_call(
        kernel,
        grid=(1,),
        in_specs=[
            scalars,
            scalars,
            pl.BlockSpec(block, lambda i: (chunk, 0, 0)),
            pl.BlockSpec((None,) + block, lambda i: (0, 0, 0, 0)),
            pl.BlockSpec((None,) + block, lambda i: (1, 0, 0, 0)),
        ],
        out_specs=[
            pl.BlockSpec(block, lambda i: (0, 0, 0)),
            pl.BlockSpec(block, lambda i: (0, 0, 0)),
            pl.BlockSpec((24, 128), lambda i: (0, 0)),
        ],
        out_shape=[out, out, jax.ShapeDtypeStruct((24, 128), F32)],
        cost_estimate=cost(8 * part * rows * sources, 16 * part * rows * sources),
        compiler_params=pltpu.CompilerParams(vmem_limit_bytes=KERNEL_BYTES),
        name="residual",
    )(alpha, damping, start, mine, got)


def body(n_sens, n_src, operator, right_side, noise_weights, damping):
    plan = Plan(operator, right_side, n_sens, n_src, CHUNKS)
    sens, src = lax.axis_index("sens"), lax.axis_index("src")
    pair, core, half, group = sens // 2, sens % 2, src % 2, src // 2
    meta = jnp.stack([pair, core, half, group]).astype(jnp.int32)
    part, rows, block = plan.part, plan.rows, plan.block
    levels = range(n_src.bit_length() - 1)
    chunks = range(plan.chunks)

    def to_core(array):
        return lax.ppermute(array, "sens", [(i, i ^ 1) for i in range(n_sens)])

    def to_pair(array):
        return lax.ppermute(array, "sens", [(i, i ^ 2) for i in range(n_sens)])

    def to_src(array, step):
        return lax.ppermute(array, "src", [(j, j ^ step) for j in range(n_src)])

    def in_turn(arrays, move):
        moved = []
        for k, array in enumerate(arrays):
            if k > 0:
                array = arrays[k] = ordered(array, moved[-1])
            moved.append(move(array))
        return moved

    def total(sums):
        steps = [sums]
        steps.append(steps[-1] + to_core(steps[-1]))
        steps.append(steps[-1] + to_pair(steps[-1]))
        for level in levels:
            steps.append(steps[-1] + to_src(steps[-1], 1 << level))
        return jnp.sum(steps[-1].reshape(-1, 8 * 128), axis=1), steps

    def double(table, level):
        other = to_src(table, 1 << level)
        low = (src >> level) % 2 == 0
        return jnp.concatenate([jnp.where(low, table, other), jnp.where(low, other, table)], axis=0)

    whole = operator.reshape(plan.pairs, 2, block, 2, plan.sensors, plan.sources)
    start = right_side.reshape(block, rows, plan.sources)

    casts = [cast_call(plan, k, start) for k in chunks]
    cuts = [cut_call(plan, k, meta, whole, (casts[0],)) for k in chunks]
    got_b = in_turn(list(casts), to_pair)
    far, pairs = [to_core(cut) for cut in cuts], []
    for k in chunks:
        wait = tuple(casts[1:]) + tuple(cuts[1:]) if k == 0 else ()
        pairs.append(forward_call(plan, k, meta, whole, far[k], True, (start, got_b[k]), wait))
    weights = double(ordered(noise_weights, pairs[-1][0]), 0)

    for level in levels[1:]:
        weights = double(weights, level)
    weights = weights.reshape(plan.pairs, 2, block, plan.sensors)
    weights_near = lax.dynamic_index_in_dim(weights, core, 1, keepdims=False)
    weights_far = to_core(lax.dynamic_index_in_dim(weights, 1 - core, 1, keepdims=False))
    weights = jnp.concatenate([weights_near, weights_far], axis=-1)
    weights = lax.dynamic_index_in_dim(weights, pair ^ half, 0, keepdims=False)
    damping_row = jnp.where(half == 0, damping, to_pair(damping))
    steps = [2 * d for d in range(1, plan.groups)]

    def reduce_field(keep, got, wait=()):
        mine, *sends = split_call(plan, meta, keep, got, wait)
        return [mine] + [to_src(piece, step) for piece, step in zip(sends, steps)]

    def to_half(array):
        return to_src(array, 1)

    def both_products(scaled, scalar_steps, last, then):
        outs, wait = [], ()
        for k in chunks:
            pieces = [scaled[k]] + [to_src(scaled[k], step) for step in steps]
            own = place_call(plan, meta, pieces, wait)
            halves = (own, to_half(own))
            wait = () if k == 0 else (outs[k - 1][1][0], scalar_steps[-1])
            out = adjoint_call(plan, k, meta, whole, far[k], halves, last, wait)
            outs.append((out, then(k, out)))
            wait = (out[0] if last else out, scalar_steps[3])
        return outs

    sends = [send for send, _ in pairs]
    got = in_turn(sends, to_half)
    pieces = [reduce_field(pairs[k][1], got[k], tuple(sends[k + 1:k + 2])) for k in chunks]
    scaled, field, stats = zip(*[
        sensor_call(plan, k, meta, weights, pieces[k], norms_call(plan, k, damping, start))
        for k in chunks
    ])
    sums, steps_0 = total(sum(stats))
    norm_0, curve_0 = sums[0], sums[1]
    alpha_0 = (norm_0 / curve_0)[None]

    def go_on(k, back):
        got = to_pair(back)
        send, keep = forward_call(plan, k, meta, whole, far[k], False, (back, got))
        return send, keep, got

    outs = both_products(scaled, steps_0, False, go_on)
    back = [out for out, _ in outs]
    sends, keeps, got_back = zip(*[rest for _, rest in outs])
    got = in_turn(list(sends), to_half)
    image_0, residual, norms = zip(*[
        residual_call(plan, k, alpha_0, damping, start, back[k], got_back[k]) for k in chunks
    ])
    pieces = [reduce_field(keeps[k], got[k]) for k in chunks]
    scaled, stats = zip(*[
        sensor_call(plan, k, meta, weights, pieces[k], norms[k], alpha_0, damping_row, field[k])
        for k in chunks
    ])
    sums, steps_1 = total(sum(stats))
    norm_1 = sums[0]
    beta = norm_1 / norm_0
    curve_1 = sums[1] + 2.0 * beta * sums[2] + beta * beta * curve_0
    alpha_1 = norm_1 / curve_1

    outs = both_products(scaled, steps_1, True, lambda k, out: (to_pair(out[0]),))
    final = [out[1] + rest[0].astype(F32) for out, rest in outs]
    residual, image_0 = jnp.concatenate(residual), jnp.concatenate(image_0)
    image_1 = jnp.concatenate(final) + damping[:, None, None] * residual + beta * image_0
    solution = alpha_0 * start + alpha_1 * (residual + beta * start)
    residual = residual - alpha_1 * image_1
    return solution.reshape(right_side.shape), residual.reshape(right_side.shape)


def solution(mesh):
    in_specs = (
        P(None, None, "sens", "src"),
        P("sens", None, None, "src"),
        P("src", "sens"),
        P("sens"),
    )
    out_specs = (P("sens", None, None, "src"), P("sens", None, None, "src"))
    shard = functools.partial(body, mesh.shape["sens"], mesh.shape["src"])
    return jax.shard_map(shard, mesh=mesh, in_specs=in_specs, out_specs=out_specs, check_vma=False)
```

```python
import functools

import jax
import jax.numpy as jnp
from jax import lax
from jax.experimental import pallas as pl
from jax.experimental.pallas import tpu as pltpu
from jax.sharding import PartitionSpec as P

CHUNKS = 2
KERNEL_BYTES = 16 * 2 ** 20
PRODUCT_BYTES = 56 * 2 ** 20
F32 = jnp.float32
BF16 = jnp.bfloat16
ANYWHERE = pl.BlockSpec(memory_space=pl.ANY)
NT = (((1,), (1,)), ((), ()))
NN = (((1,), (0,)), ((), ()))


def largest_divisor(extent, most):
    return next(size for size in range(min(extent, most), 0, -1) if extent % size == 0)


def turned(block, sign):
    half = block.shape[0] // 2
    upper, lower = block[:half], block[half:]
    return jnp.concatenate([-lower, upper] if sign < 0 else [lower, -upper], axis=0)


def forward_rows(vector, near, far):
    left = jnp.concatenate([vector, turned(vector, -1)], axis=1)
    right = jnp.concatenate(
        [jnp.concatenate([part[0], part[1]], axis=1) for part in (near, far)], axis=0
    )
    return lax.dot_general(left, right, NT, preferred_element_type=F32)


def adjoint_rows(field, near, far):
    sensors = near[0].shape[0]
    total = None
    for part, piece in ((near, field[:, :sensors]), (far, field[:, sensors:])):
        left = jnp.concatenate([piece, turned(piece, 1)], axis=1)
        right = jnp.concatenate(part, axis=0)
        term = lax.dot_general(left, right, NN, preferred_element_type=F32)
        total = term if total is None else total + term
    return total


def cost(flops, moved):
    return pl.CostEstimate(flops=flops // 1000, bytes_accessed=moved // 1000, transcendentals=0)


class Plan:
    def __init__(self, operator, right_side, n_sens, n_src, chunks):
        self.freqs, _, self.sensors, self.sources = operator.shape
        self.block = right_side.shape[0]
        self.rows = right_side.shape[1] * right_side.shape[2]
        self.pairs = n_sens // 2
        self.groups = n_src // 2
        self.chunks = chunks
        self.part = self.block // chunks
        self.step = largest_divisor(self.part, 8)
        self.steps = self.part // self.step
        self.flops = 16 * self.part * self.rows * self.sensors * self.sources * 2
        self.piece = self.part * self.rows // self.groups


class Parts:
    def __init__(self, plan, chunk, m, blk_of, refs):
        (whole, far), (near_buf, far_buf, sems) = refs
        self.buffers, self.copies = (near_buf, far_buf), {}
        for phase in range(2):
            for t in range(plan.steps):
                slot = phase * plan.steps + t
                side = m[0] ^ blk_of(phase, m)
                rows = pl.ds(t * plan.step, plan.step)
                near_rows = pl.ds(chunk * plan.part + t * plan.step, plan.step)
                self.copies[phase, t] = [
                    pltpu.make_async_copy(ref, buffer.at[slot], sems.at[slot, place])
                    for place, (ref, buffer) in enumerate((
                        (whole.at[side, m[1], near_rows], near_buf),
                        (far.at[side, rows], far_buf),
                    ))
                ]
        self.order = list(self.copies)
        for slot in self.order[:2]:
            self.start(slot)

    def start(self, slot):
        for copy in self.copies[slot]:
            copy.start()

    def get(self, plan, phase, t):
        for copy in self.copies[phase, t]:
            copy.wait()
        slot = phase * plan.steps + t
        for later in self.order[slot + 2:slot + 3]:
            self.start(later)
        return [
            tuple(tuple(buffer[slot, f, c] for c in range(2)) for buffer in self.buffers)
            for f in range(plan.step)
        ]

    @staticmethod
    def scratch(plan):
        buffer = pltpu.VMEM((2 * plan.steps, plan.step, 2, plan.sensors, plan.sources), BF16)
        return [buffer, buffer, pltpu.SemaphoreType.DMA((2 * plan.steps, 2))]


def cut_call(plan, chunk, meta, whole, wait=()):
    def kernel(m, whole_ref, *refs):
        out_ref, buffer, sems = refs[len(wait):]
        slots = [(side, t) for side in range(plan.pairs) for t in range(plan.steps)]
        ins, outs = [], []
        for slot, (side, t) in enumerate(slots):
            rows = pl.ds(chunk * plan.part + t * plan.step, plan.step)
            ins.append(pltpu.make_async_copy(
                whole_ref.at[side, 1 - m[1], rows], buffer.at[slot], sems.at[0, slot]
            ))
            outs.append(pltpu.make_async_copy(
                buffer.at[slot], out_ref.at[side, pl.ds(t * plan.step, plan.step)], sems.at[1, slot]
            ))
        for copy in ins:
            copy.start()
        for slot in range(len(slots)):
            ins[slot].wait()
            outs[slot].start()
        for copy in outs:
            copy.wait()

    shape = (plan.pairs, plan.part, 2, plan.sensors, plan.sources)
    return pl.pallas_call(
        kernel,
        in_specs=[pl.BlockSpec(memory_space=pltpu.SMEM), ANYWHERE] + [ANYWHERE] * len(wait),
        out_specs=ANYWHERE,
        out_shape=jax.ShapeDtypeStruct(shape, BF16),
        scratch_shapes=[
            pltpu.VMEM((plan.pairs * plan.steps, plan.step) + shape[2:], BF16),
            pltpu.SemaphoreType.DMA((2, plan.pairs * plan.steps)),
        ],
        cost_estimate=cost(0, 8 * plan.part * plan.sensors * plan.sources),
        compiler_params=pltpu.CompilerParams(vmem_limit_bytes=PRODUCT_BYTES),
        name="cut",
    )(meta, whole, *wait)


def cast_call(plan, chunk, start, wait=()):
    shape = (plan.part, plan.rows, plan.sources)

    def kernel(start_ref, *refs):
        out_ref, buffer, sem = refs[len(wait):]
        rows = pl.ds(chunk * plan.part, plan.part)
        copy = pltpu.make_async_copy(start_ref.at[rows], buffer, sem)
        copy.start()
        copy.wait()
        out_ref[...] = buffer[...].astype(BF16)

    return pl.pallas_call(
        kernel,
        in_specs=[ANYWHERE] + [ANYWHERE] * len(wait),
        out_specs=pl.BlockSpec(memory_space=pltpu.VMEM),
        out_shape=jax.ShapeDtypeStruct(shape, BF16),
        scratch_shapes=[pltpu.VMEM(shape, F32), pltpu.SemaphoreType.DMA(())],
        cost_estimate=cost(0, 6 * plan.part * plan.rows * plan.sources),
        compiler_params=pltpu.CompilerParams(vmem_limit_bytes=KERNEL_BYTES),
        name="cast",
    )(start, *wait)


def forward_call(plan, chunk, meta, whole, far, first, vectors, wait=()):
    blk_of = lambda p, m: 1 - (m[2] ^ p)

    def kernel(m, whole, far, one_ref, two_ref, *refs):
        outs, scratch = refs[len(wait):len(wait) + 2], refs[len(wait) + 2:]
        parts = Parts(plan, chunk, m, blk_of, ((whole, far), scratch))
        for phase in range(2):
            blk = blk_of(phase, m)
            for t in range(plan.steps):
                for i, (near_part, far_part) in enumerate(parts.get(plan, phase, t)):
                    f = t * plan.step + i
                    if first:
                        vector = jnp.where(blk == 0, one_ref[f].astype(BF16), two_ref[f])
                    else:
                        vector = one_ref[blk, f].astype(F32) + two_ref[1 - blk, f].astype(F32)
                    outs[phase][f] = forward_rows(vector.astype(BF16), near_part, far_part).astype(BF16)

    size = (plan.part, plan.rows, plan.sources)
    if first:
        vec_specs = [
            pl.BlockSpec(size, lambda i: (chunk, 0, 0)),
            pl.BlockSpec(size, lambda i: (0, 0, 0)),
        ]
    else:
        vec_specs = [pl.BlockSpec((2,) + size, lambda i: (0, 0, 0, 0))] * 2
    shape = (plan.part, plan.rows, 2 * plan.sensors)
    return pl.pallas_call(
        kernel,
        grid=(1,),
        in_specs=[pl.BlockSpec(memory_space=pltpu.SMEM)] + [ANYWHERE] * 2 + vec_specs
        + [ANYWHERE] * len(wait),
        out_specs=[pl.BlockSpec(shape, lambda i: (0, 0, 0))] * 2,
        out_shape=[jax.ShapeDtypeStruct(shape, BF16)] * 2,
        scratch_shapes=Parts.scratch(plan),
        cost_estimate=cost(plan.flops, 16 * plan.part * plan.sensors * plan.sources),
        compiler_params=pltpu.CompilerParams(vmem_limit_bytes=PRODUCT_BYTES),
        name="forward",
    )(meta, whole, far, *vectors, *wait)


def adjoint_call(plan, chunk, meta, whole, far, halves, last, wait=()):
    blk_of = lambda p, m: 1 - p
    n_out = 2 if last else 1

    def kernel(m, whole, far, own_ref, got_ref, *refs):
        outs, scratch = refs[len(wait):len(wait) + n_out], refs[len(wait) + n_out:]
        parts = Parts(plan, chunk, m, blk_of, ((whole, far), scratch))
        for phase in range(2):
            blk = blk_of(phase, m)
            for t in range(plan.steps):
                for i, (near_part, far_part) in enumerate(parts.get(plan, phase, t)):
                    f = t * plan.step + i
                    field = jnp.where(blk == m[2], own_ref[f], got_ref[f])
                    back = adjoint_rows(field, near_part, far_part)
                    if last:
                        outs[phase][f] = back.astype(outs[phase].dtype)
                    else:
                        outs[0][blk, f] = back.astype(BF16)

    size = (plan.part, plan.rows, 2 * plan.sensors)
    shape = (plan.part, plan.rows, plan.sources)
    if last:
        out_specs = [pl.BlockSpec(shape, lambda i: (0, 0, 0))] * 2
        out_shape = [jax.ShapeDtypeStruct(shape, BF16), jax.ShapeDtypeStruct(shape, F32)]
    else:
        out_specs = pl.BlockSpec((2,) + shape, lambda i: (0, 0, 0, 0))
        out_shape = jax.ShapeDtypeStruct((2,) + shape, BF16)
    return pl.pallas_call(
        kernel,
        grid=(1,),
        in_specs=[pl.BlockSpec(memory_space=pltpu.SMEM)] + [ANYWHERE] * 2
        + [pl.BlockSpec(size, lambda i: (0, 0, 0))] * 2 + [ANYWHERE] * len(wait),
        out_specs=out_specs,
        out_shape=out_shape,
        scratch_shapes=Parts.scratch(plan),
        cost_estimate=cost(plan.flops, 16 * plan.part * plan.sensors * plan.sources),
        compiler_params=pltpu.CompilerParams(vmem_limit_bytes=PRODUCT_BYTES),
        name="adjoint",
    )(meta, whole, far, *halves, *wait)


def split_call(plan, meta, keep, got, wait=()):
    piece, groups = plan.piece, plan.groups
    width = keep.shape[-1]

    def kernel(m, keep_ref, got_ref, *refs):
        mine_ref, *sends = refs[len(wait):]
        for d in range(groups):
            place = pl.ds(pl.multiple_of((m[3] ^ d) * piece, piece), piece)
            total = keep_ref[place].astype(F32) + got_ref[place].astype(F32)
            if d == 0:
                mine_ref[...] = total
            else:
                sends[d - 1][...] = total.astype(BF16)

    whole = pl.BlockSpec(memory_space=pltpu.VMEM)
    return pl.pallas_call(
        kernel,
        in_specs=[pl.BlockSpec(memory_space=pltpu.SMEM), whole, whole] + [ANYWHERE] * len(wait),
        out_specs=[whole] * groups,
        out_shape=[jax.ShapeDtypeStruct((piece, width), F32)]
        + [jax.ShapeDtypeStruct((piece, width), BF16)] * (groups - 1),
        cost_estimate=cost(groups * piece * width, groups * piece * width * 8),
        compiler_params=pltpu.CompilerParams(vmem_limit_bytes=KERNEL_BYTES),
        name="split",
    )(meta, keep.reshape(-1, width), got.reshape(-1, width), *wait)


def place_call(plan, meta, pieces, wait=()):
    piece, groups = plan.piece, plan.groups
    width = pieces[0].shape[-1]

    def kernel(m, *refs):
        for d in range(groups):
            place = pl.ds(pl.multiple_of((m[3] ^ d) * piece, piece), piece)
            refs[-1][place] = refs[d][...]

    whole = pl.BlockSpec(memory_space=pltpu.VMEM)
    out = pl.pallas_call(
        kernel,
        in_specs=[pl.BlockSpec(memory_space=pltpu.SMEM)] + [whole] * groups
        + [ANYWHERE] * len(wait),
        out_specs=whole,
        out_shape=jax.ShapeDtypeStruct((groups * piece, width), BF16),
        cost_estimate=cost(0, groups * piece * width * 4),
        compiler_params=pltpu.CompilerParams(vmem_limit_bytes=KERNEL_BYTES),
        name="place",
    )(meta, *pieces, *wait)
    return out.reshape(plan.part, plan.rows, width)


def ordered(array, *earlier):
    def kernel(*refs):
        del refs

    return pl.pallas_call(
        kernel,
        in_specs=[ANYWHERE] * (1 + len(earlier)),
        out_specs=ANYWHERE,
        out_shape=jax.ShapeDtypeStruct(array.shape, array.dtype),
        input_output_aliases={0: 0},
        cost_estimate=cost(0, 0),
        compiler_params=pltpu.CompilerParams(vmem_limit_bytes=KERNEL_BYTES),
        name="ordered",
    )(array, *earlier)


def lanes(array):
    total = jnp.sum(array.reshape(-1, 8, array.shape[-1]), axis=0)
    return sum(total[:, i:i + 128] for i in range(0, array.shape[-1], 128))


def sensor_call(
    plan, chunk, meta, weights, pieces, norms, alpha=None, damping=None, old=None, wait=()
):
    piece, rows, groups = plan.piece, plan.rows, plan.groups
    width = pieces[0].shape[-1]
    count = max(1, piece // rows)
    high = piece // count
    second = old is not None

    def kernel(m, *refs):
        if second:
            alpha_ref, damp_ref, old_ref, *refs = refs
        weights_ref, norms_ref, *refs = refs
        ins, (out_ref, *more) = refs[:groups], refs[groups + len(wait):]
        stats_ref = more[-1]
        square = cross = jnp.zeros((8, 128), F32)
        for c in range(count):
            at = pl.ds(c * high, high)
            freq = chunk * plan.part + (m[3] * piece + c * high) // rows
            field = ins[0][at]
            for ref in ins[1:]:
                field = field + ref[at].astype(F32)
            if second:
                factor = 1.0 - alpha_ref[0] * damp_ref[freq]
                field = factor * old_ref[at] - alpha_ref[0] * field
            scaled = weights_ref[pl.ds(freq, 1)] * field
            out_ref[at] = scaled.astype(BF16)
            square = square + lanes(scaled * field)
            if second:
                cross = cross + lanes(scaled * old_ref[at])
            else:
                more[0][at] = field
        stats_ref[0:8] = norms_ref[0:8]
        stats_ref[8:16] = norms_ref[8:16] + square
        stats_ref[16:24] = norms_ref[16:24] + cross

    whole = pl.BlockSpec(memory_space=pltpu.VMEM)
    scalars = pl.BlockSpec(memory_space=pltpu.SMEM)
    first_out = [] if second else [jax.ShapeDtypeStruct((piece, width), F32)]
    extra = (alpha, damping, old) if second else ()
    out_shape = [jax.ShapeDtypeStruct((piece, width), BF16)] + first_out
    out_shape = out_shape + [jax.ShapeDtypeStruct((24, 128), F32)]
    return pl.pallas_call(
        kernel,
        in_specs=[scalars] + ([scalars] * 2 + [whole] if second else []) + [whole] * (2 + groups)
        + [ANYWHERE] * len(wait),
        out_specs=[whole] * len(out_shape),
        out_shape=out_shape,
        cost_estimate=cost(8 * piece * width, 16 * piece * width),
        compiler_params=pltpu.CompilerParams(vmem_limit_bytes=KERNEL_BYTES),
        name="sensor",
    )(meta, *extra, weights, norms, *pieces, *wait)


def norms_call(plan, chunk, damping, start):
    block = (plan.part, plan.rows, plan.sources)

    def kernel(damp_ref, start_ref, stats_ref):
        plain = damped = jnp.zeros((8, 128), F32)
        for f in range(plan.part):
            term = lanes(start_ref[f] * start_ref[f])
            plain = plain + term
            damped = damped + damp_ref[chunk * plan.part + f] * term
        stats_ref[0:8] = plain
        stats_ref[8:16] = damped
        stats_ref[16:24] = jnp.zeros((8, 128), F32)

    return pl.pallas_call(
        kernel,
        grid=(1,),
        in_specs=[
            pl.BlockSpec(memory_space=pltpu.SMEM),
            pl.BlockSpec(block, lambda i: (chunk, 0, 0)),
        ],
        out_specs=pl.BlockSpec((24, 128), lambda i: (0, 0)),
        out_shape=jax.ShapeDtypeStruct((24, 128), F32),
        cost_estimate=cost(2 * start.size, 4 * start.size),
        compiler_params=pltpu.CompilerParams(vmem_limit_bytes=KERNEL_BYTES),
        name="norms",
    )(damping, start)


def residual_call(plan, chunk, alpha, damping, start, mine, got):
    part, rows, sources = plan.part, plan.rows, plan.sources

    def kernel(alpha_ref, damp_ref, start_ref, mine_ref, got_ref, image_ref, out_ref, stats_ref):
        plain = damped = mixed = jnp.zeros((8, 128), F32)
        for f in range(part):
            damp = damp_ref[chunk * part + f]
            begin = start_ref[f]
            image = mine_ref[f].astype(F32) + got_ref[f].astype(F32) + damp * begin
            residual = begin - alpha_ref[0] * image
            image_ref[f] = image
            out_ref[f] = residual
            term = lanes(residual * residual)
            plain = plain + term
            damped = damped + damp * term
            mixed = mixed + damp * lanes(residual * begin)
        stats_ref[0:8] = plain
        stats_ref[8:16] = damped
        stats_ref[16:24] = mixed

    block = (part, rows, sources)
    scalars = pl.BlockSpec(memory_space=pltpu.SMEM)
    out = jax.ShapeDtypeStruct(block, F32)
    return pl.pallas_call(
        kernel,
        grid=(1,),
        in_specs=[
            scalars,
            scalars,
            pl.BlockSpec(block, lambda i: (chunk, 0, 0)),
            pl.BlockSpec((None,) + block, lambda i: (0, 0, 0, 0)),
            pl.BlockSpec((None,) + block, lambda i: (1, 0, 0, 0)),
        ],
        out_specs=[
            pl.BlockSpec(block, lambda i: (0, 0, 0)),
            pl.BlockSpec(block, lambda i: (0, 0, 0)),
            pl.BlockSpec((24, 128), lambda i: (0, 0)),
        ],
        out_shape=[out, out, jax.ShapeDtypeStruct((24, 128), F32)],
        cost_estimate=cost(8 * part * rows * sources, 16 * part * rows * sources),
        compiler_params=pltpu.CompilerParams(vmem_limit_bytes=KERNEL_BYTES),
        name="residual",
    )(alpha, damping, start, mine, got)


def body(n_sens, n_src, operator, right_side, noise_weights, damping):
    plan = Plan(operator, right_side, n_sens, n_src, CHUNKS)
    sens, src = lax.axis_index("sens"), lax.axis_index("src")
    pair, core, half, group = sens // 2, sens % 2, src % 2, src // 2
    meta = jnp.stack([pair, core, half, group]).astype(jnp.int32)
    part, rows, block = plan.part, plan.rows, plan.block
    levels = range(n_src.bit_length() - 1)
    chunks = range(plan.chunks)

    def to_core(array):
        return lax.ppermute(array, "sens", [(i, i ^ 1) for i in range(n_sens)])

    def to_pair(array):
        return lax.ppermute(array, "sens", [(i, i ^ 2) for i in range(n_sens)])

    def to_src(array, step):
        return lax.ppermute(array, "src", [(j, j ^ step) for j in range(n_src)])

    def in_turn(arrays, move):
        moved = []
        for k, array in enumerate(arrays):
            if k > 0:
                array = arrays[k] = ordered(array, moved[-1])
            moved.append(move(array))
        return moved

    def total_near(sums):
        sums = sums + to_core(sums)
        sums = sums + to_pair(sums)
        return sums + to_src(sums, 1)

    def total_far(sums):
        for level in levels[1:]:
            sums = sums + to_src(sums, 1 << level)
        return sums, jnp.sum(sums.reshape(-1, 8 * 128), axis=1)

    def double(table, level):
        other = to_src(table, 1 << level)
        low = (src >> level) % 2 == 0
        return jnp.concatenate([jnp.where(low, table, other), jnp.where(low, other, table)], axis=0)

    whole = operator.reshape(plan.pairs, 2, block, 2, plan.sensors, plan.sources)
    start = right_side.reshape(block, rows, plan.sources)

    casts = [cast_call(plan, k, start) for k in chunks]
    cuts = [cut_call(plan, k, meta, whole, (casts[0],)) for k in chunks]
    got_b = in_turn(list(casts), to_pair)
    weights = noise_weights
    for level in levels[:2]:
        weights = double(weights, level)
    far, pairs = [to_core(cut) for cut in cuts], []
    for k in chunks:
        wait = tuple(casts[1:]) + tuple(cuts[1:]) + (weights,) if k == 0 else ()
        pairs.append(forward_call(plan, k, meta, whole, far[k], True, (start, got_b[k]), wait))

    for level in levels[2:]:
        weights = double(weights, level)
    weights = weights.reshape(plan.pairs, 2, block, plan.sensors)
    weights_near = lax.dynamic_index_in_dim(weights, core, 1, keepdims=False)
    weights_far = to_core(lax.dynamic_index_in_dim(weights, 1 - core, 1, keepdims=False))
    weights = jnp.concatenate([weights_near, weights_far], axis=-1)
    weights = lax.dynamic_index_in_dim(weights, pair ^ half, 0, keepdims=False)
    damping_row = jnp.where(half == 0, damping, to_pair(damping))
    steps = [2 * d for d in range(1, plan.groups)]

    def reduce_field(keep, got, wait=()):
        mine, *sends = split_call(plan, meta, keep, got, wait)
        return [mine] + [to_src(piece, step) for piece, step in zip(sends, steps)]

    def to_half(array):
        return to_src(array, 1)

    def both_products(scaled, near_sums, last, then):
        outs, wait, sums = [], (), None
        for k in chunks:
            pieces = [scaled[k]] + [to_src(scaled[k], step) for step in steps]
            own = place_call(plan, meta, pieces, wait)
            halves = (own, to_half(own))
            if k == 1:
                after = outs[0][1][0]
                far_sums, sums = total_far(near_sums if last else ordered(near_sums, after))
                wait = (after, far_sums)
            out = adjoint_call(plan, k, meta, whole, far[k], halves, last, wait if k > 0 else ())
            outs.append((out, then(k, out)))
            wait = (out[0] if last else out, near_sums)
        return outs, total_far(near_sums)[1] if sums is None else sums

    sends = [send for send, _ in pairs]
    got = in_turn(sends, to_half)
    pieces = [reduce_field(pairs[k][1], got[k], tuple(sends[k + 1:k + 2])) for k in chunks]
    scaled, field, stats = zip(*[
        sensor_call(
            plan, k, meta, weights, pieces[k], norms_call(plan, k, damping, start),
            wait=tuple(got[k + 1:k + 2]),
        )
        for k in chunks
    ])
    near_0 = total_near(sum(stats))

    def go_on(k, back):
        got = to_pair(back)
        send, keep = forward_call(plan, k, meta, whole, far[k], False, (back, got))
        return send, keep, got

    outs, sums = both_products(scaled, near_0, False, go_on)
    norm_0, curve_0 = sums[0], sums[1]
    alpha_0 = (norm_0 / curve_0)[None]
    back = [out for out, _ in outs]
    sends, keeps, got_back = zip(*[rest for _, rest in outs])
    got = in_turn(list(sends), to_half)
    image_0, residual, norms = zip(*[
        residual_call(plan, k, alpha_0, damping, start, back[k], got_back[k]) for k in chunks
    ])
    pieces = [reduce_field(keeps[k], got[k]) for k in chunks]
    scaled, stats = zip(*[
        sensor_call(plan, k, meta, weights, pieces[k], norms[k], alpha_0, damping_row, field[k])
        for k in chunks
    ])
    near_1 = total_near(sum(stats))
    outs, sums = both_products(scaled, near_1, True, lambda k, out: (to_pair(out[0]),))
    norm_1 = sums[0]
    beta = norm_1 / norm_0
    curve_1 = sums[1] + 2.0 * beta * sums[2] + beta * beta * curve_0
    alpha_1 = norm_1 / curve_1

    final = [out[1] + rest[0].astype(F32) for out, rest in outs]
    residual, image_0 = jnp.concatenate(residual), jnp.concatenate(image_0)
    image_1 = jnp.concatenate(final) + damping[:, None, None] * residual + beta * image_0
    solution = alpha_0 * start + alpha_1 * (residual + beta * start)
    residual = residual - alpha_1 * image_1
    return solution.reshape(right_side.shape), residual.reshape(right_side.shape)


def solution(mesh):
    in_specs = (
        P(None, None, "sens", "src"),
        P("sens", None, None, "src"),
        P("src", "sens"),
        P("sens"),
    )
    out_specs = (P("sens", None, None, "src"), P("sens", None, None, "src"))
    shard = functools.partial(body, mesh.shape["sens"], mesh.shape["src"])
    return jax.shard_map(shard, mesh=mesh, in_specs=in_specs, out_specs=out_specs, check_vma=False)
```

```python
import functools

import jax
import jax.numpy as jnp
from jax import lax
from jax.experimental import pallas as pl
from jax.experimental.pallas import tpu as pltpu
from jax.sharding import PartitionSpec as P

CHUNKS = 2
KERNEL_BYTES = 16 * 2 ** 20
PRODUCT_BYTES = 56 * 2 ** 20
F32 = jnp.float32
BF16 = jnp.bfloat16
ANYWHERE = pl.BlockSpec(memory_space=pl.ANY)
NT = (((1,), (1,)), ((), ()))
NN = (((1,), (0,)), ((), ()))


def largest_divisor(extent, most):
    return next(size for size in range(min(extent, most), 0, -1) if extent % size == 0)


def turned(block, sign):
    half = block.shape[0] // 2
    upper, lower = block[:half], block[half:]
    return jnp.concatenate([-lower, upper] if sign < 0 else [lower, -upper], axis=0)


def forward_rows(vector, near, far):
    left = jnp.concatenate([vector, turned(vector, -1)], axis=1)
    right = jnp.concatenate(
        [jnp.concatenate([part[0], part[1]], axis=1) for part in (near, far)], axis=0
    )
    return lax.dot_general(left, right, NT, preferred_element_type=F32)


def adjoint_rows(field, near, far):
    sensors = near[0].shape[0]
    total = None
    for part, piece in ((near, field[:, :sensors]), (far, field[:, sensors:])):
        left = jnp.concatenate([piece, turned(piece, 1)], axis=1)
        right = jnp.concatenate(part, axis=0)
        term = lax.dot_general(left, right, NN, preferred_element_type=F32)
        total = term if total is None else total + term
    return total


def cost(flops, moved):
    return pl.CostEstimate(flops=flops // 1000, bytes_accessed=moved // 1000, transcendentals=0)


class Plan:
    def __init__(self, operator, right_side, n_sens, n_src, chunks):
        self.freqs, _, self.sensors, self.sources = operator.shape
        self.block = right_side.shape[0]
        self.rows = right_side.shape[1] * right_side.shape[2]
        self.pairs = n_sens // 2
        self.groups = n_src // 2
        self.chunks = chunks
        self.part = self.block // chunks
        self.step = largest_divisor(self.part, 8)
        self.steps = self.part // self.step
        self.flops = 16 * self.part * self.rows * self.sensors * self.sources * 2
        self.piece = self.part * self.rows // self.groups


class Parts:
    def __init__(self, plan, chunk, m, blk_of, refs):
        (whole, far), (near_buf, far_buf, sems) = refs
        self.buffers, self.copies = (near_buf, far_buf), {}
        high = plan.step * 2 * plan.sensors
        for phase in range(2):
            for t in range(plan.steps):
                slot = phase * plan.steps + t
                side = m[0] ^ blk_of(phase, m)
                near_rows = pl.ds((chunk * plan.steps + t) * high, high)
                self.copies[phase, t] = [
                    pltpu.make_async_copy(ref, buffer.at[slot], sems.at[slot, place])
                    for place, (ref, buffer) in enumerate((
                        (whole.at[side, m[1], near_rows], near_buf),
                        (far.at[side, pl.ds(t * high, high)], far_buf),
                    ))
                ]
        for copies in self.copies.values():
            for copy in copies:
                copy.start()

    def get(self, plan, phase, t):
        for copy in self.copies[phase, t]:
            copy.wait()
        slot, high = phase * plan.steps + t, plan.sensors
        return [
            tuple(
                tuple(buffer[slot, pl.ds((2 * f + c) * high, high)] for c in range(2))
                for buffer in self.buffers
            )
            for f in range(plan.step)
        ]

    @staticmethod
    def scratch(plan):
        buffer = pltpu.VMEM((2 * plan.steps, plan.step * 2 * plan.sensors, plan.sources), BF16)
        return [buffer, buffer, pltpu.SemaphoreType.DMA((2 * plan.steps, 2))]


def cut_call(plan, chunk, meta, whole, wait=()):
    def kernel(m, whole_ref, *refs):
        out_ref, buffer, sems = refs[len(wait):]
        high = plan.step * 2 * plan.sensors
        slots = [(side, t) for side in range(plan.pairs) for t in range(plan.steps)]
        ins, outs = [], []
        for slot, (side, t) in enumerate(slots):
            rows = pl.ds((chunk * plan.steps + t) * high, high)
            ins.append(pltpu.make_async_copy(
                whole_ref.at[side, 1 - m[1], rows], buffer.at[slot], sems.at[0, slot]
            ))
            outs.append(pltpu.make_async_copy(
                buffer.at[slot], out_ref.at[side, pl.ds(t * high, high)], sems.at[1, slot]
            ))
        for copy in ins:
            copy.start()
        for slot in range(len(slots)):
            ins[slot].wait()
            outs[slot].start()
        for copy in outs:
            copy.wait()

    shape = (plan.pairs, plan.part * 2 * plan.sensors, plan.sources)
    return pl.pallas_call(
        kernel,
        in_specs=[pl.BlockSpec(memory_space=pltpu.SMEM), ANYWHERE] + [ANYWHERE] * len(wait),
        out_specs=ANYWHERE,
        out_shape=jax.ShapeDtypeStruct(shape, BF16),
        scratch_shapes=[
            pltpu.VMEM((plan.pairs * plan.steps, shape[1] // plan.steps, plan.sources), BF16),
            pltpu.SemaphoreType.DMA((2, plan.pairs * plan.steps)),
        ],
        cost_estimate=cost(0, 8 * plan.part * plan.sensors * plan.sources),
        compiler_params=pltpu.CompilerParams(vmem_limit_bytes=PRODUCT_BYTES),
        name="cut",
    )(meta, whole, *wait)


def cast_call(plan, chunk, start, wait=()):
    shape = (plan.part, plan.rows, plan.sources)

    def kernel(start_ref, *refs):
        out_ref, buffer, sem = refs[len(wait):]
        rows = pl.ds(chunk * plan.part, plan.part)
        copy = pltpu.make_async_copy(start_ref.at[rows], buffer, sem)
        copy.start()
        copy.wait()
        out_ref[...] = buffer[...].astype(BF16)

    return pl.pallas_call(
        kernel,
        in_specs=[ANYWHERE] + [ANYWHERE] * len(wait),
        out_specs=pl.BlockSpec(memory_space=pltpu.VMEM),
        out_shape=jax.ShapeDtypeStruct(shape, BF16),
        scratch_shapes=[pltpu.VMEM(shape, F32), pltpu.SemaphoreType.DMA(())],
        cost_estimate=cost(0, 6 * plan.part * plan.rows * plan.sources),
        compiler_params=pltpu.CompilerParams(vmem_limit_bytes=KERNEL_BYTES),
        name="cast",
    )(start, *wait)


def forward_call(plan, chunk, meta, whole, far, first, vectors, wait=()):
    blk_of = lambda p, m: 1 - (m[2] ^ p)

    def kernel(m, whole, far, one_ref, two_ref, *refs):
        outs, scratch = refs[len(wait):len(wait) + 2], refs[len(wait) + 2:]
        parts = Parts(plan, chunk, m, blk_of, ((whole, far), scratch))
        for phase in range(2):
            blk = blk_of(phase, m)
            for t in range(plan.steps):
                for i, (near_part, far_part) in enumerate(parts.get(plan, phase, t)):
                    f = t * plan.step + i
                    if first:
                        vector = jnp.where(blk == 0, one_ref[f].astype(BF16), two_ref[f])
                    else:
                        vector = one_ref[blk, f].astype(F32) + two_ref[1 - blk, f].astype(F32)
                    outs[phase][f] = forward_rows(vector.astype(BF16), near_part, far_part).astype(BF16)

    size = (plan.part, plan.rows, plan.sources)
    if first:
        vec_specs = [
            pl.BlockSpec(size, lambda i: (chunk, 0, 0)),
            pl.BlockSpec(size, lambda i: (0, 0, 0)),
        ]
    else:
        vec_specs = [pl.BlockSpec((2,) + size, lambda i: (0, 0, 0, 0))] * 2
    shape = (plan.part, plan.rows, 2 * plan.sensors)
    return pl.pallas_call(
        kernel,
        grid=(1,),
        in_specs=[pl.BlockSpec(memory_space=pltpu.SMEM)] + [ANYWHERE] * 2 + vec_specs
        + [ANYWHERE] * len(wait),
        out_specs=[pl.BlockSpec(shape, lambda i: (0, 0, 0))] * 2,
        out_shape=[jax.ShapeDtypeStruct(shape, BF16)] * 2,
        scratch_shapes=Parts.scratch(plan),
        cost_estimate=cost(plan.flops, 16 * plan.part * plan.sensors * plan.sources),
        compiler_params=pltpu.CompilerParams(vmem_limit_bytes=PRODUCT_BYTES),
        name="forward",
    )(meta, whole, far, *vectors, *wait)


def adjoint_call(plan, chunk, meta, whole, far, halves, last, wait=()):
    blk_of = lambda p, m: 1 - p
    n_out = 2 if last else 1

    def kernel(m, whole, far, own_ref, got_ref, *refs):
        outs, scratch = refs[len(wait):len(wait) + n_out], refs[len(wait) + n_out:]
        parts = Parts(plan, chunk, m, blk_of, ((whole, far), scratch))
        for phase in range(2):
            blk = blk_of(phase, m)
            for t in range(plan.steps):
                for i, (near_part, far_part) in enumerate(parts.get(plan, phase, t)):
                    f = t * plan.step + i
                    field = jnp.where(blk == m[2], own_ref[f], got_ref[f])
                    back = adjoint_rows(field, near_part, far_part)
                    if last:
                        outs[phase][f] = back.astype(outs[phase].dtype)
                    else:
                        outs[0][blk, f] = back.astype(BF16)

    size = (plan.part, plan.rows, 2 * plan.sensors)
    shape = (plan.part, plan.rows, plan.sources)
    if last:
        out_specs = [pl.BlockSpec(shape, lambda i: (0, 0, 0))] * 2
        out_shape = [jax.ShapeDtypeStruct(shape, BF16), jax.ShapeDtypeStruct(shape, F32)]
    else:
        out_specs = pl.BlockSpec((2,) + shape, lambda i: (0, 0, 0, 0))
        out_shape = jax.ShapeDtypeStruct((2,) + shape, BF16)
    return pl.pallas_call(
        kernel,
        grid=(1,),
        in_specs=[pl.BlockSpec(memory_space=pltpu.SMEM)] + [ANYWHERE] * 2
        + [pl.BlockSpec(size, lambda i: (0, 0, 0))] * 2 + [ANYWHERE] * len(wait),
        out_specs=out_specs,
        out_shape=out_shape,
        scratch_shapes=Parts.scratch(plan),
        cost_estimate=cost(plan.flops, 16 * plan.part * plan.sensors * plan.sources),
        compiler_params=pltpu.CompilerParams(vmem_limit_bytes=PRODUCT_BYTES),
        name="adjoint",
    )(meta, whole, far, *halves, *wait)


def split_call(plan, meta, keep, got, wait=()):
    piece, groups = plan.piece, plan.groups
    width = keep.shape[-1]

    def kernel(m, keep_ref, got_ref, *refs):
        mine_ref, *sends = refs[len(wait):]
        for d in range(groups):
            place = pl.ds(pl.multiple_of((m[3] ^ d) * piece, piece), piece)
            total = keep_ref[place].astype(F32) + got_ref[place].astype(F32)
            if d == 0:
                mine_ref[...] = total
            else:
                sends[d - 1][...] = total.astype(BF16)

    whole = pl.BlockSpec(memory_space=pltpu.VMEM)
    return pl.pallas_call(
        kernel,
        in_specs=[pl.BlockSpec(memory_space=pltpu.SMEM), whole, whole] + [ANYWHERE] * len(wait),
        out_specs=[whole] * groups,
        out_shape=[jax.ShapeDtypeStruct((piece, width), F32)]
        + [jax.ShapeDtypeStruct((piece, width), BF16)] * (groups - 1),
        cost_estimate=cost(groups * piece * width, groups * piece * width * 8),
        compiler_params=pltpu.CompilerParams(vmem_limit_bytes=KERNEL_BYTES),
        name="split",
    )(meta, keep.reshape(-1, width), got.reshape(-1, width), *wait)


def place_call(plan, meta, pieces, wait=()):
    piece, groups = plan.piece, plan.groups
    width = pieces[0].shape[-1]

    def kernel(m, *refs):
        for d in range(groups):
            place = pl.ds(pl.multiple_of((m[3] ^ d) * piece, piece), piece)
            refs[-1][place] = refs[d][...]

    whole = pl.BlockSpec(memory_space=pltpu.VMEM)
    out = pl.pallas_call(
        kernel,
        in_specs=[pl.BlockSpec(memory_space=pltpu.SMEM)] + [whole] * groups
        + [ANYWHERE] * len(wait),
        out_specs=whole,
        out_shape=jax.ShapeDtypeStruct((groups * piece, width), BF16),
        cost_estimate=cost(0, groups * piece * width * 4),
        compiler_params=pltpu.CompilerParams(vmem_limit_bytes=KERNEL_BYTES),
        name="place",
    )(meta, *pieces, *wait)
    return out.reshape(plan.part, plan.rows, width)


def ordered(array, *earlier):
    def kernel(*refs):
        del refs

    return pl.pallas_call(
        kernel,
        in_specs=[ANYWHERE] * (1 + len(earlier)),
        out_specs=ANYWHERE,
        out_shape=jax.ShapeDtypeStruct(array.shape, array.dtype),
        input_output_aliases={0: 0},
        cost_estimate=cost(0, 0),
        compiler_params=pltpu.CompilerParams(vmem_limit_bytes=KERNEL_BYTES),
        name="ordered",
    )(array, *earlier)


def lanes(array):
    total = jnp.sum(array.reshape(-1, 8, array.shape[-1]), axis=0)
    return sum(total[:, i:i + 128] for i in range(0, array.shape[-1], 128))


def sensor_call(
    plan, chunk, meta, weights, pieces, norms, alpha=None, damping=None, old=None, wait=()
):
    piece, rows, groups = plan.piece, plan.rows, plan.groups
    width = pieces[0].shape[-1]
    count = max(1, piece // rows)
    high = piece // count
    second = old is not None

    def kernel(m, *refs):
        if second:
            alpha_ref, damp_ref, old_ref, *refs = refs
        weights_ref, norms_ref, *refs = refs
        ins, (out_ref, *more) = refs[:groups], refs[groups + len(wait):]
        stats_ref = more[-1]
        square = cross = jnp.zeros((8, 128), F32)
        for c in range(count):
            at = pl.ds(c * high, high)
            freq = chunk * plan.part + (m[3] * piece + c * high) // rows
            field = ins[0][at]
            for ref in ins[1:]:
                field = field + ref[at].astype(F32)
            if second:
                factor = 1.0 - alpha_ref[0] * damp_ref[freq]
                field = factor * old_ref[at] - alpha_ref[0] * field
            scaled = weights_ref[pl.ds(freq, 1)] * field
            out_ref[at] = scaled.astype(BF16)
            square = square + lanes(scaled * field)
            if second:
                cross = cross + lanes(scaled * old_ref[at])
            else:
                more[0][at] = field
        stats_ref[0:8] = norms_ref[0:8]
        stats_ref[8:16] = norms_ref[8:16] + square
        stats_ref[16:24] = norms_ref[16:24] + cross

    whole = pl.BlockSpec(memory_space=pltpu.VMEM)
    scalars = pl.BlockSpec(memory_space=pltpu.SMEM)
    first_out = [] if second else [jax.ShapeDtypeStruct((piece, width), F32)]
    extra = (alpha, damping, old) if second else ()
    out_shape = [jax.ShapeDtypeStruct((piece, width), BF16)] + first_out
    out_shape = out_shape + [jax.ShapeDtypeStruct((24, 128), F32)]
    return pl.pallas_call(
        kernel,
        in_specs=[scalars] + ([scalars] * 2 + [whole] if second else []) + [whole] * (2 + groups)
        + [ANYWHERE] * len(wait),
        out_specs=[whole] * len(out_shape),
        out_shape=out_shape,
        cost_estimate=cost(8 * piece * width, 16 * piece * width),
        compiler_params=pltpu.CompilerParams(vmem_limit_bytes=KERNEL_BYTES),
        name="sensor",
    )(meta, *extra, weights, norms, *pieces, *wait)


def norms_call(plan, chunk, damping, start):
    block = (plan.part, plan.rows, plan.sources)

    def kernel(damp_ref, start_ref, stats_ref):
        plain = damped = jnp.zeros((8, 128), F32)
        for f in range(plan.part):
            term = lanes(start_ref[f] * start_ref[f])
            plain = plain + term
            damped = damped + damp_ref[chunk * plan.part + f] * term
        stats_ref[0:8] = plain
        stats_ref[8:16] = damped
        stats_ref[16:24] = jnp.zeros((8, 128), F32)

    return pl.pallas_call(
        kernel,
        grid=(1,),
        in_specs=[
            pl.BlockSpec(memory_space=pltpu.SMEM),
            pl.BlockSpec(block, lambda i: (chunk, 0, 0)),
        ],
        out_specs=pl.BlockSpec((24, 128), lambda i: (0, 0)),
        out_shape=jax.ShapeDtypeStruct((24, 128), F32),
        cost_estimate=cost(2 * start.size, 4 * start.size),
        compiler_params=pltpu.CompilerParams(vmem_limit_bytes=KERNEL_BYTES),
        name="norms",
    )(damping, start)


def residual_call(plan, chunk, alpha, damping, start, mine, got):
    part, rows, sources = plan.part, plan.rows, plan.sources

    def kernel(alpha_ref, damp_ref, start_ref, mine_ref, got_ref, image_ref, out_ref, stats_ref):
        plain = damped = mixed = jnp.zeros((8, 128), F32)
        for f in range(part):
            damp = damp_ref[chunk * part + f]
            begin = start_ref[f]
            image = mine_ref[f].astype(F32) + got_ref[f].astype(F32) + damp * begin
            residual = begin - alpha_ref[0] * image
            image_ref[f] = image
            out_ref[f] = residual
            term = lanes(residual * residual)
            plain = plain + term
            damped = damped + damp * term
            mixed = mixed + damp * lanes(residual * begin)
        stats_ref[0:8] = plain
        stats_ref[8:16] = damped
        stats_ref[16:24] = mixed

    block = (part, rows, sources)
    scalars = pl.BlockSpec(memory_space=pltpu.SMEM)
    out = jax.ShapeDtypeStruct(block, F32)
    return pl.pallas_call(
        kernel,
        grid=(1,),
        in_specs=[
            scalars,
            scalars,
            pl.BlockSpec(block, lambda i: (chunk, 0, 0)),
            pl.BlockSpec((None,) + block, lambda i: (0, 0, 0, 0)),
            pl.BlockSpec((None,) + block, lambda i: (1, 0, 0, 0)),
        ],
        out_specs=[
            pl.BlockSpec(block, lambda i: (0, 0, 0)),
            pl.BlockSpec(block, lambda i: (0, 0, 0)),
            pl.BlockSpec((24, 128), lambda i: (0, 0)),
        ],
        out_shape=[out, out, jax.ShapeDtypeStruct((24, 128), F32)],
        cost_estimate=cost(8 * part * rows * sources, 16 * part * rows * sources),
        compiler_params=pltpu.CompilerParams(vmem_limit_bytes=KERNEL_BYTES),
        name="residual",
    )(alpha, damping, start, mine, got)


def body(n_sens, n_src, operator, right_side, noise_weights, damping):
    plan = Plan(operator, right_side, n_sens, n_src, CHUNKS)
    sens, src = lax.axis_index("sens"), lax.axis_index("src")
    pair, core, half, group = sens // 2, sens % 2, src % 2, src // 2
    meta = jnp.stack([pair, core, half, group]).astype(jnp.int32)
    part, rows, block = plan.part, plan.rows, plan.block
    levels = range(n_src.bit_length() - 1)
    chunks = range(plan.chunks)

    def to_core(array):
        return lax.ppermute(array, "sens", [(i, i ^ 1) for i in range(n_sens)])

    def to_pair(array):
        return lax.ppermute(array, "sens", [(i, i ^ 2) for i in range(n_sens)])

    def to_src(array, step):
        return lax.ppermute(array, "src", [(j, j ^ step) for j in range(n_src)])

    def in_turn(arrays, move):
        moved = []
        for k, array in enumerate(arrays):
            if k > 0:
                array = arrays[k] = ordered(array, moved[-1])
            moved.append(move(array))
        return moved

    def total_near(sums):
        sums = sums + to_core(sums)
        sums = sums + to_pair(sums)
        return sums + to_src(sums, 1)

    def total_far(sums):
        for level in levels[1:]:
            sums = sums + to_src(sums, 1 << level)
        return sums, jnp.sum(sums.reshape(-1, 8 * 128), axis=1)

    def double(table, level):
        other = to_src(table, 1 << level)
        low = (src >> level) % 2 == 0
        return jnp.concatenate([jnp.where(low, table, other), jnp.where(low, other, table)], axis=0)

    whole = operator.reshape(plan.pairs, 2, block * 2 * plan.sensors, plan.sources)
    start = right_side.reshape(block, rows, plan.sources)

    casts = [cast_call(plan, k, start) for k in chunks]
    cuts = [cut_call(plan, k, meta, whole, (casts[0],)) for k in chunks]
    got_b = in_turn(list(casts), to_pair)
    weights = noise_weights
    for level in levels[:2]:
        weights = double(weights, level)
    far, pairs = [to_core(cut) for cut in cuts], []
    for k in chunks:
        wait = tuple(casts[1:]) + tuple(cuts[1:]) + (weights,) if k == 0 else ()
        pairs.append(forward_call(plan, k, meta, whole, far[k], True, (start, got_b[k]), wait))

    for level in levels[2:]:
        weights = double(weights, level)
    weights = weights.reshape(plan.pairs, 2, block, plan.sensors)
    weights_near = lax.dynamic_index_in_dim(weights, core, 1, keepdims=False)
    weights_far = to_core(lax.dynamic_index_in_dim(weights, 1 - core, 1, keepdims=False))
    weights = jnp.concatenate([weights_near, weights_far], axis=-1)
    weights = lax.dynamic_index_in_dim(weights, pair ^ half, 0, keepdims=False)
    damping_row = jnp.where(half == 0, damping, to_pair(damping))
    steps = [2 * d for d in range(1, plan.groups)]

    def reduce_field(keep, got, wait=()):
        mine, *sends = split_call(plan, meta, keep, got, wait)
        return [mine] + [to_src(piece, step) for piece, step in zip(sends, steps)]

    def to_half(array):
        return to_src(array, 1)

    def both_products(scaled, near_sums, last, then, received):
        outs, wait, sums = [], (), None
        for k in chunks:
            pieces = [scaled[k]] + [to_src(scaled[k], step) for step in steps]
            own = place_call(plan, meta, pieces, wait + tuple(sum(received[k + 1:k + 2], [])))
            halves = (own, to_half(own))
            if k == 1:
                after = outs[0][1][0]
                far_sums, sums = total_far(near_sums if last else ordered(near_sums, after))
                wait = (after, far_sums)
            out = adjoint_call(plan, k, meta, whole, far[k], halves, last, wait if k > 0 else ())
            outs.append((out, then(k, out)))
            wait = (out[0] if last else out, near_sums)
        return outs, total_far(near_sums)[1] if sums is None else sums

    sends = [send for send, _ in pairs]
    got = in_turn(sends, to_half)
    pieces = [reduce_field(pairs[k][1], got[k], tuple(sends[k + 1:k + 2])) for k in chunks]
    scaled, field, stats = zip(*[
        sensor_call(
            plan, k, meta, weights, pieces[k], norms_call(plan, k, damping, start),
            wait=tuple(got[k + 1:k + 2]),
        )
        for k in chunks
    ])
    near_0 = total_near(sum(stats))

    def go_on(k, back):
        got = to_pair(back)
        send, keep = forward_call(plan, k, meta, whole, far[k], False, (back, got))
        return send, keep, got

    outs, sums = both_products(scaled, near_0, False, go_on, [each[1:] for each in pieces])
    norm_0, curve_0 = sums[0], sums[1]
    alpha_0 = (norm_0 / curve_0)[None]
    back = [out for out, _ in outs]
    sends, keeps, got_back = zip(*[rest for _, rest in outs])
    got = in_turn(list(sends), to_half)
    image_0, residual, norms = zip(*[
        residual_call(plan, k, alpha_0, damping, start, back[k], got_back[k]) for k in chunks
    ])
    pieces = [reduce_field(keeps[k], got[k]) for k in chunks]
    scaled, stats = zip(*[
        sensor_call(plan, k, meta, weights, pieces[k], norms[k], alpha_0, damping_row, field[k])
        for k in chunks
    ])
    near_1 = total_near(sum(stats))
    outs, sums = both_products(scaled, near_1, True, lambda k, out: (to_pair(out[0]),), [each[1:] for each in pieces])
    norm_1 = sums[0]
    beta = norm_1 / norm_0
    curve_1 = sums[1] + 2.0 * beta * sums[2] + beta * beta * curve_0
    alpha_1 = norm_1 / curve_1

    final = [out[1] + rest[0].astype(F32) for out, rest in outs]
    residual, image_0 = jnp.concatenate(residual), jnp.concatenate(image_0)
    image_1 = jnp.concatenate(final) + damping[:, None, None] * residual + beta * image_0
    solution = alpha_0 * start + alpha_1 * (residual + beta * start)
    residual = residual - alpha_1 * image_1
    return solution.reshape(right_side.shape), residual.reshape(right_side.shape)


def solution(mesh):
    in_specs = (
        P(None, None, "sens", "src"),
        P("sens", None, None, "src"),
        P("src", "sens"),
        P("sens"),
    )
    out_specs = (P("sens", None, None, "src"), P("sens", None, None, "src"))
    shard = functools.partial(body, mesh.shape["sens"], mesh.shape["src"])
    return jax.shard_map(shard, mesh=mesh, in_specs=in_specs, out_specs=out_specs, check_vma=False)
```

```python
import functools

import jax
import jax.numpy as jnp
from jax import lax
from jax.experimental import pallas as pl
from jax.experimental.pallas import tpu as pltpu
from jax.sharding import PartitionSpec as P

CHUNKS = 2
KERNEL_BYTES = 16 * 2 ** 20
PRODUCT_BYTES = 56 * 2 ** 20
F32 = jnp.float32
BF16 = jnp.bfloat16
ANYWHERE = pl.BlockSpec(memory_space=pl.ANY)
NT = (((1,), (1,)), ((), ()))
NN = (((1,), (0,)), ((), ()))


def largest_divisor(extent, most):
    return next(size for size in range(min(extent, most), 0, -1) if extent % size == 0)


def turned(block, sign):
    half = block.shape[0] // 2
    upper, lower = block[:half], block[half:]
    return jnp.concatenate([-lower, upper] if sign < 0 else [lower, -upper], axis=0)


def forward_rows(vector, near, far):
    left = jnp.concatenate([vector, turned(vector, -1)], axis=1)
    right = jnp.concatenate(
        [jnp.concatenate([part[0], part[1]], axis=1) for part in (near, far)], axis=0
    )
    return lax.dot_general(left, right, NT, preferred_element_type=F32)


def adjoint_rows(field, near, far):
    sensors = near[0].shape[0]
    total = None
    for part, piece in ((near, field[:, :sensors]), (far, field[:, sensors:])):
        left = jnp.concatenate([piece, turned(piece, 1)], axis=1)
        right = jnp.concatenate(part, axis=0)
        term = lax.dot_general(left, right, NN, preferred_element_type=F32)
        total = term if total is None else total + term
    return total


def cost(flops, moved):
    return pl.CostEstimate(flops=flops // 1000, bytes_accessed=moved // 1000, transcendentals=0)


class Plan:
    def __init__(self, operator, right_side, n_sens, n_src, chunks):
        self.freqs, _, self.sensors, self.sources = operator.shape
        self.block = right_side.shape[0]
        self.rows = right_side.shape[1] * right_side.shape[2]
        self.pairs = n_sens // 2
        self.groups = n_src // 2
        self.chunks = chunks
        self.part = self.block // chunks
        self.step = largest_divisor(self.part, 8)
        self.steps = self.part // self.step
        self.flops = 16 * self.part * self.rows * self.sensors * self.sources * 2
        self.piece = self.part * self.rows // self.groups


class Parts:
    def __init__(self, plan, chunk, m, blk_of, refs):
        (whole, far), (near_buf, far_buf, sems) = refs
        self.buffers, self.copies = (near_buf, far_buf), {}
        high = plan.step * 2 * plan.sensors
        for phase in range(2):
            for t in range(plan.steps):
                slot = phase * plan.steps + t
                side = m[0] ^ blk_of(phase, m)
                near_rows = pl.ds((chunk * plan.steps + t) * high, high)
                self.copies[phase, t] = [
                    pltpu.make_async_copy(ref, buffer.at[slot], sems.at[slot, place])
                    for place, (ref, buffer) in enumerate((
                        (whole.at[side, m[1], near_rows], near_buf),
                        (far.at[side, pl.ds(t * high, high)], far_buf),
                    ))
                ]
        for copies in self.copies.values():
            for copy in copies:
                copy.start()

    def get(self, plan, phase, t):
        for copy in self.copies[phase, t]:
            copy.wait()
        slot, high = phase * plan.steps + t, plan.sensors
        return [
            tuple(
                tuple(buffer[slot, pl.ds((2 * f + c) * high, high)] for c in range(2))
                for buffer in self.buffers
            )
            for f in range(plan.step)
        ]

    @staticmethod
    def scratch(plan):
        buffer = pltpu.VMEM((2 * plan.steps, plan.step * 2 * plan.sensors, plan.sources), BF16)
        return [buffer, buffer, pltpu.SemaphoreType.DMA((2 * plan.steps, 2))]


def cut_call(plan, chunk, meta, whole, wait=()):
    def kernel(m, whole_ref, *refs):
        out_ref, buffer, sems = refs[len(wait):]
        high = plan.step * 2 * plan.sensors
        slots = [(side, t) for side in range(plan.pairs) for t in range(plan.steps)]
        ins, outs = [], []
        for slot, (side, t) in enumerate(slots):
            rows = pl.ds((chunk * plan.steps + t) * high, high)
            ins.append(pltpu.make_async_copy(
                whole_ref.at[side, 1 - m[1], rows], buffer.at[slot], sems.at[0, slot]
            ))
            outs.append(pltpu.make_async_copy(
                buffer.at[slot], out_ref.at[side, pl.ds(t * high, high)], sems.at[1, slot]
            ))
        for copy in ins:
            copy.start()
        for slot in range(len(slots)):
            ins[slot].wait()
            outs[slot].start()
        for copy in outs:
            copy.wait()

    shape = (plan.pairs, plan.part * 2 * plan.sensors, plan.sources)
    return pl.pallas_call(
        kernel,
        in_specs=[pl.BlockSpec(memory_space=pltpu.SMEM), ANYWHERE] + [ANYWHERE] * len(wait),
        out_specs=ANYWHERE,
        out_shape=jax.ShapeDtypeStruct(shape, BF16),
        scratch_shapes=[
            pltpu.VMEM((plan.pairs * plan.steps, shape[1] // plan.steps, plan.sources), BF16),
            pltpu.SemaphoreType.DMA((2, plan.pairs * plan.steps)),
        ],
        cost_estimate=cost(0, 8 * plan.part * plan.sensors * plan.sources),
        compiler_params=pltpu.CompilerParams(vmem_limit_bytes=PRODUCT_BYTES),
        name="cut",
    )(meta, whole, *wait)


def cast_call(plan, chunk, start, wait=()):
    shape = (plan.part, plan.rows, plan.sources)

    def kernel(start_ref, *refs):
        out_ref, buffer, sem = refs[len(wait):]
        rows = pl.ds(chunk * plan.part, plan.part)
        copy = pltpu.make_async_copy(start_ref.at[rows], buffer, sem)
        copy.start()
        copy.wait()
        out_ref[...] = buffer[...].astype(BF16)

    return pl.pallas_call(
        kernel,
        in_specs=[ANYWHERE] + [ANYWHERE] * len(wait),
        out_specs=pl.BlockSpec(memory_space=pltpu.VMEM),
        out_shape=jax.ShapeDtypeStruct(shape, BF16),
        scratch_shapes=[pltpu.VMEM(shape, F32), pltpu.SemaphoreType.DMA(())],
        cost_estimate=cost(0, 6 * plan.part * plan.rows * plan.sources),
        compiler_params=pltpu.CompilerParams(vmem_limit_bytes=KERNEL_BYTES),
        name="cast",
    )(start, *wait)


def forward_call(plan, chunk, meta, whole, far, first, vectors, wait=()):
    blk_of = lambda p, m: 1 - (m[2] ^ p)

    def kernel(m, whole, far, one_ref, two_ref, *refs):
        outs, scratch = refs[len(wait):len(wait) + 2], refs[len(wait) + 2:]
        parts = Parts(plan, chunk, m, blk_of, ((whole, far), scratch))
        for phase in range(2):
            blk = blk_of(phase, m)
            for t in range(plan.steps):
                for i, (near_part, far_part) in enumerate(parts.get(plan, phase, t)):
                    f = t * plan.step + i
                    if first:
                        vector = jnp.where(blk == 0, one_ref[f].astype(BF16), two_ref[f])
                    else:
                        vector = one_ref[blk, f].astype(F32) + two_ref[1 - blk, f].astype(F32)
                    outs[phase][f] = forward_rows(vector.astype(BF16), near_part, far_part).astype(BF16)

    size = (plan.part, plan.rows, plan.sources)
    if first:
        vec_specs = [
            pl.BlockSpec(size, lambda i: (chunk, 0, 0)),
            pl.BlockSpec(size, lambda i: (0, 0, 0)),
        ]
    else:
        vec_specs = [pl.BlockSpec((2,) + size, lambda i: (0, 0, 0, 0))] * 2
    shape = (plan.part, plan.rows, 2 * plan.sensors)
    return pl.pallas_call(
        kernel,
        grid=(1,),
        in_specs=[pl.BlockSpec(memory_space=pltpu.SMEM)] + [ANYWHERE] * 2 + vec_specs
        + [ANYWHERE] * len(wait),
        out_specs=[pl.BlockSpec(shape, lambda i: (0, 0, 0))] * 2,
        out_shape=[jax.ShapeDtypeStruct(shape, BF16)] * 2,
        scratch_shapes=Parts.scratch(plan),
        cost_estimate=cost(plan.flops, 16 * plan.part * plan.sensors * plan.sources),
        compiler_params=pltpu.CompilerParams(vmem_limit_bytes=PRODUCT_BYTES),
        name="forward",
    )(meta, whole, far, *vectors, *wait)


def adjoint_call(plan, chunk, meta, whole, far, halves, last, wait=()):
    blk_of = lambda p, m: 1 - p
    n_out = 2 if last else 1

    def kernel(m, whole, far, own_ref, got_ref, *refs):
        outs, scratch = refs[len(wait):len(wait) + n_out], refs[len(wait) + n_out:]
        parts = Parts(plan, chunk, m, blk_of, ((whole, far), scratch))
        for phase in range(2):
            blk = blk_of(phase, m)
            for t in range(plan.steps):
                for i, (near_part, far_part) in enumerate(parts.get(plan, phase, t)):
                    f = t * plan.step + i
                    field = jnp.where(blk == m[2], own_ref[f], got_ref[f])
                    back = adjoint_rows(field, near_part, far_part)
                    if last:
                        outs[phase][f] = back.astype(outs[phase].dtype)
                    else:
                        outs[0][blk, f] = back.astype(BF16)

    size = (plan.part, plan.rows, 2 * plan.sensors)
    shape = (plan.part, plan.rows, plan.sources)
    if last:
        out_specs = [pl.BlockSpec(shape, lambda i: (0, 0, 0))] * 2
        out_shape = [jax.ShapeDtypeStruct(shape, BF16), jax.ShapeDtypeStruct(shape, F32)]
    else:
        out_specs = pl.BlockSpec((2,) + shape, lambda i: (0, 0, 0, 0))
        out_shape = jax.ShapeDtypeStruct((2,) + shape, BF16)
    return pl.pallas_call(
        kernel,
        grid=(1,),
        in_specs=[pl.BlockSpec(memory_space=pltpu.SMEM)] + [ANYWHERE] * 2
        + [pl.BlockSpec(size, lambda i: (0, 0, 0))] * 2 + [ANYWHERE] * len(wait),
        out_specs=out_specs,
        out_shape=out_shape,
        scratch_shapes=Parts.scratch(plan),
        cost_estimate=cost(plan.flops, 16 * plan.part * plan.sensors * plan.sources),
        compiler_params=pltpu.CompilerParams(vmem_limit_bytes=PRODUCT_BYTES),
        name="adjoint",
    )(meta, whole, far, *halves, *wait)


def split_call(plan, meta, keep, got, wait=()):
    piece, groups = plan.piece, plan.groups
    width = keep.shape[-1]

    def kernel(m, keep_ref, got_ref, *refs):
        mine_ref, *sends = refs[len(wait):]
        for d in range(groups):
            place = pl.ds(pl.multiple_of((m[3] ^ d) * piece, piece), piece)
            total = keep_ref[place].astype(F32) + got_ref[place].astype(F32)
            if d == 0:
                mine_ref[...] = total
            else:
                sends[d - 1][...] = total.astype(BF16)

    whole = pl.BlockSpec(memory_space=pltpu.VMEM)
    return pl.pallas_call(
        kernel,
        in_specs=[pl.BlockSpec(memory_space=pltpu.SMEM), whole, whole] + [ANYWHERE] * len(wait),
        out_specs=[whole] * groups,
        out_shape=[jax.ShapeDtypeStruct((piece, width), F32)]
        + [jax.ShapeDtypeStruct((piece, width), BF16)] * (groups - 1),
        cost_estimate=cost(groups * piece * width, groups * piece * width * 8),
        compiler_params=pltpu.CompilerParams(vmem_limit_bytes=KERNEL_BYTES),
        name="split",
    )(meta, keep.reshape(-1, width), got.reshape(-1, width), *wait)


def place_call(plan, meta, pieces, wait=()):
    piece, groups = plan.piece, plan.groups
    width = pieces[0].shape[-1]

    def kernel(m, *refs):
        for d in range(groups):
            place = pl.ds(pl.multiple_of((m[3] ^ d) * piece, piece), piece)
            refs[-1][place] = refs[d][...]

    whole = pl.BlockSpec(memory_space=pltpu.VMEM)
    out = pl.pallas_call(
        kernel,
        in_specs=[pl.BlockSpec(memory_space=pltpu.SMEM)] + [whole] * groups
        + [ANYWHERE] * len(wait),
        out_specs=whole,
        out_shape=jax.ShapeDtypeStruct((groups * piece, width), BF16),
        cost_estimate=cost(0, groups * piece * width * 4),
        compiler_params=pltpu.CompilerParams(vmem_limit_bytes=KERNEL_BYTES),
        name="place",
    )(meta, *pieces, *wait)
    return out.reshape(plan.part, plan.rows, width)


def ordered(array, *earlier):
    def kernel(*refs):
        del refs

    return pl.pallas_call(
        kernel,
        in_specs=[ANYWHERE] * (1 + len(earlier)),
        out_specs=ANYWHERE,
        out_shape=jax.ShapeDtypeStruct(array.shape, array.dtype),
        input_output_aliases={0: 0},
        cost_estimate=cost(0, 0),
        compiler_params=pltpu.CompilerParams(vmem_limit_bytes=KERNEL_BYTES),
        name="ordered",
    )(array, *earlier)


def lanes(array):
    total = jnp.sum(array.reshape(-1, 8, array.shape[-1]), axis=0)
    return sum(total[:, i:i + 128] for i in range(0, array.shape[-1], 128))


def sensor_call(
    plan, chunk, meta, weights, pieces, norms, alpha=None, damping=None, old=None, wait=()
):
    piece, rows, groups = plan.piece, plan.rows, plan.groups
    width = pieces[0].shape[-1]
    count = max(1, piece // rows)
    high = piece // count
    second = old is not None

    def kernel(m, *refs):
        if second:
            alpha_ref, damp_ref, old_ref, *refs = refs
        weights_ref, norms_ref, *refs = refs
        ins, (out_ref, *more) = refs[:groups], refs[groups + len(wait):]
        stats_ref = more[-1]
        square = cross = jnp.zeros((8, 128), F32)
        for c in range(count):
            at = pl.ds(c * high, high)
            freq = chunk * plan.part + (m[3] * piece + c * high) // rows
            field = ins[0][at]
            for ref in ins[1:]:
                field = field + ref[at].astype(F32)
            if second:
                factor = 1.0 - alpha_ref[0] * damp_ref[freq]
                field = factor * old_ref[at] - alpha_ref[0] * field
            scaled = weights_ref[pl.ds(freq, 1)] * field
            out_ref[at] = scaled.astype(BF16)
            square = square + lanes(scaled * field)
            if second:
                cross = cross + lanes(scaled * old_ref[at])
            else:
                more[0][at] = field
        stats_ref[0:8] = norms_ref[0:8]
        stats_ref[8:16] = norms_ref[8:16] + square
        stats_ref[16:24] = norms_ref[16:24] + cross

    whole = pl.BlockSpec(memory_space=pltpu.VMEM)
    scalars = pl.BlockSpec(memory_space=pltpu.SMEM)
    first_out = [] if second else [jax.ShapeDtypeStruct((piece, width), F32)]
    extra = (alpha, damping, old) if second else ()
    out_shape = [jax.ShapeDtypeStruct((piece, width), BF16)] + first_out
    out_shape = out_shape + [jax.ShapeDtypeStruct((24, 128), F32)]
    return pl.pallas_call(
        kernel,
        in_specs=[scalars] + ([scalars] * 2 + [whole] if second else []) + [whole] * (2 + groups)
        + [ANYWHERE] * len(wait),
        out_specs=[whole] * len(out_shape),
        out_shape=out_shape,
        cost_estimate=cost(8 * piece * width, 16 * piece * width),
        compiler_params=pltpu.CompilerParams(vmem_limit_bytes=KERNEL_BYTES),
        name="sensor",
    )(meta, *extra, weights, norms, *pieces, *wait)


def norms_call(plan, chunk, damping, start):
    block = (plan.part, plan.rows, plan.sources)

    def kernel(damp_ref, start_ref, stats_ref):
        plain = damped = jnp.zeros((8, 128), F32)
        for f in range(plan.part):
            term = lanes(start_ref[f] * start_ref[f])
            plain = plain + term
            damped = damped + damp_ref[chunk * plan.part + f] * term
        stats_ref[0:8] = plain
        stats_ref[8:16] = damped
        stats_ref[16:24] = jnp.zeros((8, 128), F32)

    return pl.pallas_call(
        kernel,
        grid=(1,),
        in_specs=[
            pl.BlockSpec(memory_space=pltpu.SMEM),
            pl.BlockSpec(block, lambda i: (chunk, 0, 0)),
        ],
        out_specs=pl.BlockSpec((24, 128), lambda i: (0, 0)),
        out_shape=jax.ShapeDtypeStruct((24, 128), F32),
        cost_estimate=cost(2 * start.size, 4 * start.size),
        compiler_params=pltpu.CompilerParams(vmem_limit_bytes=KERNEL_BYTES),
        name="norms",
    )(damping, start)


def residual_call(plan, chunk, alpha, damping, start, mine, got):
    part, rows, sources = plan.part, plan.rows, plan.sources

    def kernel(alpha_ref, damp_ref, start_ref, mine_ref, got_ref, image_ref, out_ref, stats_ref):
        plain = damped = mixed = jnp.zeros((8, 128), F32)
        for f in range(part):
            damp = damp_ref[chunk * part + f]
            begin = start_ref[f]
            image = mine_ref[f].astype(F32) + got_ref[f].astype(F32) + damp * begin
            residual = begin - alpha_ref[0] * image
            image_ref[f] = image
            out_ref[f] = residual
            term = lanes(residual * residual)
            plain = plain + term
            damped = damped + damp * term
            mixed = mixed + damp * lanes(residual * begin)
        stats_ref[0:8] = plain
        stats_ref[8:16] = damped
        stats_ref[16:24] = mixed

    block = (part, rows, sources)
    scalars = pl.BlockSpec(memory_space=pltpu.SMEM)
    out = jax.ShapeDtypeStruct(block, F32)
    return pl.pallas_call(
        kernel,
        grid=(1,),
        in_specs=[
            scalars,
            scalars,
            pl.BlockSpec(block, lambda i: (chunk, 0, 0)),
            pl.BlockSpec((None,) + block, lambda i: (0, 0, 0, 0)),
            pl.BlockSpec((None,) + block, lambda i: (1, 0, 0, 0)),
        ],
        out_specs=[
            pl.BlockSpec(block, lambda i: (0, 0, 0)),
            pl.BlockSpec(block, lambda i: (0, 0, 0)),
            pl.BlockSpec((24, 128), lambda i: (0, 0)),
        ],
        out_shape=[out, out, jax.ShapeDtypeStruct((24, 128), F32)],
        cost_estimate=cost(8 * part * rows * sources, 16 * part * rows * sources),
        compiler_params=pltpu.CompilerParams(vmem_limit_bytes=KERNEL_BYTES),
        name="residual",
    )(alpha, damping, start, mine, got)


def update_call(plan, chunk, scalars, damping, start, residual, image, mine, got, outs):
    block = (plan.part, plan.rows, plan.sources)

    def kernel(scalars_ref, damp_ref, start_ref, residual_ref, image_ref, mine_ref, got_ref, *refs):
        solution_ref, out_ref = refs[len(outs):]
        alpha_0, alpha_1, beta = scalars_ref[0], scalars_ref[1], scalars_ref[2]
        for f in range(plan.part):
            begin, rest = start_ref[f], residual_ref[f]
            second = mine_ref[f] + got_ref[f].astype(F32) + damp_ref[chunk * plan.part + f] * rest
            second = second + beta * image_ref[f]
            solution_ref[f] = alpha_0 * begin + alpha_1 * (rest + beta * begin)
            out_ref[f] = rest - alpha_1 * second

    here = pl.BlockSpec(block, lambda i: (chunk, 0, 0))
    alone = pl.BlockSpec(block, lambda i: (0, 0, 0))
    values = pl.BlockSpec(memory_space=pltpu.SMEM)
    return pl.pallas_call(
        kernel,
        grid=(1,),
        in_specs=[values, values, here, alone, alone, alone, alone] + [ANYWHERE] * len(outs),
        out_specs=[here, here],
        out_shape=[jax.ShapeDtypeStruct(start.shape, F32)] * 2,
        input_output_aliases={7 + i: i for i in range(len(outs))},
        cost_estimate=cost(8 * start.size, 16 * start.size),
        compiler_params=pltpu.CompilerParams(vmem_limit_bytes=KERNEL_BYTES),
        name="update",
    )(scalars, damping, start, residual, image, mine, got, *outs)


def body(n_sens, n_src, operator, right_side, noise_weights, damping):
    plan = Plan(operator, right_side, n_sens, n_src, CHUNKS)
    sens, src = lax.axis_index("sens"), lax.axis_index("src")
    pair, core, half, group = sens // 2, sens % 2, src % 2, src // 2
    meta = jnp.stack([pair, core, half, group]).astype(jnp.int32)
    part, rows, block = plan.part, plan.rows, plan.block
    levels = range(n_src.bit_length() - 1)
    chunks = range(plan.chunks)

    def to_core(array):
        return lax.ppermute(array, "sens", [(i, i ^ 1) for i in range(n_sens)])

    def to_pair(array):
        return lax.ppermute(array, "sens", [(i, i ^ 2) for i in range(n_sens)])

    def to_src(array, step):
        return lax.ppermute(array, "src", [(j, j ^ step) for j in range(n_src)])

    def in_turn(arrays, move):
        moved = []
        for k, array in enumerate(arrays):
            if k > 0:
                array = arrays[k] = ordered(array, moved[-1])
            moved.append(move(array))
        return moved

    def total_near(sums):
        sums = sums + to_core(sums)
        sums = sums + to_pair(sums)
        return sums + to_src(sums, 1)

    def total_far(sums):
        for level in levels[1:]:
            sums = sums + to_src(sums, 1 << level)
        return sums, jnp.sum(sums.reshape(-1, 8 * 128), axis=1)

    def double(table, level):
        other = to_src(table, 1 << level)
        low = (src >> level) % 2 == 0
        return jnp.concatenate([jnp.where(low, table, other), jnp.where(low, other, table)], axis=0)

    whole = operator.reshape(plan.pairs, 2, block * 2 * plan.sensors, plan.sources)
    start = right_side.reshape(block, rows, plan.sources)

    casts = [cast_call(plan, k, start) for k in chunks]
    cuts = [cut_call(plan, k, meta, whole, (casts[0],)) for k in chunks]
    got_b = in_turn(list(casts), to_pair)
    weights = noise_weights
    for level in levels[:2]:
        weights = double(weights, level)
    far, pairs = [to_core(cut) for cut in cuts], []
    for k in chunks:
        wait = tuple(casts[1:]) + tuple(cuts[1:]) + (weights,) if k == 0 else ()
        pairs.append(forward_call(plan, k, meta, whole, far[k], True, (start, got_b[k]), wait))

    for level in levels[2:]:
        weights = double(weights, level)
    weights = weights.reshape(plan.pairs, 2, block, plan.sensors)
    weights_near = lax.dynamic_index_in_dim(weights, core, 1, keepdims=False)
    weights_far = to_core(lax.dynamic_index_in_dim(weights, 1 - core, 1, keepdims=False))
    weights = jnp.concatenate([weights_near, weights_far], axis=-1)
    weights = lax.dynamic_index_in_dim(weights, pair ^ half, 0, keepdims=False)
    damping_row = jnp.where(half == 0, damping, to_pair(damping))
    steps = [2 * d for d in range(1, plan.groups)]

    def reduce_field(keep, got, wait=()):
        mine, *sends = split_call(plan, meta, keep, got, wait)
        return [mine] + [to_src(piece, step) for piece, step in zip(sends, steps)]

    def to_half(array):
        return to_src(array, 1)

    def both_products(scaled, near_sums, last, then, received):
        outs, wait, sums = [], (), None
        pieces = [[one] + [to_src(one, step) for step in steps] for one in scaled]
        for k in chunks:
            own = place_call(plan, meta, pieces[k], wait + tuple(sum(received[k + 1:k + 2], [])))
            halves = (own, to_half(own))
            if k == 0:
                wait = tuple(sum(pieces[1:2], [])) if received else ()
            if k == 1:
                far_sums, sums = total_far(near_sums)
                wait = (outs[0][1][0], far_sums)
            out = adjoint_call(plan, k, meta, whole, far[k], halves, last, wait)
            outs.append((out, then(k, out)))
            wait = (out,) if received else (out[0] if last else out, near_sums)
        return outs, total_far(near_sums)[1] if sums is None else sums

    sends = [send for send, _ in pairs]
    got = in_turn(sends, to_half)
    pieces = [reduce_field(pairs[k][1], got[k], tuple(sends[k + 1:k + 2])) for k in chunks]
    scaled, field, stats = zip(*[
        sensor_call(
            plan, k, meta, weights, pieces[k], norms_call(plan, k, damping, start),
            wait=tuple(got[k + 1:k + 2]),
        )
        for k in chunks
    ])
    near_0 = total_near(sum(stats))

    def go_on(k, back):
        got = to_pair(back)
        send, keep = forward_call(plan, k, meta, whole, far[k], False, (back, got))
        return send, keep, got

    outs, sums = both_products(scaled, near_0, False, go_on, [each[1:] for each in pieces])
    norm_0, curve_0 = sums[0], sums[1]
    alpha_0 = (norm_0 / curve_0)[None]
    back = [out for out, _ in outs]
    sends, keeps, got_back = zip(*[rest for _, rest in outs])
    got = in_turn(list(sends), to_half)
    image_0, residual, norms = zip(*[
        residual_call(plan, k, alpha_0, damping, start, back[k], got_back[k]) for k in chunks
    ])
    pieces = [reduce_field(keeps[k], got[k]) for k in chunks]
    scaled, stats = zip(*[
        sensor_call(plan, k, meta, weights, pieces[k], norms[k], alpha_0, damping_row, field[k])
        for k in chunks
    ])
    near_1 = total_near(sum(stats))
    outs, sums = both_products(scaled, near_1, True, lambda k, out: (to_pair(out[0]),), [])
    norm_1 = sums[0]
    beta = norm_1 / norm_0
    curve_1 = sums[1] + 2.0 * beta * sums[2] + beta * beta * curve_0
    alpha_1 = norm_1 / curve_1

    scalars = jnp.stack([alpha_0[0], alpha_1, beta])
    results = ()
    for k in chunks:
        (_, mine), (got,) = outs[k]
        results = update_call(
            plan, k, scalars, damping, start, residual[k], image_0[k], mine, got, results
        )
    return tuple(result.reshape(right_side.shape) for result in results)


def solution(mesh):
    in_specs = (
        P(None, None, "sens", "src"),
        P("sens", None, None, "src"),
        P("src", "sens"),
        P("sens"),
    )
    out_specs = (P("sens", None, None, "src"), P("sens", None, None, "src"))
    shard = functools.partial(body, mesh.shape["sens"], mesh.shape["src"])
    return jax.shard_map(shard, mesh=mesh, in_specs=in_specs, out_specs=out_specs, check_vma=False)
```

```python
import functools

import jax
import jax.numpy as jnp
from jax import lax
from jax.experimental import pallas as pl
from jax.experimental.pallas import tpu as pltpu
from jax.sharding import PartitionSpec as P

CHUNKS = 2
KERNEL_BYTES = 16 * 2 ** 20
PRODUCT_BYTES = 56 * 2 ** 20
F32 = jnp.float32
BF16 = jnp.bfloat16
ANYWHERE = pl.BlockSpec(memory_space=pl.ANY)
NT = (((1,), (1,)), ((), ()))
NN = (((1,), (0,)), ((), ()))


def largest_divisor(extent, most):
    return next(size for size in range(min(extent, most), 0, -1) if extent % size == 0)


def turned(block, sign):
    half = block.shape[0] // 2
    upper, lower = block[:half], block[half:]
    return jnp.concatenate([-lower, upper] if sign < 0 else [lower, -upper], axis=0)


def forward_rows(vector, near, far):
    left = jnp.concatenate([vector, turned(vector, -1)], axis=1)
    right = jnp.concatenate(
        [jnp.concatenate([part[0], part[1]], axis=1) for part in (near, far)], axis=0
    )
    return lax.dot_general(left, right, NT, preferred_element_type=F32)


def adjoint_rows(field, near, far):
    sensors = near[0].shape[0]
    total = None
    for part, piece in ((near, field[:, :sensors]), (far, field[:, sensors:])):
        left = jnp.concatenate([piece, turned(piece, 1)], axis=1)
        right = jnp.concatenate(part, axis=0)
        term = lax.dot_general(left, right, NN, preferred_element_type=F32)
        total = term if total is None else total + term
    return total


def cost(flops, moved):
    return pl.CostEstimate(flops=flops // 1000, bytes_accessed=moved // 1000, transcendentals=0)


class Plan:
    def __init__(self, operator, right_side, n_sens, n_src, chunks):
        self.freqs, _, self.sensors, self.sources = operator.shape
        self.block = right_side.shape[0]
        self.rows = right_side.shape[1] * right_side.shape[2]
        self.pairs = n_sens // 2
        self.groups = n_src // 2
        self.chunks = chunks
        self.part = self.block // chunks
        self.step = largest_divisor(self.part, 8)
        self.steps = self.part // self.step
        self.flops = 16 * self.part * self.rows * self.sensors * self.sources * 2
        self.piece = self.part * self.rows // self.groups


class Parts:
    def __init__(self, plan, chunk, m, blk_of, refs, whole):
        (near, far), (near_buf, far_buf, sems) = refs
        self.buffers, self.copies = (near_buf, far_buf), {}
        high = plan.step * 2 * plan.sensors
        for phase in range(2):
            for t in range(plan.steps):
                slot = phase * plan.steps + t
                side = m[0] ^ blk_of(phase, m)
                rows = pl.ds(t * high, high)
                near_rows = pl.ds((chunk * plan.steps + t) * high, high)
                source = near.at[side, m[1], near_rows] if whole else near.at[side, rows]
                self.copies[phase, t] = [
                    pltpu.make_async_copy(ref, buffer.at[slot], sems.at[slot, place])
                    for place, (ref, buffer) in enumerate((
                        (source, near_buf),
                        (far.at[side, rows], far_buf),
                    ))
                ]
        for copies in self.copies.values():
            for copy in copies:
                copy.start()

    def get(self, plan, phase, t):
        for copy in self.copies[phase, t]:
            copy.wait()
        slot, high = phase * plan.steps + t, plan.sensors
        return [
            tuple(
                tuple(buffer[slot, pl.ds((2 * f + c) * high, high)] for c in range(2))
                for buffer in self.buffers
            )
            for f in range(plan.step)
        ]

    @staticmethod
    def scratch(plan):
        buffer = pltpu.VMEM((2 * plan.steps, plan.step * 2 * plan.sensors, plan.sources), BF16)
        return [buffer, buffer, pltpu.SemaphoreType.DMA((2 * plan.steps, 2))]


def cut_call(plan, chunk, meta, whole, wait=()):
    def kernel(m, whole_ref, *refs):
        out_ref, buffer, sems = refs[len(wait):]
        high = plan.step * 2 * plan.sensors
        slots = [(side, t) for side in range(plan.pairs) for t in range(plan.steps)]
        ins, outs = [], []
        for slot, (side, t) in enumerate(slots):
            rows = pl.ds((chunk * plan.steps + t) * high, high)
            ins.append(pltpu.make_async_copy(
                whole_ref.at[side, 1 - m[1], rows], buffer.at[slot], sems.at[0, slot]
            ))
            outs.append(pltpu.make_async_copy(
                buffer.at[slot], out_ref.at[side, pl.ds(t * high, high)], sems.at[1, slot]
            ))
        for copy in ins:
            copy.start()
        for slot in range(len(slots)):
            ins[slot].wait()
            outs[slot].start()
        for copy in outs:
            copy.wait()

    shape = (plan.pairs, plan.part * 2 * plan.sensors, plan.sources)
    return pl.pallas_call(
        kernel,
        in_specs=[pl.BlockSpec(memory_space=pltpu.SMEM), ANYWHERE] + [ANYWHERE] * len(wait),
        out_specs=ANYWHERE,
        out_shape=jax.ShapeDtypeStruct(shape, BF16),
        scratch_shapes=[
            pltpu.VMEM((plan.pairs * plan.steps, shape[1] // plan.steps, plan.sources), BF16),
            pltpu.SemaphoreType.DMA((2, plan.pairs * plan.steps)),
        ],
        cost_estimate=cost(0, 8 * plan.part * plan.sensors * plan.sources),
        compiler_params=pltpu.CompilerParams(vmem_limit_bytes=PRODUCT_BYTES),
        name="cut",
    )(meta, whole, *wait)


def cast_call(plan, chunk, start, wait=()):
    shape = (plan.part, plan.rows, plan.sources)

    def kernel(start_ref, *refs):
        out_ref, buffer, sem = refs[len(wait):]
        rows = pl.ds(chunk * plan.part, plan.part)
        copy = pltpu.make_async_copy(start_ref.at[rows], buffer, sem)
        copy.start()
        copy.wait()
        out_ref[...] = buffer[...].astype(BF16)

    return pl.pallas_call(
        kernel,
        in_specs=[ANYWHERE] + [ANYWHERE] * len(wait),
        out_specs=pl.BlockSpec(memory_space=pltpu.VMEM),
        out_shape=jax.ShapeDtypeStruct(shape, BF16),
        scratch_shapes=[pltpu.VMEM(shape, F32), pltpu.SemaphoreType.DMA(())],
        cost_estimate=cost(0, 6 * plan.part * plan.rows * plan.sources),
        compiler_params=pltpu.CompilerParams(vmem_limit_bytes=KERNEL_BYTES),
        name="cast",
    )(start, *wait)


def forward_call(plan, chunk, meta, near, far, first, vectors, wait=()):
    n_out = 3 if first else 2
    blk_of = lambda p, m: 1 - (m[2] ^ p)

    def kernel(m, near, far, one_ref, two_ref, *refs):
        outs, scratch = refs[len(wait):len(wait) + n_out], refs[len(wait) + n_out:]
        parts = Parts(plan, chunk, m, blk_of, ((near, far), scratch[:3]), first)
        saves = []
        for phase in range(2):
            blk = blk_of(phase, m)
            for t in range(plan.steps):
                blocks = parts.get(plan, phase, t)
                if first:
                    slot, high = phase * plan.steps + t, plan.step * 2 * plan.sensors
                    saves.append(pltpu.make_async_copy(
                        scratch[0].at[slot],
                        outs[2].at[m[0] ^ blk, pl.ds(t * high, high)],
                        scratch[3].at[slot],
                    ))
                    saves[-1].start()
                for i, (near_part, far_part) in enumerate(blocks):
                    f = t * plan.step + i
                    if first:
                        vector = jnp.where(blk == 0, one_ref[f].astype(BF16), two_ref[f])
                    else:
                        vector = one_ref[blk, f].astype(F32) + two_ref[1 - blk, f].astype(F32)
                    outs[phase][f] = forward_rows(vector.astype(BF16), near_part, far_part).astype(BF16)
        for save in saves:
            save.wait()

    size = (plan.part, plan.rows, plan.sources)
    if first:
        vec_specs = [
            pl.BlockSpec(size, lambda i: (chunk, 0, 0)),
            pl.BlockSpec(size, lambda i: (0, 0, 0)),
        ]
    else:
        vec_specs = [pl.BlockSpec((2,) + size, lambda i: (0, 0, 0, 0))] * 2
    shape = (plan.part, plan.rows, 2 * plan.sensors)
    return pl.pallas_call(
        kernel,
        grid=(1,),
        in_specs=[pl.BlockSpec(memory_space=pltpu.SMEM)] + [ANYWHERE] * 2 + vec_specs
        + [ANYWHERE] * len(wait),
        out_specs=[pl.BlockSpec(shape, lambda i: (0, 0, 0))] * 2 + [ANYWHERE] * (n_out - 2),
        out_shape=[jax.ShapeDtypeStruct(shape, BF16)] * 2
        + [jax.ShapeDtypeStruct(far.shape, BF16)] * (n_out - 2),
        scratch_shapes=Parts.scratch(plan) + [pltpu.SemaphoreType.DMA((2 * plan.steps,))],
        cost_estimate=cost(plan.flops, 16 * plan.part * plan.sensors * plan.sources),
        compiler_params=pltpu.CompilerParams(vmem_limit_bytes=PRODUCT_BYTES if first else KERNEL_BYTES),
        name="forward",
    )(meta, near, far, *vectors, *wait)


def adjoint_call(plan, chunk, meta, near, far, halves, last, wait=()):
    blk_of = lambda p, m: 1 - p
    n_out = 2 if last else 1

    def kernel(m, near, far, own_ref, got_ref, *refs):
        outs, scratch = refs[len(wait):len(wait) + n_out], refs[len(wait) + n_out:]
        parts = Parts(plan, chunk, m, blk_of, ((near, far), scratch), False)
        for phase in range(2):
            blk = blk_of(phase, m)
            for t in range(plan.steps):
                for i, (near_part, far_part) in enumerate(parts.get(plan, phase, t)):
                    f = t * plan.step + i
                    field = jnp.where(blk == m[2], own_ref[f], got_ref[f])
                    back = adjoint_rows(field, near_part, far_part)
                    if last:
                        outs[phase][f] = back.astype(outs[phase].dtype)
                    else:
                        outs[0][blk, f] = back.astype(BF16)

    size = (plan.part, plan.rows, 2 * plan.sensors)
    shape = (plan.part, plan.rows, plan.sources)
    if last:
        out_specs = [pl.BlockSpec(shape, lambda i: (0, 0, 0))] * 2
        out_shape = [jax.ShapeDtypeStruct(shape, BF16), jax.ShapeDtypeStruct(shape, F32)]
    else:
        out_specs = pl.BlockSpec((2,) + shape, lambda i: (0, 0, 0, 0))
        out_shape = jax.ShapeDtypeStruct((2,) + shape, BF16)
    return pl.pallas_call(
        kernel,
        grid=(1,),
        in_specs=[pl.BlockSpec(memory_space=pltpu.SMEM)] + [ANYWHERE] * 2
        + [pl.BlockSpec(size, lambda i: (0, 0, 0))] * 2 + [ANYWHERE] * len(wait),
        out_specs=out_specs,
        out_shape=out_shape,
        scratch_shapes=Parts.scratch(plan),
        cost_estimate=cost(plan.flops, 16 * plan.part * plan.sensors * plan.sources),
        compiler_params=pltpu.CompilerParams(vmem_limit_bytes=KERNEL_BYTES),
        name="adjoint",
    )(meta, near, far, *halves, *wait)


def split_call(plan, meta, keep, got, wait=()):
    piece, groups = plan.piece, plan.groups
    width = keep.shape[-1]

    def kernel(m, keep_ref, got_ref, *refs):
        mine_ref, *sends = refs[len(wait):]
        for d in range(groups):
            place = pl.ds(pl.multiple_of((m[3] ^ d) * piece, piece), piece)
            total = keep_ref[place].astype(F32) + got_ref[place].astype(F32)
            if d == 0:
                mine_ref[...] = total
            else:
                sends[d - 1][...] = total.astype(BF16)

    whole = pl.BlockSpec(memory_space=pltpu.VMEM)
    return pl.pallas_call(
        kernel,
        in_specs=[pl.BlockSpec(memory_space=pltpu.SMEM), whole, whole] + [ANYWHERE] * len(wait),
        out_specs=[whole] * groups,
        out_shape=[jax.ShapeDtypeStruct((piece, width), F32)]
        + [jax.ShapeDtypeStruct((piece, width), BF16)] * (groups - 1),
        cost_estimate=cost(groups * piece * width, groups * piece * width * 8),
        compiler_params=pltpu.CompilerParams(vmem_limit_bytes=KERNEL_BYTES),
        name="split",
    )(meta, keep.reshape(-1, width), got.reshape(-1, width), *wait)


def place_call(plan, meta, pieces, wait=()):
    piece, groups = plan.piece, plan.groups
    width = pieces[0].shape[-1]

    def kernel(m, *refs):
        for d in range(groups):
            place = pl.ds(pl.multiple_of((m[3] ^ d) * piece, piece), piece)
            refs[-1][place] = refs[d][...]

    whole = pl.BlockSpec(memory_space=pltpu.VMEM)
    out = pl.pallas_call(
        kernel,
        in_specs=[pl.BlockSpec(memory_space=pltpu.SMEM)] + [whole] * groups
        + [ANYWHERE] * len(wait),
        out_specs=whole,
        out_shape=jax.ShapeDtypeStruct((groups * piece, width), BF16),
        cost_estimate=cost(0, groups * piece * width * 4),
        compiler_params=pltpu.CompilerParams(vmem_limit_bytes=KERNEL_BYTES),
        name="place",
    )(meta, *pieces, *wait)
    return out.reshape(plan.part, plan.rows, width)


def ordered(array, *earlier):
    def kernel(*refs):
        del refs

    return pl.pallas_call(
        kernel,
        in_specs=[ANYWHERE] * (1 + len(earlier)),
        out_specs=ANYWHERE,
        out_shape=jax.ShapeDtypeStruct(array.shape, array.dtype),
        input_output_aliases={0: 0},
        cost_estimate=cost(0, 0),
        compiler_params=pltpu.CompilerParams(vmem_limit_bytes=KERNEL_BYTES),
        name="ordered",
    )(array, *earlier)


def lanes(array):
    total = jnp.sum(array.reshape(-1, 8, array.shape[-1]), axis=0)
    return sum(total[:, i:i + 128] for i in range(0, array.shape[-1], 128))


def sensor_call(
    plan, chunk, meta, weights, pieces, norms, alpha=None, damping=None, old=None, wait=()
):
    piece, rows, groups = plan.piece, plan.rows, plan.groups
    width = pieces[0].shape[-1]
    count = max(1, piece // rows)
    high = piece // count
    second = old is not None

    def kernel(m, *refs):
        if second:
            alpha_ref, damp_ref, old_ref, *refs = refs
        weights_ref, norms_ref, *refs = refs
        ins, (out_ref, *more) = refs[:groups], refs[groups + len(wait):]
        stats_ref = more[-1]
        square = cross = jnp.zeros((8, 128), F32)
        for c in range(count):
            at = pl.ds(c * high, high)
            freq = chunk * plan.part + (m[3] * piece + c * high) // rows
            field = ins[0][at]
            for ref in ins[1:]:
                field = field + ref[at].astype(F32)
            if second:
                factor = 1.0 - alpha_ref[0] * damp_ref[freq]
                field = factor * old_ref[at] - alpha_ref[0] * field
            scaled = weights_ref[pl.ds(freq, 1)] * field
            out_ref[at] = scaled.astype(BF16)
            square = square + lanes(scaled * field)
            if second:
                cross = cross + lanes(scaled * old_ref[at])
            else:
                more[0][at] = field
        stats_ref[0:8] = norms_ref[0:8]
        stats_ref[8:16] = norms_ref[8:16] + square
        stats_ref[16:24] = norms_ref[16:24] + cross

    whole = pl.BlockSpec(memory_space=pltpu.VMEM)
    scalars = pl.BlockSpec(memory_space=pltpu.SMEM)
    first_out = [] if second else [jax.ShapeDtypeStruct((piece, width), F32)]
    extra = (alpha, damping, old) if second else ()
    out_shape = [jax.ShapeDtypeStruct((piece, width), BF16)] + first_out
    out_shape = out_shape + [jax.ShapeDtypeStruct((24, 128), F32)]
    return pl.pallas_call(
        kernel,
        in_specs=[scalars] + ([scalars] * 2 + [whole] if second else []) + [whole] * (2 + groups)
        + [ANYWHERE] * len(wait),
        out_specs=[whole] * len(out_shape),
        out_shape=out_shape,
        cost_estimate=cost(8 * piece * width, 16 * piece * width),
        compiler_params=pltpu.CompilerParams(vmem_limit_bytes=KERNEL_BYTES),
        name="sensor",
    )(meta, *extra, weights, norms, *pieces, *wait)


def norms_call(plan, chunk, damping, start):
    block = (plan.part, plan.rows, plan.sources)

    def kernel(damp_ref, start_ref, stats_ref):
        plain = damped = jnp.zeros((8, 128), F32)
        for f in range(plan.part):
            term = lanes(start_ref[f] * start_ref[f])
            plain = plain + term
            damped = damped + damp_ref[chunk * plan.part + f] * term
        stats_ref[0:8] = plain
        stats_ref[8:16] = damped
        stats_ref[16:24] = jnp.zeros((8, 128), F32)

    return pl.pallas_call(
        kernel,
        grid=(1,),
        in_specs=[
            pl.BlockSpec(memory_space=pltpu.SMEM),
            pl.BlockSpec(block, lambda i: (chunk, 0, 0)),
        ],
        out_specs=pl.BlockSpec((24, 128), lambda i: (0, 0)),
        out_shape=jax.ShapeDtypeStruct((24, 128), F32),
        cost_estimate=cost(2 * start.size, 4 * start.size),
        compiler_params=pltpu.CompilerParams(vmem_limit_bytes=KERNEL_BYTES),
        name="norms",
    )(damping, start)


def residual_call(plan, chunk, alpha, damping, start, mine, got):
    part, rows, sources = plan.part, plan.rows, plan.sources

    def kernel(alpha_ref, damp_ref, start_ref, mine_ref, got_ref, image_ref, out_ref, stats_ref):
        plain = damped = mixed = jnp.zeros((8, 128), F32)
        for f in range(part):
            damp = damp_ref[chunk * part + f]
            begin = start_ref[f]
            image = mine_ref[f].astype(F32) + got_ref[f].astype(F32) + damp * begin
            residual = begin - alpha_ref[0] * image
            image_ref[f] = image
            out_ref[f] = residual
            term = lanes(residual * residual)
            plain = plain + term
            damped = damped + damp * term
            mixed = mixed + damp * lanes(residual * begin)
        stats_ref[0:8] = plain
        stats_ref[8:16] = damped
        stats_ref[16:24] = mixed

    block = (part, rows, sources)
    scalars = pl.BlockSpec(memory_space=pltpu.SMEM)
    out = jax.ShapeDtypeStruct(block, F32)
    return pl.pallas_call(
        kernel,
        grid=(1,),
        in_specs=[
            scalars,
            scalars,
            pl.BlockSpec(block, lambda i: (chunk, 0, 0)),
            pl.BlockSpec((None,) + block, lambda i: (0, 0, 0, 0)),
            pl.BlockSpec((None,) + block, lambda i: (1, 0, 0, 0)),
        ],
        out_specs=[
            pl.BlockSpec(block, lambda i: (0, 0, 0)),
            pl.BlockSpec(block, lambda i: (0, 0, 0)),
            pl.BlockSpec((24, 128), lambda i: (0, 0)),
        ],
        out_shape=[out, out, jax.ShapeDtypeStruct((24, 128), F32)],
        cost_estimate=cost(8 * part * rows * sources, 16 * part * rows * sources),
        compiler_params=pltpu.CompilerParams(vmem_limit_bytes=KERNEL_BYTES),
        name="residual",
    )(alpha, damping, start, mine, got)


def update_call(plan, chunk, scalars, damping, start, residual, image, mine, got, outs):
    block = (plan.part, plan.rows, plan.sources)

    def kernel(scalars_ref, damp_ref, start_ref, residual_ref, image_ref, mine_ref, got_ref, *refs):
        solution_ref, out_ref = refs[len(outs):]
        alpha_0, alpha_1, beta = scalars_ref[0], scalars_ref[1], scalars_ref[2]
        for f in range(plan.part):
            begin, rest = start_ref[f], residual_ref[f]
            second = mine_ref[f] + got_ref[f].astype(F32) + damp_ref[chunk * plan.part + f] * rest
            second = second + beta * image_ref[f]
            solution_ref[f] = alpha_0 * begin + alpha_1 * (rest + beta * begin)
            out_ref[f] = rest - alpha_1 * second

    here = pl.BlockSpec(block, lambda i: (chunk, 0, 0))
    alone = pl.BlockSpec(block, lambda i: (0, 0, 0))
    values = pl.BlockSpec(memory_space=pltpu.SMEM)
    return pl.pallas_call(
        kernel,
        grid=(1,),
        in_specs=[values, values, here, alone, alone, alone, alone] + [ANYWHERE] * len(outs),
        out_specs=[here, here],
        out_shape=[jax.ShapeDtypeStruct(start.shape, F32)] * 2,
        input_output_aliases={7 + i: i for i in range(len(outs))},
        cost_estimate=cost(8 * start.size, 16 * start.size),
        compiler_params=pltpu.CompilerParams(vmem_limit_bytes=KERNEL_BYTES),
        name="update",
    )(scalars, damping, start, residual, image, mine, got, *outs)


def body(n_sens, n_src, operator, right_side, noise_weights, damping):
    plan = Plan(operator, right_side, n_sens, n_src, CHUNKS)
    sens, src = lax.axis_index("sens"), lax.axis_index("src")
    pair, core, half, group = sens // 2, sens % 2, src % 2, src // 2
    meta = jnp.stack([pair, core, half, group]).astype(jnp.int32)
    part, rows, block = plan.part, plan.rows, plan.block
    levels = range(n_src.bit_length() - 1)
    chunks = range(plan.chunks)

    def to_core(array):
        return lax.ppermute(array, "sens", [(i, i ^ 1) for i in range(n_sens)])

    def to_pair(array):
        return lax.ppermute(array, "sens", [(i, i ^ 2) for i in range(n_sens)])

    def to_src(array, step):
        return lax.ppermute(array, "src", [(j, j ^ step) for j in range(n_src)])

    def in_turn(arrays, move):
        moved = []
        for k, array in enumerate(arrays):
            if k > 0:
                array = arrays[k] = ordered(array, moved[-1])
            moved.append(move(array))
        return moved

    def total_near(sums):
        sums = sums + to_core(sums)
        sums = sums + to_pair(sums)
        return sums + to_src(sums, 1)

    def total_far(sums):
        for level in levels[1:]:
            sums = sums + to_src(sums, 1 << level)
        return sums, jnp.sum(sums.reshape(-1, 8 * 128), axis=1)

    def double(table, level):
        other = to_src(table, 1 << level)
        low = (src >> level) % 2 == 0
        return jnp.concatenate([jnp.where(low, table, other), jnp.where(low, other, table)], axis=0)

    whole = operator.reshape(plan.pairs, 2, block * 2 * plan.sensors, plan.sources)
    start = right_side.reshape(block, rows, plan.sources)

    casts = [cast_call(plan, k, start) for k in chunks]
    cuts = [cut_call(plan, k, meta, whole, (casts[0],)) for k in chunks]
    got_b = in_turn(list(casts), to_pair)
    weights = noise_weights
    for level in levels[:2]:
        weights = double(weights, level)
    far, pairs = [to_core(cut) for cut in cuts], []
    for k in chunks:
        wait = tuple(casts[1:]) + tuple(cuts[1:]) + (weights,) if k == 0 else ()
        pairs.append(forward_call(plan, k, meta, whole, far[k], True, (start, got_b[k]), wait))

    for level in levels[2:]:
        weights = double(weights, level)
    weights = weights.reshape(plan.pairs, 2, block, plan.sensors)
    weights_near = lax.dynamic_index_in_dim(weights, core, 1, keepdims=False)
    weights_far = to_core(lax.dynamic_index_in_dim(weights, 1 - core, 1, keepdims=False))
    weights = jnp.concatenate([weights_near, weights_far], axis=-1)
    weights = lax.dynamic_index_in_dim(weights, pair ^ half, 0, keepdims=False)
    damping_row = jnp.where(half == 0, damping, to_pair(damping))
    steps = [2 * d for d in range(1, plan.groups)]

    def reduce_field(keep, got, wait=()):
        mine, *sends = split_call(plan, meta, keep, got, wait)
        return [mine] + [to_src(piece, step) for piece, step in zip(sends, steps)]

    def to_half(array):
        return to_src(array, 1)

    def both_products(scaled, near_sums, last, then):
        outs, wait, sums = [], (), None
        for k in chunks:
            pieces = [scaled[k]] + [to_src(scaled[k], step) for step in steps]
            own = place_call(plan, meta, pieces, wait)
            halves = (own, to_half(own))
            if k == 1:
                after = outs[0][1][0]
                far_sums, sums = total_far(near_sums if last else ordered(near_sums, after))
                wait = (after, far_sums)
            out = adjoint_call(plan, k, meta, near[k], far[k], halves, last, wait if k > 0 else ())
            outs.append((out, then(k, out)))
            wait = (out[0] if last else out, near_sums)
        return outs, total_far(near_sums)[1] if sums is None else sums

    sends, near = [each[0] for each in pairs], [each[2] for each in pairs]
    got = in_turn(sends, to_half)
    pieces = [reduce_field(pairs[k][1], got[k], tuple(sends[k + 1:k + 2])) for k in chunks]
    scaled, field, stats = zip(*[
        sensor_call(
            plan, k, meta, weights, pieces[k], norms_call(plan, k, damping, start),
            wait=tuple(got[k + 1:k + 2]),
        )
        for k in chunks
    ])
    near_0 = total_near(sum(stats))

    def go_on(k, back):
        got = to_pair(back)
        send, keep = forward_call(plan, k, meta, near[k], far[k], False, (back, got))
        return send, keep, got

    outs, sums = both_products(scaled, near_0, False, go_on)
    norm_0, curve_0 = sums[0], sums[1]
    alpha_0 = (norm_0 / curve_0)[None]
    back = [out for out, _ in outs]
    sends, keeps, got_back = zip(*[rest for _, rest in outs])
    got = in_turn(list(sends), to_half)
    image_0, residual, norms = zip(*[
        residual_call(plan, k, alpha_0, damping, start, back[k], got_back[k]) for k in chunks
    ])
    pieces = [reduce_field(keeps[k], got[k]) for k in chunks]
    scaled, stats = zip(*[
        sensor_call(plan, k, meta, weights, pieces[k], norms[k], alpha_0, damping_row, field[k])
        for k in chunks
    ])
    near_1 = total_near(sum(stats))
    outs, sums = both_products(scaled, near_1, True, lambda k, out: (to_pair(out[0]),))
    norm_1 = sums[0]
    beta = norm_1 / norm_0
    curve_1 = sums[1] + 2.0 * beta * sums[2] + beta * beta * curve_0
    alpha_1 = norm_1 / curve_1

    scalars = jnp.stack([alpha_0[0], alpha_1, beta])
    results = ()
    for k in chunks:
        (_, mine), (got,) = outs[k]
        results = update_call(
            plan, k, scalars, damping, start, residual[k], image_0[k], mine, got, results
        )
    return tuple(result.reshape(right_side.shape) for result in results)


def solution(mesh):
    in_specs = (
        P(None, None, "sens", "src"),
        P("sens", None, None, "src"),
        P("src", "sens"),
        P("sens"),
    )
    out_specs = (P("sens", None, None, "src"), P("sens", None, None, "src"))
    shard = functools.partial(body, mesh.shape["sens"], mesh.shape["src"])
    return jax.shard_map(shard, mesh=mesh, in_specs=in_specs, out_specs=out_specs, check_vma=False)
```

```python
import functools

import jax
import jax.numpy as jnp
from jax import lax
from jax.experimental import pallas as pl
from jax.experimental.pallas import tpu as pltpu
from jax.sharding import PartitionSpec as P

CHUNKS = 2
KERNEL_BYTES = 16 * 2 ** 20
PRODUCT_BYTES = 56 * 2 ** 20
F32 = jnp.float32
BF16 = jnp.bfloat16
ANYWHERE = pl.BlockSpec(memory_space=pl.ANY)
NT = (((1,), (1,)), ((), ()))
NN = (((1,), (0,)), ((), ()))


def largest_divisor(extent, most):
    return next(size for size in range(min(extent, most), 0, -1) if extent % size == 0)


def turned(block, sign):
    half = block.shape[0] // 2
    upper, lower = block[:half], block[half:]
    return jnp.concatenate([-lower, upper] if sign < 0 else [lower, -upper], axis=0)


def forward_rows(vector, near, far):
    left = jnp.concatenate([vector, turned(vector, -1)], axis=1)
    right = jnp.concatenate(
        [jnp.concatenate([part[0], part[1]], axis=1) for part in (near, far)], axis=0
    )
    return lax.dot_general(left, right, NT, preferred_element_type=F32)


def adjoint_rows(field, near, far):
    sensors = near[0].shape[0]
    total = None
    for part, piece in ((near, field[:, :sensors]), (far, field[:, sensors:])):
        left = jnp.concatenate([piece, turned(piece, 1)], axis=1)
        right = jnp.concatenate(part, axis=0)
        term = lax.dot_general(left, right, NN, preferred_element_type=F32)
        total = term if total is None else total + term
    return total


def cost(flops, moved):
    return pl.CostEstimate(flops=flops // 1000, bytes_accessed=moved // 1000, transcendentals=0)


class Plan:
    def __init__(self, operator, right_side, n_sens, n_src, chunks):
        self.freqs, _, self.sensors, self.sources = operator.shape
        self.block = right_side.shape[0]
        self.rows = right_side.shape[1] * right_side.shape[2]
        self.pairs = n_sens // 2
        self.groups = n_src // 2
        self.chunks = chunks
        self.part = self.block // chunks
        self.step = largest_divisor(self.part, 8)
        self.steps = self.part // self.step
        self.flops = 16 * self.part * self.rows * self.sensors * self.sources * 2
        self.piece = self.part * self.rows // self.groups


class Parts:
    def __init__(self, plan, chunk, m, blk_of, refs, whole):
        (near, far), (near_buf, far_buf, sems) = refs
        self.buffers, self.copies = (near_buf, far_buf), {}
        high = plan.step * 2 * plan.sensors
        for phase in range(2):
            for t in range(plan.steps):
                slot = phase * plan.steps + t
                side = m[0] ^ blk_of(phase, m)
                rows = pl.ds(t * high, high)
                near_rows = pl.ds((chunk * plan.steps + t) * high, high)
                source = near.at[side, m[1], near_rows] if whole else near.at[side, rows]
                self.copies[phase, t] = [
                    pltpu.make_async_copy(ref, buffer.at[slot], sems.at[slot, place])
                    for place, (ref, buffer) in enumerate((
                        (source, near_buf),
                        (far.at[side, rows], far_buf),
                    ))
                ]
        for copies in self.copies.values():
            for copy in copies:
                copy.start()

    def get(self, plan, phase, t):
        for copy in self.copies[phase, t]:
            copy.wait()
        slot, high = phase * plan.steps + t, plan.sensors
        return [
            tuple(
                tuple(buffer[slot, pl.ds((2 * f + c) * high, high)] for c in range(2))
                for buffer in self.buffers
            )
            for f in range(plan.step)
        ]

    @staticmethod
    def scratch(plan):
        buffer = pltpu.VMEM((2 * plan.steps, plan.step * 2 * plan.sensors, plan.sources), BF16)
        return [buffer, buffer, pltpu.SemaphoreType.DMA((2 * plan.steps, 2))]


def cut_call(plan, chunk, meta, whole, wait=()):
    def kernel(m, whole_ref, *refs):
        out_ref, buffer, sems = refs[len(wait):]
        high = plan.step * 2 * plan.sensors
        slots = [(side, t) for side in range(plan.pairs) for t in range(plan.steps)]
        ins, outs = [], []
        for slot, (side, t) in enumerate(slots):
            rows = pl.ds((chunk * plan.steps + t) * high, high)
            ins.append(pltpu.make_async_copy(
                whole_ref.at[side, 1 - m[1], rows], buffer.at[slot], sems.at[0, slot]
            ))
            outs.append(pltpu.make_async_copy(
                buffer.at[slot], out_ref.at[side, pl.ds(t * high, high)], sems.at[1, slot]
            ))
        for copy in ins:
            copy.start()
        for slot in range(len(slots)):
            ins[slot].wait()
            outs[slot].start()
        for copy in outs:
            copy.wait()

    shape = (plan.pairs, plan.part * 2 * plan.sensors, plan.sources)
    return pl.pallas_call(
        kernel,
        in_specs=[pl.BlockSpec(memory_space=pltpu.SMEM), ANYWHERE] + [ANYWHERE] * len(wait),
        out_specs=ANYWHERE,
        out_shape=jax.ShapeDtypeStruct(shape, BF16),
        scratch_shapes=[
            pltpu.VMEM((plan.pairs * plan.steps, shape[1] // plan.steps, plan.sources), BF16),
            pltpu.SemaphoreType.DMA((2, plan.pairs * plan.steps)),
        ],
        cost_estimate=cost(0, 8 * plan.part * plan.sensors * plan.sources),
        compiler_params=pltpu.CompilerParams(vmem_limit_bytes=PRODUCT_BYTES),
        name="cut",
    )(meta, whole, *wait)


def cast_call(plan, chunk, start, wait=()):
    shape = (plan.part, plan.rows, plan.sources)

    def kernel(start_ref, *refs):
        out_ref, buffer, sem = refs[len(wait):]
        rows = pl.ds(chunk * plan.part, plan.part)
        copy = pltpu.make_async_copy(start_ref.at[rows], buffer, sem)
        copy.start()
        copy.wait()
        out_ref[...] = buffer[...].astype(BF16)

    return pl.pallas_call(
        kernel,
        in_specs=[ANYWHERE] + [ANYWHERE] * len(wait),
        out_specs=pl.BlockSpec(memory_space=pltpu.VMEM),
        out_shape=jax.ShapeDtypeStruct(shape, BF16),
        scratch_shapes=[pltpu.VMEM(shape, F32), pltpu.SemaphoreType.DMA(())],
        cost_estimate=cost(0, 6 * plan.part * plan.rows * plan.sources),
        compiler_params=pltpu.CompilerParams(vmem_limit_bytes=KERNEL_BYTES),
        name="cast",
    )(start, *wait)


def forward_call(plan, chunk, meta, near, far, first, vectors, wait=()):
    n_out = 3 if first else 2
    blk_of = lambda p, m: 1 - (m[2] ^ p)

    def kernel(m, near, far, one_ref, two_ref, *refs):
        outs, scratch = refs[len(wait):len(wait) + n_out], refs[len(wait) + n_out:]
        parts = Parts(plan, chunk, m, blk_of, ((near, far), scratch[:3]), first)
        saves = []
        for phase in range(2):
            blk = blk_of(phase, m)
            for t in range(plan.steps):
                blocks = parts.get(plan, phase, t)
                if first:
                    slot, high = phase * plan.steps + t, plan.step * 2 * plan.sensors
                    saves.append(pltpu.make_async_copy(
                        scratch[0].at[slot],
                        outs[2].at[m[0] ^ blk, pl.ds(t * high, high)],
                        scratch[3].at[slot],
                    ))
                    saves[-1].start()
                for i, (near_part, far_part) in enumerate(blocks):
                    f = t * plan.step + i
                    if first:
                        vector = jnp.where(blk == 0, one_ref[f].astype(BF16), two_ref[f])
                    else:
                        vector = one_ref[blk, f].astype(F32) + two_ref[1 - blk, f].astype(F32)
                    outs[phase][f] = forward_rows(vector.astype(BF16), near_part, far_part).astype(BF16)
        for save in saves:
            save.wait()

    size = (plan.part, plan.rows, plan.sources)
    if first:
        vec_specs = [
            pl.BlockSpec(size, lambda i: (chunk, 0, 0)),
            pl.BlockSpec(size, lambda i: (0, 0, 0)),
        ]
    else:
        vec_specs = [pl.BlockSpec((2,) + size, lambda i: (0, 0, 0, 0))] * 2
    shape = (plan.part, plan.rows, 2 * plan.sensors)
    return pl.pallas_call(
        kernel,
        grid=(1,),
        in_specs=[pl.BlockSpec(memory_space=pltpu.SMEM)] + [ANYWHERE] * 2 + vec_specs
        + [ANYWHERE] * len(wait),
        out_specs=[pl.BlockSpec(shape, lambda i: (0, 0, 0))] * 2 + [ANYWHERE] * (n_out - 2),
        out_shape=[jax.ShapeDtypeStruct(shape, BF16)] * 2
        + [jax.ShapeDtypeStruct(far.shape, BF16)] * (n_out - 2),
        scratch_shapes=Parts.scratch(plan) + [pltpu.SemaphoreType.DMA((2 * plan.steps,))],
        cost_estimate=cost(plan.flops, 16 * plan.part * plan.sensors * plan.sources),
        compiler_params=pltpu.CompilerParams(vmem_limit_bytes=PRODUCT_BYTES if first else KERNEL_BYTES),
        name="forward",
    )(meta, near, far, *vectors, *wait)


def adjoint_call(plan, chunk, meta, near, far, halves, last, wait=()):
    blk_of = lambda p, m: 1 - p
    n_out = 2 if last else 1

    def kernel(m, near, far, own_ref, got_ref, *refs):
        outs, scratch = refs[len(wait):len(wait) + n_out], refs[len(wait) + n_out:]
        parts = Parts(plan, chunk, m, blk_of, ((near, far), scratch), False)
        for phase in range(2):
            blk = blk_of(phase, m)
            for t in range(plan.steps):
                for i, (near_part, far_part) in enumerate(parts.get(plan, phase, t)):
                    f = t * plan.step + i
                    field = jnp.where(blk == m[2], own_ref[f], got_ref[f])
                    back = adjoint_rows(field, near_part, far_part)
                    if last:
                        outs[phase][f] = back.astype(outs[phase].dtype)
                    else:
                        outs[0][blk, f] = back.astype(BF16)

    size = (plan.part, plan.rows, 2 * plan.sensors)
    shape = (plan.part, plan.rows, plan.sources)
    if last:
        out_specs = [pl.BlockSpec(shape, lambda i: (0, 0, 0))] * 2
        out_shape = [jax.ShapeDtypeStruct(shape, BF16), jax.ShapeDtypeStruct(shape, F32)]
    else:
        out_specs = pl.BlockSpec((2,) + shape, lambda i: (0, 0, 0, 0))
        out_shape = jax.ShapeDtypeStruct((2,) + shape, BF16)
    return pl.pallas_call(
        kernel,
        grid=(1,),
        in_specs=[pl.BlockSpec(memory_space=pltpu.SMEM)] + [ANYWHERE] * 2
        + [pl.BlockSpec(size, lambda i: (0, 0, 0))] * 2 + [ANYWHERE] * len(wait),
        out_specs=out_specs,
        out_shape=out_shape,
        scratch_shapes=Parts.scratch(plan),
        cost_estimate=cost(plan.flops, 16 * plan.part * plan.sensors * plan.sources),
        compiler_params=pltpu.CompilerParams(vmem_limit_bytes=KERNEL_BYTES),
        name="adjoint",
    )(meta, near, far, *halves, *wait)


def split_call(plan, meta, keep, got, wait=()):
    piece, groups = plan.piece, plan.groups
    width = keep.shape[-1]

    def kernel(m, keep_ref, got_ref, *refs):
        mine_ref, *sends = refs[len(wait):]
        for d in range(groups):
            place = pl.ds(pl.multiple_of((m[3] ^ d) * piece, piece), piece)
            total = keep_ref[place].astype(F32) + got_ref[place].astype(F32)
            if d == 0:
                mine_ref[...] = total
            else:
                sends[d - 1][...] = total.astype(BF16)

    whole = pl.BlockSpec(memory_space=pltpu.VMEM)
    return pl.pallas_call(
        kernel,
        in_specs=[pl.BlockSpec(memory_space=pltpu.SMEM), whole, whole] + [ANYWHERE] * len(wait),
        out_specs=[whole] * groups,
        out_shape=[jax.ShapeDtypeStruct((piece, width), F32)]
        + [jax.ShapeDtypeStruct((piece, width), BF16)] * (groups - 1),
        cost_estimate=cost(groups * piece * width, groups * piece * width * 8),
        compiler_params=pltpu.CompilerParams(vmem_limit_bytes=KERNEL_BYTES),
        name="split",
    )(meta, keep.reshape(-1, width), got.reshape(-1, width), *wait)


def place_call(plan, meta, pieces, wait=()):
    piece, groups = plan.piece, plan.groups
    width = pieces[0].shape[-1]

    def kernel(m, *refs):
        for d in range(groups):
            place = pl.ds(pl.multiple_of((m[3] ^ d) * piece, piece), piece)
            refs[-1][place] = refs[d][...]

    whole = pl.BlockSpec(memory_space=pltpu.VMEM)
    out = pl.pallas_call(
        kernel,
        in_specs=[pl.BlockSpec(memory_space=pltpu.SMEM)] + [whole] * groups
        + [ANYWHERE] * len(wait),
        out_specs=whole,
        out_shape=jax.ShapeDtypeStruct((groups * piece, width), BF16),
        cost_estimate=cost(0, groups * piece * width * 4),
        compiler_params=pltpu.CompilerParams(vmem_limit_bytes=KERNEL_BYTES),
        name="place",
    )(meta, *pieces, *wait)
    return out.reshape(plan.part, plan.rows, width)


def ordered(array, *earlier):
    def kernel(*refs):
        del refs

    return pl.pallas_call(
        kernel,
        in_specs=[ANYWHERE] * (1 + len(earlier)),
        out_specs=ANYWHERE,
        out_shape=jax.ShapeDtypeStruct(array.shape, array.dtype),
        input_output_aliases={0: 0},
        cost_estimate=cost(0, 0),
        compiler_params=pltpu.CompilerParams(vmem_limit_bytes=KERNEL_BYTES),
        name="ordered",
    )(array, *earlier)


def lanes(array):
    total = jnp.sum(array.reshape(-1, 8, array.shape[-1]), axis=0)
    return sum(total[:, i:i + 128] for i in range(0, array.shape[-1], 128))


def sensor_call(
    plan, chunk, meta, weights, pieces, norms, alpha=None, damping=None, old=None, wait=()
):
    piece, rows, groups = plan.piece, plan.rows, plan.groups
    width = pieces[0].shape[-1]
    count = max(1, piece // rows)
    high = piece // count
    second = old is not None

    def kernel(m, *refs):
        if second:
            alpha_ref, damp_ref, old_ref, *refs = refs
        weights_ref, norms_ref, *refs = refs
        ins, (out_ref, *more) = refs[:groups], refs[groups + len(wait):]
        stats_ref = more[-1]
        square = cross = jnp.zeros((8, 128), F32)
        for c in range(count):
            at = pl.ds(c * high, high)
            freq = chunk * plan.part + (m[3] * piece + c * high) // rows
            field = ins[0][at]
            for ref in ins[1:]:
                field = field + ref[at].astype(F32)
            if second:
                factor = 1.0 - alpha_ref[0] * damp_ref[freq]
                field = factor * old_ref[at] - alpha_ref[0] * field
            scaled = weights_ref[pl.ds(freq, 1)] * field
            out_ref[at] = scaled.astype(BF16)
            square = square + lanes(scaled * field)
            if second:
                cross = cross + lanes(scaled * old_ref[at])
            else:
                more[0][at] = field
        stats_ref[0:8] = norms_ref[0:8]
        stats_ref[8:16] = norms_ref[8:16] + square
        stats_ref[16:24] = norms_ref[16:24] + cross

    whole = pl.BlockSpec(memory_space=pltpu.VMEM)
    scalars = pl.BlockSpec(memory_space=pltpu.SMEM)
    first_out = [] if second else [jax.ShapeDtypeStruct((piece, width), F32)]
    extra = (alpha, damping, old) if second else ()
    out_shape = [jax.ShapeDtypeStruct((piece, width), BF16)] + first_out
    out_shape = out_shape + [jax.ShapeDtypeStruct((24, 128), F32)]
    return pl.pallas_call(
        kernel,
        in_specs=[scalars] + ([scalars] * 2 + [whole] if second else []) + [whole] * (2 + groups)
        + [ANYWHERE] * len(wait),
        out_specs=[whole] * len(out_shape),
        out_shape=out_shape,
        cost_estimate=cost(8 * piece * width, 16 * piece * width),
        compiler_params=pltpu.CompilerParams(vmem_limit_bytes=KERNEL_BYTES),
        name="sensor",
    )(meta, *extra, weights, norms, *pieces, *wait)


def norms_call(plan, chunk, damping, start):
    block = (plan.part, plan.rows, plan.sources)

    def kernel(damp_ref, start_ref, stats_ref):
        plain = damped = jnp.zeros((8, 128), F32)
        for f in range(plan.part):
            term = lanes(start_ref[f] * start_ref[f])
            plain = plain + term
            damped = damped + damp_ref[chunk * plan.part + f] * term
        stats_ref[0:8] = plain
        stats_ref[8:16] = damped
        stats_ref[16:24] = jnp.zeros((8, 128), F32)

    return pl.pallas_call(
        kernel,
        grid=(1,),
        in_specs=[
            pl.BlockSpec(memory_space=pltpu.SMEM),
            pl.BlockSpec(block, lambda i: (chunk, 0, 0)),
        ],
        out_specs=pl.BlockSpec((24, 128), lambda i: (0, 0)),
        out_shape=jax.ShapeDtypeStruct((24, 128), F32),
        cost_estimate=cost(2 * start.size, 4 * start.size),
        compiler_params=pltpu.CompilerParams(vmem_limit_bytes=KERNEL_BYTES),
        name="norms",
    )(damping, start)


def residual_call(plan, chunk, alpha, damping, start, mine, got):
    part, rows, sources = plan.part, plan.rows, plan.sources

    def kernel(alpha_ref, damp_ref, start_ref, mine_ref, got_ref, image_ref, out_ref, stats_ref):
        plain = damped = mixed = jnp.zeros((8, 128), F32)
        for f in range(part):
            damp = damp_ref[chunk * part + f]
            begin = start_ref[f]
            image = mine_ref[f].astype(F32) + got_ref[f].astype(F32) + damp * begin
            residual = begin - alpha_ref[0] * image
            image_ref[f] = image
            out_ref[f] = residual
            term = lanes(residual * residual)
            plain = plain + term
            damped = damped + damp * term
            mixed = mixed + damp * lanes(residual * begin)
        stats_ref[0:8] = plain
        stats_ref[8:16] = damped
        stats_ref[16:24] = mixed

    block = (part, rows, sources)
    scalars = pl.BlockSpec(memory_space=pltpu.SMEM)
    out = jax.ShapeDtypeStruct(block, F32)
    return pl.pallas_call(
        kernel,
        grid=(1,),
        in_specs=[
            scalars,
            scalars,
            pl.BlockSpec(block, lambda i: (chunk, 0, 0)),
            pl.BlockSpec((None,) + block, lambda i: (0, 0, 0, 0)),
            pl.BlockSpec((None,) + block, lambda i: (1, 0, 0, 0)),
        ],
        out_specs=[
            pl.BlockSpec(block, lambda i: (0, 0, 0)),
            pl.BlockSpec(block, lambda i: (0, 0, 0)),
            pl.BlockSpec((24, 128), lambda i: (0, 0)),
        ],
        out_shape=[out, out, jax.ShapeDtypeStruct((24, 128), F32)],
        cost_estimate=cost(8 * part * rows * sources, 16 * part * rows * sources),
        compiler_params=pltpu.CompilerParams(vmem_limit_bytes=KERNEL_BYTES),
        name="residual",
    )(alpha, damping, start, mine, got)


def body(n_sens, n_src, operator, right_side, noise_weights, damping):
    plan = Plan(operator, right_side, n_sens, n_src, CHUNKS)
    sens, src = lax.axis_index("sens"), lax.axis_index("src")
    pair, core, half, group = sens // 2, sens % 2, src % 2, src // 2
    meta = jnp.stack([pair, core, half, group]).astype(jnp.int32)
    part, rows, block = plan.part, plan.rows, plan.block
    levels = range(n_src.bit_length() - 1)
    chunks = range(plan.chunks)

    def to_core(array):
        return lax.ppermute(array, "sens", [(i, i ^ 1) for i in range(n_sens)])

    def to_pair(array):
        return lax.ppermute(array, "sens", [(i, i ^ 2) for i in range(n_sens)])

    def to_src(array, step):
        return lax.ppermute(array, "src", [(j, j ^ step) for j in range(n_src)])

    def in_turn(arrays, move):
        moved = []
        for k, array in enumerate(arrays):
            if k > 0:
                array = arrays[k] = ordered(array, moved[-1])
            moved.append(move(array))
        return moved

    def total_near(sums):
        sums = sums + to_core(sums)
        sums = sums + to_pair(sums)
        return sums + to_src(sums, 1)

    def total_far(sums):
        for level in levels[1:]:
            sums = sums + to_src(sums, 1 << level)
        return sums, jnp.sum(sums.reshape(-1, 8 * 128), axis=1)

    def double(table, level):
        other = to_src(table, 1 << level)
        low = (src >> level) % 2 == 0
        return jnp.concatenate([jnp.where(low, table, other), jnp.where(low, other, table)], axis=0)

    whole = operator.reshape(plan.pairs, 2, block * 2 * plan.sensors, plan.sources)
    start = right_side.reshape(block, rows, plan.sources)

    casts = [cast_call(plan, k, start) for k in chunks]
    cuts = [cut_call(plan, k, meta, whole, (casts[0],)) for k in chunks]
    got_b = in_turn(list(casts), to_pair)
    weights = noise_weights
    for level in levels[:2]:
        weights = double(weights, level)
    far, pairs = [to_core(cut) for cut in cuts], []
    for k in chunks:
        wait = tuple(casts[1:]) + tuple(cuts[1:]) + (weights,) if k == 0 else ()
        pairs.append(forward_call(plan, k, meta, whole, far[k], True, (start, got_b[k]), wait))

    for level in levels[2:]:
        weights = double(weights, level)
    weights = weights.reshape(plan.pairs, 2, block, plan.sensors)
    weights_near = lax.dynamic_index_in_dim(weights, core, 1, keepdims=False)
    weights_far = to_core(lax.dynamic_index_in_dim(weights, 1 - core, 1, keepdims=False))
    weights = jnp.concatenate([weights_near, weights_far], axis=-1)
    weights = lax.dynamic_index_in_dim(weights, pair ^ half, 0, keepdims=False)
    damping_row = jnp.where(half == 0, damping, to_pair(damping))
    steps = [2 * d for d in range(1, plan.groups)]

    def reduce_field(keep, got, wait=()):
        mine, *sends = split_call(plan, meta, keep, got, wait)
        return [mine] + [to_src(piece, step) for piece, step in zip(sends, steps)]

    def to_half(array):
        return to_src(array, 1)

    def both_products(scaled, near_sums, last, then):
        outs, wait, sums = [], (), None
        for k in chunks:
            pieces = [scaled[k]] + [to_src(scaled[k], step) for step in steps]
            own = place_call(plan, meta, pieces, wait)
            halves = (own, to_half(own))
            if k == 1:
                after = outs[0][1][0]
                far_sums, sums = total_far(near_sums if last else ordered(near_sums, after))
                wait = (after, far_sums)
            out = adjoint_call(plan, k, meta, near[k], far[k], halves, last, wait if k > 0 else ())
            outs.append((out, then(k, out)))
            wait = (out[0] if last else out, near_sums)
        return outs, total_far(near_sums)[1] if sums is None else sums

    sends, near = [each[0] for each in pairs], [each[2] for each in pairs]
    got = in_turn(sends, to_half)
    pieces = [reduce_field(pairs[k][1], got[k], tuple(sends[k + 1:k + 2])) for k in chunks]
    scaled, field, stats = zip(*[
        sensor_call(
            plan, k, meta, weights, pieces[k], norms_call(plan, k, damping, start),
            wait=tuple(got[k + 1:k + 2]),
        )
        for k in chunks
    ])
    near_0 = total_near(sum(stats))

    def go_on(k, back):
        got = to_pair(back)
        send, keep = forward_call(plan, k, meta, near[k], far[k], False, (back, got))
        return send, keep, got

    outs, sums = both_products(scaled, near_0, False, go_on)
    norm_0, curve_0 = sums[0], sums[1]
    alpha_0 = (norm_0 / curve_0)[None]
    back = [out for out, _ in outs]
    sends, keeps, got_back = zip(*[rest for _, rest in outs])
    got = in_turn(list(sends), to_half)
    image_0, residual, norms = zip(*[
        residual_call(plan, k, alpha_0, damping, start, back[k], got_back[k]) for k in chunks
    ])
    pieces = [reduce_field(keeps[k], got[k], (norms[k],)) for k in chunks]
    scaled, stats = zip(*[
        sensor_call(plan, k, meta, weights, pieces[k], norms[k], alpha_0, damping_row, field[k])
        for k in chunks
    ])
    near_1 = total_near(sum(stats))
    outs, sums = both_products(scaled, near_1, True, lambda k, out: (to_pair(out[0]),))
    norm_1 = sums[0]
    beta = norm_1 / norm_0
    curve_1 = sums[1] + 2.0 * beta * sums[2] + beta * beta * curve_0
    alpha_1 = norm_1 / curve_1

    final = [mine + rest[0].astype(F32) for (_, mine), rest in outs]
    residual, image_0 = jnp.concatenate(residual), jnp.concatenate(image_0)
    image_1 = jnp.concatenate(final) + damping[:, None, None] * residual + beta * image_0
    solution = alpha_0 * start + alpha_1 * (residual + beta * start)
    residual = residual - alpha_1 * image_1
    return solution.reshape(right_side.shape), residual.reshape(right_side.shape)


def solution(mesh):
    in_specs = (
        P(None, None, "sens", "src"),
        P("sens", None, None, "src"),
        P("src", "sens"),
        P("sens"),
    )
    out_specs = (P("sens", None, None, "src"), P("sens", None, None, "src"))
    shard = functools.partial(body, mesh.shape["sens"], mesh.shape["src"])
    return jax.shard_map(shard, mesh=mesh, in_specs=in_specs, out_specs=out_specs, check_vma=False)
```

```python
import functools

import jax
import jax.numpy as jnp
from jax import lax
from jax.experimental import pallas as pl
from jax.experimental.pallas import tpu as pltpu
from jax.sharding import PartitionSpec as P

CHUNKS = 2
KERNEL_BYTES = 16 * 2 ** 20
PRODUCT_BYTES = 56 * 2 ** 20
F32 = jnp.float32
BF16 = jnp.bfloat16
ANYWHERE = pl.BlockSpec(memory_space=pl.ANY)
NT = (((1,), (1,)), ((), ()))
NN = (((1,), (0,)), ((), ()))


def largest_divisor(extent, most):
    return next(size for size in range(min(extent, most), 0, -1) if extent % size == 0)


def turned(block, sign):
    half = block.shape[0] // 2
    upper, lower = block[:half], block[half:]
    return jnp.concatenate([-lower, upper] if sign < 0 else [lower, -upper], axis=0)


def forward_rows(vector, near, far):
    left = jnp.concatenate([vector, turned(vector, -1)], axis=1)
    right = jnp.concatenate(
        [jnp.concatenate([part[0], part[1]], axis=1) for part in (near, far)], axis=0
    )
    return lax.dot_general(left, right, NT, preferred_element_type=F32)


def adjoint_rows(field, near, far):
    sensors = near[0].shape[0]
    total = None
    for part, piece in ((near, field[:, :sensors]), (far, field[:, sensors:])):
        left = jnp.concatenate([piece, turned(piece, 1)], axis=1)
        right = jnp.concatenate(part, axis=0)
        term = lax.dot_general(left, right, NN, preferred_element_type=F32)
        total = term if total is None else total + term
    return total


def cost(flops, moved):
    return pl.CostEstimate(flops=flops // 1000, bytes_accessed=moved // 1000, transcendentals=0)


class Plan:
    def __init__(self, operator, right_side, n_sens, n_src, chunks):
        self.freqs, _, self.sensors, self.sources = operator.shape
        self.block = right_side.shape[0]
        self.rows = right_side.shape[1] * right_side.shape[2]
        self.pairs = n_sens // 2
        self.groups = n_src // 2
        self.chunks = chunks
        self.part = self.block // chunks
        self.step = largest_divisor(self.part, 8)
        self.steps = self.part // self.step
        self.flops = 16 * self.part * self.rows * self.sensors * self.sources * 2
        self.piece = self.part * self.rows // self.groups


class Parts:
    def __init__(self, plan, chunk, m, blk_of, refs, whole):
        (near, far), (near_buf, far_buf, sems) = refs
        self.buffers, self.copies = (near_buf, far_buf), {}
        high = plan.step * 2 * plan.sensors
        for phase in range(2):
            for t in range(plan.steps):
                slot = phase * plan.steps + t
                side = m[0] ^ blk_of(phase, m)
                rows = pl.ds(t * high, high)
                near_rows = pl.ds((chunk * plan.steps + t) * high, high)
                source = near.at[side, m[1], near_rows] if whole else near.at[side, rows]
                self.copies[phase, t] = [
                    pltpu.make_async_copy(ref, buffer.at[slot], sems.at[slot, place])
                    for place, (ref, buffer) in enumerate((
                        (source, near_buf),
                        (far.at[side, rows], far_buf),
                    ))
                ]
        for copies in self.copies.values():
            for copy in copies:
                copy.start()

    def get(self, plan, phase, t):
        for copy in self.copies[phase, t]:
            copy.wait()
        slot, high = phase * plan.steps + t, plan.sensors
        return [
            tuple(
                tuple(buffer[slot, pl.ds((2 * f + c) * high, high)] for c in range(2))
                for buffer in self.buffers
            )
            for f in range(plan.step)
        ]

    @staticmethod
    def scratch(plan):
        buffer = pltpu.VMEM((2 * plan.steps, plan.step * 2 * plan.sensors, plan.sources), BF16)
        return [buffer, buffer, pltpu.SemaphoreType.DMA((2 * plan.steps, 2))]


def cut_call(plan, chunk, meta, whole, wait=()):
    def kernel(m, whole_ref, *refs):
        out_ref, buffer, sems = refs[len(wait):]
        high = plan.step * 2 * plan.sensors
        slots = [(side, t) for side in range(plan.pairs) for t in range(plan.steps)]
        ins, outs = [], []
        for slot, (side, t) in enumerate(slots):
            rows = pl.ds((chunk * plan.steps + t) * high, high)
            ins.append(pltpu.make_async_copy(
                whole_ref.at[side, 1 - m[1], rows], buffer.at[slot], sems.at[0, slot]
            ))
            outs.append(pltpu.make_async_copy(
                buffer.at[slot], out_ref.at[side, pl.ds(t * high, high)], sems.at[1, slot]
            ))
        for copy in ins:
            copy.start()
        for slot in range(len(slots)):
            ins[slot].wait()
            outs[slot].start()
        for copy in outs:
            copy.wait()

    shape = (plan.pairs, plan.part * 2 * plan.sensors, plan.sources)
    return pl.pallas_call(
        kernel,
        in_specs=[pl.BlockSpec(memory_space=pltpu.SMEM), ANYWHERE] + [ANYWHERE] * len(wait),
        out_specs=ANYWHERE,
        out_shape=jax.ShapeDtypeStruct(shape, BF16),
        scratch_shapes=[
            pltpu.VMEM((plan.pairs * plan.steps, shape[1] // plan.steps, plan.sources), BF16),
            pltpu.SemaphoreType.DMA((2, plan.pairs * plan.steps)),
        ],
        cost_estimate=cost(0, 8 * plan.part * plan.sensors * plan.sources),
        compiler_params=pltpu.CompilerParams(vmem_limit_bytes=PRODUCT_BYTES),
        name="cut",
    )(meta, whole, *wait)


def cast_call(plan, chunk, start, wait=()):
    shape = (plan.part, plan.rows, plan.sources)

    def kernel(start_ref, *refs):
        out_ref, buffer, sem = refs[len(wait):]
        rows = pl.ds(chunk * plan.part, plan.part)
        copy = pltpu.make_async_copy(start_ref.at[rows], buffer, sem)
        copy.start()
        copy.wait()
        out_ref[...] = buffer[...].astype(BF16)

    return pl.pallas_call(
        kernel,
        in_specs=[ANYWHERE] + [ANYWHERE] * len(wait),
        out_specs=pl.BlockSpec(memory_space=pltpu.VMEM),
        out_shape=jax.ShapeDtypeStruct(shape, BF16),
        scratch_shapes=[pltpu.VMEM(shape, F32), pltpu.SemaphoreType.DMA(())],
        cost_estimate=cost(0, 6 * plan.part * plan.rows * plan.sources),
        compiler_params=pltpu.CompilerParams(vmem_limit_bytes=KERNEL_BYTES),
        name="cast",
    )(start, *wait)


def forward_call(plan, chunk, meta, near, far, first, vectors, wait=()):
    n_out = 3 if first else 2
    blk_of = lambda p, m: 1 - (m[2] ^ p)

    def kernel(m, near, far, one_ref, two_ref, *refs):
        outs, scratch = refs[len(wait):len(wait) + n_out], refs[len(wait) + n_out:]
        parts = Parts(plan, chunk, m, blk_of, ((near, far), scratch[:3]), first)
        saves = []
        for phase in range(2):
            blk = blk_of(phase, m)
            for t in range(plan.steps):
                blocks = parts.get(plan, phase, t)
                if first:
                    slot, high = phase * plan.steps + t, plan.step * 2 * plan.sensors
                    saves.append(pltpu.make_async_copy(
                        scratch[0].at[slot],
                        outs[2].at[m[0] ^ blk, pl.ds(t * high, high)],
                        scratch[3].at[slot],
                    ))
                    saves[-1].start()
                for i, (near_part, far_part) in enumerate(blocks):
                    f = t * plan.step + i
                    if first:
                        vector = jnp.where(blk == 0, one_ref[f].astype(BF16), two_ref[f])
                    else:
                        vector = one_ref[blk, f].astype(F32) + two_ref[1 - blk, f].astype(F32)
                    outs[phase][f] = forward_rows(vector.astype(BF16), near_part, far_part).astype(BF16)
        for save in saves:
            save.wait()

    size = (plan.part, plan.rows, plan.sources)
    if first:
        vec_specs = [
            pl.BlockSpec(size, lambda i: (chunk, 0, 0)),
            pl.BlockSpec(size, lambda i: (0, 0, 0)),
        ]
    else:
        vec_specs = [pl.BlockSpec((2,) + size, lambda i: (0, 0, 0, 0))] * 2
    shape = (plan.part, plan.rows, 2 * plan.sensors)
    return pl.pallas_call(
        kernel,
        grid=(1,),
        in_specs=[pl.BlockSpec(memory_space=pltpu.SMEM)] + [ANYWHERE] * 2 + vec_specs
        + [ANYWHERE] * len(wait),
        out_specs=[pl.BlockSpec(shape, lambda i: (0, 0, 0))] * 2 + [ANYWHERE] * (n_out - 2),
        out_shape=[jax.ShapeDtypeStruct(shape, BF16)] * 2
        + [jax.ShapeDtypeStruct(far.shape, BF16)] * (n_out - 2),
        scratch_shapes=Parts.scratch(plan) + [pltpu.SemaphoreType.DMA((2 * plan.steps,))],
        cost_estimate=cost(plan.flops, 16 * plan.part * plan.sensors * plan.sources),
        compiler_params=pltpu.CompilerParams(vmem_limit_bytes=PRODUCT_BYTES if first else KERNEL_BYTES),
        name="forward",
    )(meta, near, far, *vectors, *wait)


def adjoint_call(plan, chunk, meta, near, far, halves, last, wait=()):
    blk_of = lambda p, m: 1 - p
    n_out = 2 if last else 1

    def kernel(m, near, far, own_ref, got_ref, *refs):
        outs, scratch = refs[len(wait):len(wait) + n_out], refs[len(wait) + n_out:]
        parts = Parts(plan, chunk, m, blk_of, ((near, far), scratch), False)
        for phase in range(2):
            blk = blk_of(phase, m)
            for t in range(plan.steps):
                for i, (near_part, far_part) in enumerate(parts.get(plan, phase, t)):
                    f = t * plan.step + i
                    field = jnp.where(blk == m[2], own_ref[f], got_ref[f])
                    back = adjoint_rows(field, near_part, far_part)
                    if last:
                        outs[phase][f] = back.astype(outs[phase].dtype)
                    else:
                        outs[0][blk, f] = back.astype(BF16)

    size = (plan.part, plan.rows, 2 * plan.sensors)
    shape = (plan.part, plan.rows, plan.sources)
    if last:
        out_specs = [pl.BlockSpec(shape, lambda i: (0, 0, 0))] * 2
        out_shape = [jax.ShapeDtypeStruct(shape, BF16), jax.ShapeDtypeStruct(shape, F32)]
    else:
        out_specs = pl.BlockSpec((2,) + shape, lambda i: (0, 0, 0, 0))
        out_shape = jax.ShapeDtypeStruct((2,) + shape, BF16)
    return pl.pallas_call(
        kernel,
        grid=(1,),
        in_specs=[pl.BlockSpec(memory_space=pltpu.SMEM)] + [ANYWHERE] * 2
        + [pl.BlockSpec(size, lambda i: (0, 0, 0))] * 2 + [ANYWHERE] * len(wait),
        out_specs=out_specs,
        out_shape=out_shape,
        scratch_shapes=Parts.scratch(plan),
        cost_estimate=cost(plan.flops, 16 * plan.part * plan.sensors * plan.sources),
        compiler_params=pltpu.CompilerParams(vmem_limit_bytes=KERNEL_BYTES),
        name="adjoint",
    )(meta, near, far, *halves, *wait)


def split_call(plan, meta, keep, got, wait=()):
    piece, groups = plan.piece, plan.groups
    width = keep.shape[-1]

    def kernel(m, keep_ref, got_ref, *refs):
        mine_ref, *sends = refs[len(wait):]
        for d in range(groups):
            place = pl.ds(pl.multiple_of((m[3] ^ d) * piece, piece), piece)
            total = keep_ref[place].astype(F32) + got_ref[place].astype(F32)
            if d == 0:
                mine_ref[...] = total
            else:
                sends[d - 1][...] = total.astype(BF16)

    whole = pl.BlockSpec(memory_space=pltpu.VMEM)
    return pl.pallas_call(
        kernel,
        in_specs=[pl.BlockSpec(memory_space=pltpu.SMEM), whole, whole] + [ANYWHERE] * len(wait),
        out_specs=[whole] * groups,
        out_shape=[jax.ShapeDtypeStruct((piece, width), F32)]
        + [jax.ShapeDtypeStruct((piece, width), BF16)] * (groups - 1),
        cost_estimate=cost(groups * piece * width, groups * piece * width * 8),
        compiler_params=pltpu.CompilerParams(vmem_limit_bytes=KERNEL_BYTES),
        name="split",
    )(meta, keep.reshape(-1, width), got.reshape(-1, width), *wait)


def place_call(plan, meta, pieces, wait=()):
    piece, groups = plan.piece, plan.groups
    width = pieces[0].shape[-1]

    def kernel(m, *refs):
        for d in range(groups):
            place = pl.ds(pl.multiple_of((m[3] ^ d) * piece, piece), piece)
            refs[-1][place] = refs[d][...]

    whole = pl.BlockSpec(memory_space=pltpu.VMEM)
    out = pl.pallas_call(
        kernel,
        in_specs=[pl.BlockSpec(memory_space=pltpu.SMEM)] + [whole] * groups
        + [ANYWHERE] * len(wait),
        out_specs=whole,
        out_shape=jax.ShapeDtypeStruct((groups * piece, width), BF16),
        cost_estimate=cost(0, groups * piece * width * 4),
        compiler_params=pltpu.CompilerParams(vmem_limit_bytes=KERNEL_BYTES),
        name="place",
    )(meta, *pieces, *wait)
    return out.reshape(plan.part, plan.rows, width)


def ordered(array, *earlier):
    def kernel(*refs):
        del refs

    return pl.pallas_call(
        kernel,
        in_specs=[ANYWHERE] * (1 + len(earlier)),
        out_specs=ANYWHERE,
        out_shape=jax.ShapeDtypeStruct(array.shape, array.dtype),
        input_output_aliases={0: 0},
        cost_estimate=cost(0, 0),
        compiler_params=pltpu.CompilerParams(vmem_limit_bytes=KERNEL_BYTES),
        name="ordered",
    )(array, *earlier)


def lanes(array):
    total = jnp.sum(array.reshape(-1, 8, array.shape[-1]), axis=0)
    return sum(total[:, i:i + 128] for i in range(0, array.shape[-1], 128))


def sensor_call(
    plan, chunk, meta, weights, pieces, norms, alpha=None, damping=None, old=None, wait=()
):
    piece, rows, groups = plan.piece, plan.rows, plan.groups
    width = pieces[0].shape[-1]
    count = max(1, piece // rows)
    high = piece // count
    second = old is not None

    def kernel(m, *refs):
        if second:
            alpha_ref, damp_ref, old_ref, *refs = refs
        weights_ref, norms_ref, *refs = refs
        ins, (out_ref, *more) = refs[:groups], refs[groups + len(wait):]
        stats_ref = more[-1]
        square = cross = jnp.zeros((8, 128), F32)
        for c in range(count):
            at = pl.ds(c * high, high)
            freq = chunk * plan.part + (m[3] * piece + c * high) // rows
            field = ins[0][at]
            for ref in ins[1:]:
                field = field + ref[at].astype(F32)
            if second:
                factor = 1.0 - alpha_ref[0] * damp_ref[freq]
                field = factor * old_ref[at] - alpha_ref[0] * field
            scaled = weights_ref[pl.ds(freq, 1)] * field
            out_ref[at] = scaled.astype(BF16)
            square = square + lanes(scaled * field)
            if second:
                cross = cross + lanes(scaled * old_ref[at])
            else:
                more[0][at] = field
        stats_ref[0:8] = norms_ref[0:8]
        stats_ref[8:16] = norms_ref[8:16] + square
        stats_ref[16:24] = norms_ref[16:24] + cross

    whole = pl.BlockSpec(memory_space=pltpu.VMEM)
    scalars = pl.BlockSpec(memory_space=pltpu.SMEM)
    first_out = [] if second else [jax.ShapeDtypeStruct((piece, width), F32)]
    extra = (alpha, damping, old) if second else ()
    out_shape = [jax.ShapeDtypeStruct((piece, width), BF16)] + first_out
    out_shape = out_shape + [jax.ShapeDtypeStruct((24, 128), F32)]
    return pl.pallas_call(
        kernel,
        in_specs=[scalars] + ([scalars] * 2 + [whole] if second else []) + [whole] * (2 + groups)
        + [ANYWHERE] * len(wait),
        out_specs=[whole] * len(out_shape),
        out_shape=out_shape,
        cost_estimate=cost(8 * piece * width, 16 * piece * width),
        compiler_params=pltpu.CompilerParams(vmem_limit_bytes=KERNEL_BYTES),
        name="sensor",
    )(meta, *extra, weights, norms, *pieces, *wait)


def norms_call(plan, chunk, damping, start):
    block = (plan.part, plan.rows, plan.sources)

    def kernel(damp_ref, start_ref, stats_ref):
        plain = damped = jnp.zeros((8, 128), F32)
        for f in range(plan.part):
            term = lanes(start_ref[f] * start_ref[f])
            plain = plain + term
            damped = damped + damp_ref[chunk * plan.part + f] * term
        stats_ref[0:8] = plain
        stats_ref[8:16] = damped
        stats_ref[16:24] = jnp.zeros((8, 128), F32)

    return pl.pallas_call(
        kernel,
        grid=(1,),
        in_specs=[
            pl.BlockSpec(memory_space=pltpu.SMEM),
            pl.BlockSpec(block, lambda i: (chunk, 0, 0)),
        ],
        out_specs=pl.BlockSpec((24, 128), lambda i: (0, 0)),
        out_shape=jax.ShapeDtypeStruct((24, 128), F32),
        cost_estimate=cost(2 * start.size, 4 * start.size),
        compiler_params=pltpu.CompilerParams(vmem_limit_bytes=KERNEL_BYTES),
        name="norms",
    )(damping, start)


def residual_call(plan, chunk, alpha, damping, start, mine, got):
    part, rows, sources = plan.part, plan.rows, plan.sources

    def kernel(alpha_ref, damp_ref, start_ref, mine_ref, got_ref, image_ref, out_ref, stats_ref):
        plain = damped = mixed = jnp.zeros((8, 128), F32)
        for f in range(part):
            damp = damp_ref[chunk * part + f]
            begin = start_ref[f]
            image = mine_ref[f].astype(F32) + got_ref[f].astype(F32) + damp * begin
            residual = begin - alpha_ref[0] * image
            image_ref[f] = image
            out_ref[f] = residual
            term = lanes(residual * residual)
            plain = plain + term
            damped = damped + damp * term
            mixed = mixed + damp * lanes(residual * begin)
        stats_ref[0:8] = plain
        stats_ref[8:16] = damped
        stats_ref[16:24] = mixed

    block = (part, rows, sources)
    scalars = pl.BlockSpec(memory_space=pltpu.SMEM)
    out = jax.ShapeDtypeStruct(block, F32)
    return pl.pallas_call(
        kernel,
        grid=(1,),
        in_specs=[
            scalars,
            scalars,
            pl.BlockSpec(block, lambda i: (chunk, 0, 0)),
            pl.BlockSpec((None,) + block, lambda i: (0, 0, 0, 0)),
            pl.BlockSpec((None,) + block, lambda i: (1, 0, 0, 0)),
        ],
        out_specs=[
            pl.BlockSpec(block, lambda i: (0, 0, 0)),
            pl.BlockSpec(block, lambda i: (0, 0, 0)),
            pl.BlockSpec((24, 128), lambda i: (0, 0)),
        ],
        out_shape=[out, out, jax.ShapeDtypeStruct((24, 128), F32)],
        cost_estimate=cost(8 * part * rows * sources, 16 * part * rows * sources),
        compiler_params=pltpu.CompilerParams(vmem_limit_bytes=KERNEL_BYTES),
        name="residual",
    )(alpha, damping, start, mine, got)


def body(n_sens, n_src, operator, right_side, noise_weights, damping):
    plan = Plan(operator, right_side, n_sens, n_src, CHUNKS)
    sens, src = lax.axis_index("sens"), lax.axis_index("src")
    pair, core, half, group = sens // 2, sens % 2, src % 2, src // 2
    meta = jnp.stack([pair, core, half, group]).astype(jnp.int32)
    part, rows, block = plan.part, plan.rows, plan.block
    levels = range(n_src.bit_length() - 1)
    chunks = range(plan.chunks)

    def to_core(array):
        return lax.ppermute(array, "sens", [(i, i ^ 1) for i in range(n_sens)])

    def to_pair(array):
        return lax.ppermute(array, "sens", [(i, i ^ 2) for i in range(n_sens)])

    def to_src(array, step):
        return lax.ppermute(array, "src", [(j, j ^ step) for j in range(n_src)])

    def in_turn(arrays, move):
        moved = []
        for k, array in enumerate(arrays):
            if k > 0:
                array = arrays[k] = ordered(array, moved[-1])
            moved.append(move(array))
        return moved

    def total_near(sums, last):
        sums = sums + (to_src(sums, 1) if last else to_core(sums))
        sums = sums + to_pair(sums)
        return sums if last else sums + to_src(sums, 1)

    def total_far(sums, last):
        if last:
            sums = sums + to_core(sums)
        for level in levels[1:]:
            sums = sums + to_src(sums, 1 << level)
        return sums, jnp.sum(sums.reshape(-1, 8 * 128), axis=1)

    def double(table, level):
        other = to_src(table, 1 << level)
        low = (src >> level) % 2 == 0
        return jnp.concatenate([jnp.where(low, table, other), jnp.where(low, other, table)], axis=0)

    whole = operator.reshape(plan.pairs, 2, block * 2 * plan.sensors, plan.sources)
    start = right_side.reshape(block, rows, plan.sources)

    casts = [cast_call(plan, k, start) for k in chunks]
    cuts = [cut_call(plan, k, meta, whole, (casts[0],)) for k in chunks]
    got_b = in_turn(list(casts), to_pair)
    weights = noise_weights
    for level in levels[:2]:
        weights = double(weights, level)
    far, pairs = [to_core(cut) for cut in cuts], []
    for k in chunks:
        wait = tuple(casts[1:]) + tuple(cuts[1:]) + (weights,) if k == 0 else ()
        pairs.append(forward_call(plan, k, meta, whole, far[k], True, (start, got_b[k]), wait))

    for level in levels[2:]:
        weights = double(weights, level)
    weights = weights.reshape(plan.pairs, 2, block, plan.sensors)
    weights_near = lax.dynamic_index_in_dim(weights, core, 1, keepdims=False)
    weights_far = to_core(lax.dynamic_index_in_dim(weights, 1 - core, 1, keepdims=False))
    weights = jnp.concatenate([weights_near, weights_far], axis=-1)
    weights = lax.dynamic_index_in_dim(weights, pair ^ half, 0, keepdims=False)
    damping_row = jnp.where(half == 0, damping, to_pair(damping))
    steps = [2 * d for d in range(1, plan.groups)]

    def reduce_field(keep, got, wait=()):
        mine, *sends = split_call(plan, meta, keep, got, wait)
        return [mine] + [to_src(piece, step) for piece, step in zip(sends, steps)]

    def to_half(array):
        return to_src(array, 1)

    def both_products(scaled, near_sums, last, then):
        outs, wait, sums = [], (), None
        for k in chunks:
            pieces = [scaled[k]] + [to_src(scaled[k], step) for step in steps]
            own = place_call(plan, meta, pieces, wait)
            halves = (own, to_half(own))
            if k == 1:
                after = outs[0][1][0]
                far_sums, sums = total_far(near_sums if last else ordered(near_sums, after), last)
                wait = (after, far_sums)
            out = adjoint_call(plan, k, meta, near[k], far[k], halves, last, wait if k > 0 else ())
            outs.append((out, then(k, out)))
            wait = (out[0] if last else out, near_sums)
        return outs, total_far(near_sums, last)[1] if sums is None else sums

    sends, near = [each[0] for each in pairs], [each[2] for each in pairs]
    got = in_turn(sends, to_half)
    pieces = [reduce_field(pairs[k][1], got[k], tuple(sends[k + 1:k + 2])) for k in chunks]
    scaled, field, stats = zip(*[
        sensor_call(
            plan, k, meta, weights, pieces[k], norms_call(plan, k, damping, start),
            wait=tuple(got[k + 1:k + 2]),
        )
        for k in chunks
    ])
    near_0 = total_near(sum(stats), False)

    def go_on(k, back):
        got = to_pair(back)
        send, keep = forward_call(plan, k, meta, near[k], far[k], False, (back, got))
        return send, keep, got

    outs, sums = both_products(scaled, near_0, False, go_on)
    norm_0, curve_0 = sums[0], sums[1]
    alpha_0 = (norm_0 / curve_0)[None]
    back = [out for out, _ in outs]
    sends, keeps, got_back = zip(*[rest for _, rest in outs])
    got = in_turn(list(sends), to_half)
    image_0, residual, norms = zip(*[
        residual_call(plan, k, alpha_0, damping, start, back[k], got_back[k]) for k in chunks
    ])
    pieces = [reduce_field(keeps[k], got[k], (norms[k],)) for k in chunks]
    scaled, stats = zip(*[
        sensor_call(plan, k, meta, weights, pieces[k], norms[k], alpha_0, damping_row, field[k])
        for k in chunks
    ])
    near_1 = total_near(sum(stats), True)
    outs, sums = both_products(scaled, near_1, True, lambda k, out: (to_pair(out[0]),))
    norm_1 = sums[0]
    beta = norm_1 / norm_0
    curve_1 = sums[1] + 2.0 * beta * sums[2] + beta * beta * curve_0
    alpha_1 = norm_1 / curve_1

    final = [mine + rest[0].astype(F32) for (_, mine), rest in outs]
    residual, image_0 = jnp.concatenate(residual), jnp.concatenate(image_0)
    image_1 = jnp.concatenate(final) + damping[:, None, None] * residual + beta * image_0
    solution = alpha_0 * start + alpha_1 * (residual + beta * start)
    residual = residual - alpha_1 * image_1
    return solution.reshape(right_side.shape), residual.reshape(right_side.shape)


def solution(mesh):
    in_specs = (
        P(None, None, "sens", "src"),
        P("sens", None, None, "src"),
        P("src", "sens"),
        P("sens"),
    )
    out_specs = (P("sens", None, None, "src"), P("sens", None, None, "src"))
    shard = functools.partial(body, mesh.shape["sens"], mesh.shape["src"])
    return jax.shard_map(shard, mesh=mesh, in_specs=in_specs, out_specs=out_specs, check_vma=False)
```

```python
import functools

import jax
import jax.numpy as jnp
from jax import lax
from jax.experimental import pallas as pl
from jax.experimental.pallas import tpu as pltpu
from jax.sharding import PartitionSpec as P

CHUNKS = 2
KERNEL_BYTES = 16 * 2 ** 20
PRODUCT_BYTES = 56 * 2 ** 20
F32 = jnp.float32
BF16 = jnp.bfloat16
ANYWHERE = pl.BlockSpec(memory_space=pl.ANY)
NT = (((1,), (1,)), ((), ()))
NN = (((1,), (0,)), ((), ()))


def largest_divisor(extent, most):
    return next(size for size in range(min(extent, most), 0, -1) if extent % size == 0)


def turned(block, sign):
    half = block.shape[0] // 2
    upper, lower = block[:half], block[half:]
    return jnp.concatenate([-lower, upper] if sign < 0 else [lower, -upper], axis=0)


def forward_rows(vector, near, far):
    left = jnp.concatenate([vector, turned(vector, -1)], axis=1)
    right = jnp.concatenate(
        [jnp.concatenate([part[0], part[1]], axis=1) for part in (near, far)], axis=0
    )
    return lax.dot_general(left, right, NT, preferred_element_type=F32)


def adjoint_rows(field, near, far):
    sensors = near[0].shape[0]
    total = None
    for part, piece in ((near, field[:, :sensors]), (far, field[:, sensors:])):
        left = jnp.concatenate([piece, turned(piece, 1)], axis=1)
        right = jnp.concatenate(part, axis=0)
        term = lax.dot_general(left, right, NN, preferred_element_type=F32)
        total = term if total is None else total + term
    return total


def cost(flops, moved):
    return pl.CostEstimate(flops=flops // 1000, bytes_accessed=moved // 1000, transcendentals=0)


class Plan:
    def __init__(self, operator, right_side, n_sens, n_src, chunks):
        self.freqs, _, self.sensors, self.sources = operator.shape
        self.block = right_side.shape[0]
        self.rows = right_side.shape[1] * right_side.shape[2]
        self.pairs = n_sens // 2
        self.groups = n_src // 2
        self.chunks = chunks
        self.part = self.block // chunks
        self.step = largest_divisor(self.part, 8)
        self.steps = self.part // self.step
        self.flops = 16 * self.part * self.rows * self.sensors * self.sources * 2
        self.piece = self.part * self.rows // self.groups


class Parts:
    def __init__(self, plan, chunk, m, blk_of, refs, whole):
        (near, far), (near_buf, far_buf, sems) = refs
        self.buffers, self.copies = (near_buf, far_buf), {}
        high = plan.step * 2 * plan.sensors
        for phase in range(2):
            for t in range(plan.steps):
                slot = phase * plan.steps + t
                side = m[0] ^ blk_of(phase, m)
                rows = pl.ds(t * high, high)
                near_rows = pl.ds((chunk * plan.steps + t) * high, high)
                source = near.at[side, m[1], near_rows] if whole else near.at[side, rows]
                self.copies[phase, t] = [
                    pltpu.make_async_copy(ref, buffer.at[slot], sems.at[slot, place])
                    for place, (ref, buffer) in enumerate((
                        (source, near_buf),
                        (far.at[side, rows], far_buf),
                    ))
                ]
        for copies in self.copies.values():
            for copy in copies:
                copy.start()

    def get(self, plan, phase, t):
        for copy in self.copies[phase, t]:
            copy.wait()
        slot, high = phase * plan.steps + t, plan.sensors
        return [
            tuple(
                tuple(buffer[slot, pl.ds((2 * f + c) * high, high)] for c in range(2))
                for buffer in self.buffers
            )
            for f in range(plan.step)
        ]

    @staticmethod
    def scratch(plan):
        buffer = pltpu.VMEM((2 * plan.steps, plan.step * 2 * plan.sensors, plan.sources), BF16)
        return [buffer, buffer, pltpu.SemaphoreType.DMA((2 * plan.steps, 2))]


def cut_call(plan, chunk, meta, whole, wait=()):
    def kernel(m, whole_ref, *refs):
        out_ref, buffer, sems = refs[len(wait):]
        high = plan.step * 2 * plan.sensors
        slots = [(side, t) for side in range(plan.pairs) for t in range(plan.steps)]
        ins, outs = [], []
        for slot, (side, t) in enumerate(slots):
            rows = pl.ds((chunk * plan.steps + t) * high, high)
            ins.append(pltpu.make_async_copy(
                whole_ref.at[side, 1 - m[1], rows], buffer.at[slot], sems.at[0, slot]
            ))
            outs.append(pltpu.make_async_copy(
                buffer.at[slot], out_ref.at[side, pl.ds(t * high, high)], sems.at[1, slot]
            ))
        for copy in ins:
            copy.start()
        for slot in range(len(slots)):
            ins[slot].wait()
            outs[slot].start()
        for copy in outs:
            copy.wait()

    shape = (plan.pairs, plan.part * 2 * plan.sensors, plan.sources)
    return pl.pallas_call(
        kernel,
        in_specs=[pl.BlockSpec(memory_space=pltpu.SMEM), ANYWHERE] + [ANYWHERE] * len(wait),
        out_specs=ANYWHERE,
        out_shape=jax.ShapeDtypeStruct(shape, BF16),
        scratch_shapes=[
            pltpu.VMEM((plan.pairs * plan.steps, shape[1] // plan.steps, plan.sources), BF16),
            pltpu.SemaphoreType.DMA((2, plan.pairs * plan.steps)),
        ],
        cost_estimate=cost(0, 8 * plan.part * plan.sensors * plan.sources),
        compiler_params=pltpu.CompilerParams(vmem_limit_bytes=PRODUCT_BYTES),
        name="cut",
    )(meta, whole, *wait)


def cast_call(plan, chunk, start, wait=()):
    shape = (plan.part, plan.rows, plan.sources)

    def kernel(start_ref, *refs):
        out_ref, buffer, sem = refs[len(wait):]
        rows = pl.ds(chunk * plan.part, plan.part)
        copy = pltpu.make_async_copy(start_ref.at[rows], buffer, sem)
        copy.start()
        copy.wait()
        out_ref[...] = buffer[...].astype(BF16)

    return pl.pallas_call(
        kernel,
        in_specs=[ANYWHERE] + [ANYWHERE] * len(wait),
        out_specs=pl.BlockSpec(memory_space=pltpu.VMEM),
        out_shape=jax.ShapeDtypeStruct(shape, BF16),
        scratch_shapes=[pltpu.VMEM(shape, F32), pltpu.SemaphoreType.DMA(())],
        cost_estimate=cost(0, 6 * plan.part * plan.rows * plan.sources),
        compiler_params=pltpu.CompilerParams(vmem_limit_bytes=KERNEL_BYTES),
        name="cast",
    )(start, *wait)


def forward_call(plan, chunk, meta, near, far, first, vectors, wait=()):
    n_out = 3 if first else 2
    blk_of = lambda p, m: 1 - (m[2] ^ p)

    def kernel(m, near, far, one_ref, two_ref, *refs):
        outs, scratch = refs[len(wait):len(wait) + n_out], refs[len(wait) + n_out:]
        parts = Parts(plan, chunk, m, blk_of, ((near, far), scratch[:3]), first)
        saves = []
        for phase in range(2):
            blk = blk_of(phase, m)
            for t in range(plan.steps):
                blocks = parts.get(plan, phase, t)
                if first:
                    slot, high = phase * plan.steps + t, plan.step * 2 * plan.sensors
                    saves.append(pltpu.make_async_copy(
                        scratch[0].at[slot],
                        outs[2].at[m[0] ^ blk, pl.ds(t * high, high)],
                        scratch[3].at[slot],
                    ))
                    saves[-1].start()
                for i, (near_part, far_part) in enumerate(blocks):
                    f = t * plan.step + i
                    if first:
                        vector = jnp.where(blk == 0, one_ref[f].astype(BF16), two_ref[f])
                    else:
                        vector = one_ref[blk, f].astype(F32) + two_ref[1 - blk, f].astype(F32)
                    outs[phase][f] = forward_rows(vector.astype(BF16), near_part, far_part).astype(BF16)
        for save in saves:
            save.wait()

    size = (plan.part, plan.rows, plan.sources)
    if first:
        vec_specs = [
            pl.BlockSpec(size, lambda i: (chunk, 0, 0)),
            pl.BlockSpec(size, lambda i: (0, 0, 0)),
        ]
    else:
        vec_specs = [pl.BlockSpec((2,) + size, lambda i: (0, 0, 0, 0))] * 2
    shape = (plan.part, plan.rows, 2 * plan.sensors)
    return pl.pallas_call(
        kernel,
        grid=(1,),
        in_specs=[pl.BlockSpec(memory_space=pltpu.SMEM)] + [ANYWHERE] * 2 + vec_specs
        + [ANYWHERE] * len(wait),
        out_specs=[pl.BlockSpec(shape, lambda i: (0, 0, 0))] * 2 + [ANYWHERE] * (n_out - 2),
        out_shape=[jax.ShapeDtypeStruct(shape, BF16)] * 2
        + [jax.ShapeDtypeStruct(far.shape, BF16)] * (n_out - 2),
        scratch_shapes=Parts.scratch(plan) + [pltpu.SemaphoreType.DMA((2 * plan.steps,))],
        cost_estimate=cost(plan.flops, 16 * plan.part * plan.sensors * plan.sources),
        compiler_params=pltpu.CompilerParams(vmem_limit_bytes=PRODUCT_BYTES if first else KERNEL_BYTES),
        name="forward",
    )(meta, near, far, *vectors, *wait)


def adjoint_call(plan, chunk, meta, near, far, halves, last, wait=()):
    blk_of = lambda p, m: 1 - p
    n_out = 2 if last else 1

    def kernel(m, near, far, own_ref, got_ref, *refs):
        outs, scratch = refs[len(wait):len(wait) + n_out], refs[len(wait) + n_out:]
        parts = Parts(plan, chunk, m, blk_of, ((near, far), scratch), False)
        for phase in range(2):
            blk = blk_of(phase, m)
            for t in range(plan.steps):
                for i, (near_part, far_part) in enumerate(parts.get(plan, phase, t)):
                    f = t * plan.step + i
                    field = jnp.where(blk == m[2], own_ref[f], got_ref[f])
                    back = adjoint_rows(field, near_part, far_part)
                    if last:
                        outs[phase][f] = back.astype(outs[phase].dtype)
                    else:
                        outs[0][blk, f] = back.astype(BF16)

    size = (plan.part, plan.rows, 2 * plan.sensors)
    shape = (plan.part, plan.rows, plan.sources)
    if last:
        out_specs = [pl.BlockSpec(shape, lambda i: (0, 0, 0))] * 2
        out_shape = [jax.ShapeDtypeStruct(shape, BF16), jax.ShapeDtypeStruct(shape, F32)]
    else:
        out_specs = pl.BlockSpec((2,) + shape, lambda i: (0, 0, 0, 0))
        out_shape = jax.ShapeDtypeStruct((2,) + shape, BF16)
    return pl.pallas_call(
        kernel,
        grid=(1,),
        in_specs=[pl.BlockSpec(memory_space=pltpu.SMEM)] + [ANYWHERE] * 2
        + [pl.BlockSpec(size, lambda i: (0, 0, 0))] * 2 + [ANYWHERE] * len(wait),
        out_specs=out_specs,
        out_shape=out_shape,
        scratch_shapes=Parts.scratch(plan),
        cost_estimate=cost(plan.flops, 16 * plan.part * plan.sensors * plan.sources),
        compiler_params=pltpu.CompilerParams(vmem_limit_bytes=KERNEL_BYTES),
        name="adjoint",
    )(meta, near, far, *halves, *wait)


def split_call(plan, meta, keep, got, wait=()):
    piece, groups = plan.piece, plan.groups
    width = keep.shape[-1]

    def kernel(m, keep_ref, got_ref, *refs):
        mine_ref, *sends = refs[len(wait):]
        for d in range(groups):
            place = pl.ds(pl.multiple_of((m[3] ^ d) * piece, piece), piece)
            total = keep_ref[place].astype(F32) + got_ref[place].astype(F32)
            if d == 0:
                mine_ref[...] = total
            else:
                sends[d - 1][...] = total.astype(BF16)

    whole = pl.BlockSpec(memory_space=pltpu.VMEM)
    return pl.pallas_call(
        kernel,
        in_specs=[pl.BlockSpec(memory_space=pltpu.SMEM), whole, whole] + [ANYWHERE] * len(wait),
        out_specs=[whole] * groups,
        out_shape=[jax.ShapeDtypeStruct((piece, width), F32)]
        + [jax.ShapeDtypeStruct((piece, width), BF16)] * (groups - 1),
        cost_estimate=cost(groups * piece * width, groups * piece * width * 8),
        compiler_params=pltpu.CompilerParams(vmem_limit_bytes=KERNEL_BYTES),
        name="split",
    )(meta, keep.reshape(-1, width), got.reshape(-1, width), *wait)


def place_call(plan, meta, pieces, wait=()):
    piece, groups = plan.piece, plan.groups
    width = pieces[0].shape[-1]

    def kernel(m, *refs):
        for d in range(groups):
            place = pl.ds(pl.multiple_of((m[3] ^ d) * piece, piece), piece)
            refs[-1][place] = refs[d][...]

    whole = pl.BlockSpec(memory_space=pltpu.VMEM)
    out = pl.pallas_call(
        kernel,
        in_specs=[pl.BlockSpec(memory_space=pltpu.SMEM)] + [whole] * groups
        + [ANYWHERE] * len(wait),
        out_specs=whole,
        out_shape=jax.ShapeDtypeStruct((groups * piece, width), BF16),
        cost_estimate=cost(0, groups * piece * width * 4),
        compiler_params=pltpu.CompilerParams(vmem_limit_bytes=KERNEL_BYTES),
        name="place",
    )(meta, *pieces, *wait)
    return out.reshape(plan.part, plan.rows, width)


def ordered(array, *earlier):
    def kernel(*refs):
        del refs

    return pl.pallas_call(
        kernel,
        in_specs=[ANYWHERE] * (1 + len(earlier)),
        out_specs=ANYWHERE,
        out_shape=jax.ShapeDtypeStruct(array.shape, array.dtype),
        input_output_aliases={0: 0},
        cost_estimate=cost(0, 0),
        compiler_params=pltpu.CompilerParams(vmem_limit_bytes=KERNEL_BYTES),
        name="ordered",
    )(array, *earlier)


def lanes(array):
    total = jnp.sum(array.reshape(-1, 8, array.shape[-1]), axis=0)
    return sum(total[:, i:i + 128] for i in range(0, array.shape[-1], 128))


def sensor_call(
    plan, chunk, meta, weights, pieces, norms, alpha=None, damping=None, old=None, wait=()
):
    piece, rows, groups = plan.piece, plan.rows, plan.groups
    width = pieces[0].shape[-1]
    count = max(1, piece // rows)
    high = piece // count
    second = old is not None

    def kernel(m, *refs):
        if second:
            alpha_ref, damp_ref, old_ref, *refs = refs
        weights_ref, norms_ref, *refs = refs
        ins, (out_ref, *more) = refs[:groups], refs[groups + len(wait):]
        stats_ref = more[-1]
        square = cross = jnp.zeros((8, 128), F32)
        for c in range(count):
            at = pl.ds(c * high, high)
            freq = chunk * plan.part + (m[3] * piece + c * high) // rows
            field = ins[0][at]
            for ref in ins[1:]:
                field = field + ref[at].astype(F32)
            if second:
                factor = 1.0 - alpha_ref[0] * damp_ref[freq]
                field = factor * old_ref[at] - alpha_ref[0] * field
            scaled = weights_ref[pl.ds(freq, 1)] * field
            out_ref[at] = scaled.astype(BF16)
            square = square + lanes(scaled * field)
            if second:
                cross = cross + lanes(scaled * old_ref[at])
            else:
                more[0][at] = field
        stats_ref[0:8] = norms_ref[0:8]
        stats_ref[8:16] = norms_ref[8:16] + square
        stats_ref[16:24] = norms_ref[16:24] + cross

    whole = pl.BlockSpec(memory_space=pltpu.VMEM)
    scalars = pl.BlockSpec(memory_space=pltpu.SMEM)
    first_out = [] if second else [jax.ShapeDtypeStruct((piece, width), F32)]
    extra = (alpha, damping, old) if second else ()
    out_shape = [jax.ShapeDtypeStruct((piece, width), BF16)] + first_out
    out_shape = out_shape + [jax.ShapeDtypeStruct((24, 128), F32)]
    return pl.pallas_call(
        kernel,
        in_specs=[scalars] + ([scalars] * 2 + [whole] if second else []) + [whole] * (2 + groups)
        + [ANYWHERE] * len(wait),
        out_specs=[whole] * len(out_shape),
        out_shape=out_shape,
        cost_estimate=cost(8 * piece * width, 16 * piece * width),
        compiler_params=pltpu.CompilerParams(vmem_limit_bytes=KERNEL_BYTES),
        name="sensor",
    )(meta, *extra, weights, norms, *pieces, *wait)


def norms_call(plan, chunk, damping, start):
    block = (plan.part, plan.rows, plan.sources)

    def kernel(damp_ref, start_ref, stats_ref):
        plain = damped = jnp.zeros((8, 128), F32)
        for f in range(plan.part):
            term = lanes(start_ref[f] * start_ref[f])
            plain = plain + term
            damped = damped + damp_ref[chunk * plan.part + f] * term
        stats_ref[0:8] = plain
        stats_ref[8:16] = damped
        stats_ref[16:24] = jnp.zeros((8, 128), F32)

    return pl.pallas_call(
        kernel,
        grid=(1,),
        in_specs=[
            pl.BlockSpec(memory_space=pltpu.SMEM),
            pl.BlockSpec(block, lambda i: (chunk, 0, 0)),
        ],
        out_specs=pl.BlockSpec((24, 128), lambda i: (0, 0)),
        out_shape=jax.ShapeDtypeStruct((24, 128), F32),
        cost_estimate=cost(2 * start.size, 4 * start.size),
        compiler_params=pltpu.CompilerParams(vmem_limit_bytes=KERNEL_BYTES),
        name="norms",
    )(damping, start)


def residual_call(plan, chunk, alpha, damping, start, mine, got):
    part, rows, sources = plan.part, plan.rows, plan.sources

    def kernel(alpha_ref, damp_ref, start_ref, mine_ref, got_ref, image_ref, out_ref, stats_ref):
        plain = damped = mixed = jnp.zeros((8, 128), F32)
        for f in range(part):
            damp = damp_ref[chunk * part + f]
            begin = start_ref[f]
            image = mine_ref[f].astype(F32) + got_ref[f].astype(F32) + damp * begin
            residual = begin - alpha_ref[0] * image
            image_ref[f] = image
            out_ref[f] = residual
            term = lanes(residual * residual)
            plain = plain + term
            damped = damped + damp * term
            mixed = mixed + damp * lanes(residual * begin)
        stats_ref[0:8] = plain
        stats_ref[8:16] = damped
        stats_ref[16:24] = mixed

    block = (part, rows, sources)
    scalars = pl.BlockSpec(memory_space=pltpu.SMEM)
    out = jax.ShapeDtypeStruct(block, F32)
    return pl.pallas_call(
        kernel,
        grid=(1,),
        in_specs=[
            scalars,
            scalars,
            pl.BlockSpec(block, lambda i: (chunk, 0, 0)),
            pl.BlockSpec((None,) + block, lambda i: (0, 0, 0, 0)),
            pl.BlockSpec((None,) + block, lambda i: (1, 0, 0, 0)),
        ],
        out_specs=[
            pl.BlockSpec(block, lambda i: (0, 0, 0)),
            pl.BlockSpec(block, lambda i: (0, 0, 0)),
            pl.BlockSpec((24, 128), lambda i: (0, 0)),
        ],
        out_shape=[out, out, jax.ShapeDtypeStruct((24, 128), F32)],
        cost_estimate=cost(8 * part * rows * sources, 16 * part * rows * sources),
        compiler_params=pltpu.CompilerParams(vmem_limit_bytes=KERNEL_BYTES),
        name="residual",
    )(alpha, damping, start, mine, got)


def body(n_sens, n_src, operator, right_side, noise_weights, damping):
    plan = Plan(operator, right_side, n_sens, n_src, CHUNKS)
    sens, src = lax.axis_index("sens"), lax.axis_index("src")
    pair, core, half, group = sens // 2, sens % 2, src % 2, src // 2
    meta = jnp.stack([pair, core, half, group]).astype(jnp.int32)
    part, rows, block = plan.part, plan.rows, plan.block
    levels = range(n_src.bit_length() - 1)
    chunks = range(plan.chunks)

    def to_core(array):
        return lax.ppermute(array, "sens", [(i, i ^ 1) for i in range(n_sens)])

    def to_pair(array):
        return lax.ppermute(array, "sens", [(i, i ^ 2) for i in range(n_sens)])

    def to_src(array, step):
        return lax.ppermute(array, "src", [(j, j ^ step) for j in range(n_src)])

    def in_turn(arrays, move):
        moved = []
        for k, array in enumerate(arrays):
            if k > 0:
                array = arrays[k] = ordered(array, moved[-1])
            moved.append(move(array))
        return moved

    def total_near(sums):
        sums = sums + to_src(sums, 1)
        return sums + to_pair(sums)

    def total_far(sums):
        sums = sums + to_core(sums)
        for level in levels[1:]:
            sums = sums + to_src(sums, 1 << level)
        return sums, jnp.sum(sums.reshape(-1, 8 * 128), axis=1)

    def double(table, level):
        other = to_src(table, 1 << level)
        low = (src >> level) % 2 == 0
        return jnp.concatenate([jnp.where(low, table, other), jnp.where(low, other, table)], axis=0)

    whole = operator.reshape(plan.pairs, 2, block * 2 * plan.sensors, plan.sources)
    start = right_side.reshape(block, rows, plan.sources)

    casts = [cast_call(plan, k, start) for k in chunks]
    cuts = [cut_call(plan, k, meta, whole, (casts[0],)) for k in chunks]
    got_b = in_turn(list(casts), to_pair)
    weights = noise_weights
    for level in levels[:2]:
        weights = double(weights, level)
    far, pairs = [to_core(cut) for cut in cuts], []
    for k in chunks:
        wait = tuple(casts[1:]) + tuple(cuts[1:]) + (weights,) if k == 0 else ()
        pairs.append(forward_call(plan, k, meta, whole, far[k], True, (start, got_b[k]), wait))

    for level in levels[2:]:
        weights = double(weights, level)
    weights = weights.reshape(plan.pairs, 2, block, plan.sensors)
    weights_near = lax.dynamic_index_in_dim(weights, core, 1, keepdims=False)
    weights_far = to_core(lax.dynamic_index_in_dim(weights, 1 - core, 1, keepdims=False))
    weights = jnp.concatenate([weights_near, weights_far], axis=-1)
    weights = lax.dynamic_index_in_dim(weights, pair ^ half, 0, keepdims=False)
    damping_row = jnp.where(half == 0, damping, to_pair(damping))
    steps = [2 * d for d in range(1, plan.groups)]

    def reduce_field(keep, got, wait=()):
        mine, *sends = split_call(plan, meta, keep, got, wait)
        return [mine] + [to_src(piece, step) for piece, step in zip(sends, steps)]

    def to_half(array):
        return to_src(array, 1)

    def both_products(scaled, near_sums, last, then):
        outs, wait, sums = [], (), None
        for k in chunks:
            pieces = [scaled[k]] + [to_src(scaled[k], step) for step in steps]
            own = place_call(plan, meta, pieces, wait)
            halves = (own, to_half(own))
            if k == 1:
                after = outs[0][1][0]
                far_sums, sums = total_far(near_sums if last else ordered(near_sums, after))
                wait = (after, far_sums)
            out = adjoint_call(plan, k, meta, near[k], far[k], halves, last, wait if k > 0 else ())
            outs.append((out, then(k, out)))
            wait = (out[0] if last else out, near_sums)
        return outs, total_far(near_sums)[1] if sums is None else sums

    sends, near = [each[0] for each in pairs], [each[2] for each in pairs]
    got = in_turn(sends, to_half)
    pieces = [reduce_field(pairs[k][1], got[k], tuple(sends[k + 1:k + 2])) for k in chunks]
    scaled, field, stats = zip(*[
        sensor_call(
            plan, k, meta, weights, pieces[k], norms_call(plan, k, damping, start),
            wait=tuple(got[k + 1:k + 2]),
        )
        for k in chunks
    ])
    near_0 = total_near(sum(stats))

    def go_on(k, back):
        got = to_pair(back)
        send, keep = forward_call(plan, k, meta, near[k], far[k], False, (back, got))
        return send, keep, got

    outs, sums = both_products(scaled, near_0, False, go_on)
    norm_0, curve_0 = sums[0], sums[1]
    alpha_0 = (norm_0 / curve_0)[None]
    back = [out for out, _ in outs]
    sends, keeps, got_back = zip(*[rest for _, rest in outs])
    got = in_turn(list(sends), to_half)
    image_0, residual, norms = zip(*[
        residual_call(plan, k, alpha_0, damping, start, back[k], got_back[k]) for k in chunks
    ])
    pieces = [reduce_field(keeps[k], got[k], (norms[k],)) for k in chunks]
    scaled, stats = zip(*[
        sensor_call(plan, k, meta, weights, pieces[k], norms[k], alpha_0, damping_row, field[k])
        for k in chunks
    ])
    near_1 = total_near(sum(stats))
    outs, sums = both_products(scaled, near_1, True, lambda k, out: (to_pair(out[0]),))
    norm_1 = sums[0]
    beta = norm_1 / norm_0
    curve_1 = sums[1] + 2.0 * beta * sums[2] + beta * beta * curve_0
    alpha_1 = norm_1 / curve_1

    final = [mine + rest[0].astype(F32) for (_, mine), rest in outs]
    residual, image_0 = jnp.concatenate(residual), jnp.concatenate(image_0)
    image_1 = jnp.concatenate(final) + damping[:, None, None] * residual + beta * image_0
    solution = alpha_0 * start + alpha_1 * (residual + beta * start)
    residual = residual - alpha_1 * image_1
    return solution.reshape(right_side.shape), residual.reshape(right_side.shape)


def solution(mesh):
    in_specs = (
        P(None, None, "sens", "src"),
        P("sens", None, None, "src"),
        P("src", "sens"),
        P("sens"),
    )
    out_specs = (P("sens", None, None, "src"), P("sens", None, None, "src"))
    shard = functools.partial(body, mesh.shape["sens"], mesh.shape["src"])
    return jax.shard_map(shard, mesh=mesh, in_specs=in_specs, out_specs=out_specs, check_vma=False)
```

```python
import functools

import jax
import jax.numpy as jnp
from jax import lax
from jax.experimental import pallas as pl
from jax.experimental.pallas import tpu as pltpu
from jax.sharding import PartitionSpec as P

CHUNKS = 2
KERNEL_BYTES = 16 * 2 ** 20
PRODUCT_BYTES = 56 * 2 ** 20
F32 = jnp.float32
BF16 = jnp.bfloat16
ANYWHERE = pl.BlockSpec(memory_space=pl.ANY)
NT = (((1,), (1,)), ((), ()))
NN = (((1,), (0,)), ((), ()))


def largest_divisor(extent, most):
    return next(size for size in range(min(extent, most), 0, -1) if extent % size == 0)


def turned(block, sign):
    half = block.shape[0] // 2
    upper, lower = block[:half], block[half:]
    return jnp.concatenate([-lower, upper] if sign < 0 else [lower, -upper], axis=0)


def forward_rows(vector, near, far):
    left = jnp.concatenate([vector, turned(vector, -1)], axis=1)
    right = jnp.concatenate(
        [jnp.concatenate([part[0], part[1]], axis=1) for part in (near, far)], axis=0
    )
    return lax.dot_general(left, right, NT, preferred_element_type=F32)


def adjoint_rows(field, near, far):
    sensors = near[0].shape[0]
    total = None
    for part, piece in ((near, field[:, :sensors]), (far, field[:, sensors:])):
        left = jnp.concatenate([piece, turned(piece, 1)], axis=1)
        right = jnp.concatenate(part, axis=0)
        term = lax.dot_general(left, right, NN, preferred_element_type=F32)
        total = term if total is None else total + term
    return total


def cost(flops, moved):
    return pl.CostEstimate(flops=flops // 1000, bytes_accessed=moved // 1000, transcendentals=0)


class Plan:
    def __init__(self, operator, right_side, n_sens, n_src, chunks):
        self.freqs, _, self.sensors, self.sources = operator.shape
        self.block = right_side.shape[0]
        self.rows = right_side.shape[1] * right_side.shape[2]
        self.pairs = n_sens // 2
        self.groups = n_src // 2
        self.chunks = chunks
        self.part = self.block // chunks
        self.step = largest_divisor(self.part, 8)
        self.steps = self.part // self.step
        self.flops = 16 * self.part * self.rows * self.sensors * self.sources * 2
        self.piece = self.part * self.rows // self.groups


class Parts:
    def __init__(self, plan, chunk, m, blk_of, refs, whole):
        (near, far), (near_buf, far_buf, sems) = refs
        self.buffers, self.copies = (near_buf, far_buf), {}
        high = plan.step * 2 * plan.sensors
        for phase in range(2):
            for t in range(plan.steps):
                slot = phase * plan.steps + t
                side = m[0] ^ blk_of(phase, m)
                rows = pl.ds(t * high, high)
                near_rows = pl.ds((chunk * plan.steps + t) * high, high)
                source = near.at[side, m[1], near_rows] if whole else near.at[side, rows]
                self.copies[phase, t] = [
                    pltpu.make_async_copy(ref, buffer.at[slot], sems.at[slot, place])
                    for place, (ref, buffer) in enumerate((
                        (source, near_buf),
                        (far.at[side, rows], far_buf),
                    ))
                ]
        for copies in self.copies.values():
            for copy in copies:
                copy.start()

    def get(self, plan, phase, t):
        for copy in self.copies[phase, t]:
            copy.wait()
        slot, high = phase * plan.steps + t, plan.sensors
        return [
            tuple(
                tuple(buffer[slot, pl.ds((2 * f + c) * high, high)] for c in range(2))
                for buffer in self.buffers
            )
            for f in range(plan.step)
        ]

    @staticmethod
    def scratch(plan):
        buffer = pltpu.VMEM((2 * plan.steps, plan.step * 2 * plan.sensors, plan.sources), BF16)
        return [buffer, buffer, pltpu.SemaphoreType.DMA((2 * plan.steps, 2))]


def cut_call(plan, chunk, meta, whole, wait=()):
    def kernel(m, whole_ref, *refs):
        out_ref, buffer, sems = refs[len(wait):]
        high = plan.step * 2 * plan.sensors
        slots = [(side, t) for side in range(plan.pairs) for t in range(plan.steps)]
        ins, outs = [], []
        for slot, (side, t) in enumerate(slots):
            rows = pl.ds((chunk * plan.steps + t) * high, high)
            ins.append(pltpu.make_async_copy(
                whole_ref.at[side, 1 - m[1], rows], buffer.at[slot], sems.at[0, slot]
            ))
            outs.append(pltpu.make_async_copy(
                buffer.at[slot], out_ref.at[side, pl.ds(t * high, high)], sems.at[1, slot]
            ))
        for copy in ins:
            copy.start()
        for slot in range(len(slots)):
            ins[slot].wait()
            outs[slot].start()
        for copy in outs:
            copy.wait()

    shape = (plan.pairs, plan.part * 2 * plan.sensors, plan.sources)
    return pl.pallas_call(
        kernel,
        in_specs=[pl.BlockSpec(memory_space=pltpu.SMEM), ANYWHERE] + [ANYWHERE] * len(wait),
        out_specs=ANYWHERE,
        out_shape=jax.ShapeDtypeStruct(shape, BF16),
        scratch_shapes=[
            pltpu.VMEM((plan.pairs * plan.steps, shape[1] // plan.steps, plan.sources), BF16),
            pltpu.SemaphoreType.DMA((2, plan.pairs * plan.steps)),
        ],
        cost_estimate=cost(0, 8 * plan.part * plan.sensors * plan.sources),
        compiler_params=pltpu.CompilerParams(vmem_limit_bytes=PRODUCT_BYTES),
        name="cut",
    )(meta, whole, *wait)


def cast_call(plan, chunk, start, wait=()):
    shape = (plan.part, plan.rows, plan.sources)

    def kernel(start_ref, *refs):
        out_ref, buffer, sem = refs[len(wait):]
        rows = pl.ds(chunk * plan.part, plan.part)
        copy = pltpu.make_async_copy(start_ref.at[rows], buffer, sem)
        copy.start()
        copy.wait()
        out_ref[...] = buffer[...].astype(BF16)

    return pl.pallas_call(
        kernel,
        in_specs=[ANYWHERE] + [ANYWHERE] * len(wait),
        out_specs=pl.BlockSpec(memory_space=pltpu.VMEM),
        out_shape=jax.ShapeDtypeStruct(shape, BF16),
        scratch_shapes=[pltpu.VMEM(shape, F32), pltpu.SemaphoreType.DMA(())],
        cost_estimate=cost(0, 6 * plan.part * plan.rows * plan.sources),
        compiler_params=pltpu.CompilerParams(vmem_limit_bytes=KERNEL_BYTES),
        name="cast",
    )(start, *wait)


def forward_call(plan, chunk, meta, near, far, first, vectors, wait=()):
    n_out = 3 if first else 2
    blk_of = lambda p, m: 1 - (m[2] ^ p)

    def kernel(m, near, far, one_ref, two_ref, *refs):
        outs, scratch = refs[len(wait):len(wait) + n_out], refs[len(wait) + n_out:]
        parts = Parts(plan, chunk, m, blk_of, ((near, far), scratch[:3]), first)
        saves = []
        for phase in range(2):
            blk = blk_of(phase, m)
            for t in range(plan.steps):
                blocks = parts.get(plan, phase, t)
                if first:
                    slot, high = phase * plan.steps + t, plan.step * 2 * plan.sensors
                    saves.append(pltpu.make_async_copy(
                        scratch[0].at[slot],
                        outs[2].at[m[0] ^ blk, pl.ds(t * high, high)],
                        scratch[3].at[slot],
                    ))
                    saves[-1].start()
                for i, (near_part, far_part) in enumerate(blocks):
                    f = t * plan.step + i
                    if first:
                        vector = jnp.where(blk == 0, one_ref[f].astype(BF16), two_ref[f])
                    else:
                        vector = one_ref[blk, f].astype(F32) + two_ref[1 - blk, f].astype(F32)
                    outs[phase][f] = forward_rows(vector.astype(BF16), near_part, far_part).astype(BF16)
        for save in saves:
            save.wait()

    size = (plan.part, plan.rows, plan.sources)
    if first:
        vec_specs = [
            pl.BlockSpec(size, lambda i: (chunk, 0, 0)),
            pl.BlockSpec(size, lambda i: (0, 0, 0)),
        ]
    else:
        vec_specs = [pl.BlockSpec((2,) + size, lambda i: (0, 0, 0, 0))] * 2
    shape = (plan.part, plan.rows, 2 * plan.sensors)
    return pl.pallas_call(
        kernel,
        grid=(1,),
        in_specs=[pl.BlockSpec(memory_space=pltpu.SMEM)] + [ANYWHERE] * 2 + vec_specs
        + [ANYWHERE] * len(wait),
        out_specs=[pl.BlockSpec(shape, lambda i: (0, 0, 0))] * 2 + [ANYWHERE] * (n_out - 2),
        out_shape=[jax.ShapeDtypeStruct(shape, BF16)] * 2
        + [jax.ShapeDtypeStruct(far.shape, BF16)] * (n_out - 2),
        scratch_shapes=Parts.scratch(plan) + [pltpu.SemaphoreType.DMA((2 * plan.steps,))],
        cost_estimate=cost(plan.flops, 16 * plan.part * plan.sensors * plan.sources),
        compiler_params=pltpu.CompilerParams(vmem_limit_bytes=PRODUCT_BYTES if first else KERNEL_BYTES),
        name="forward",
    )(meta, near, far, *vectors, *wait)


def adjoint_call(plan, chunk, meta, near, far, halves, last, wait=()):
    blk_of = lambda p, m: 1 - p
    n_out = 2 if last else 1

    def kernel(m, near, far, own_ref, got_ref, *refs):
        outs, scratch = refs[len(wait):len(wait) + n_out], refs[len(wait) + n_out:]
        parts = Parts(plan, chunk, m, blk_of, ((near, far), scratch), False)
        for phase in range(2):
            blk = blk_of(phase, m)
            for t in range(plan.steps):
                for i, (near_part, far_part) in enumerate(parts.get(plan, phase, t)):
                    f = t * plan.step + i
                    field = jnp.where(blk == m[2], own_ref[f], got_ref[f])
                    back = adjoint_rows(field, near_part, far_part)
                    if last:
                        outs[phase][f] = back.astype(outs[phase].dtype)
                    else:
                        outs[0][blk, f] = back.astype(BF16)

    size = (plan.part, plan.rows, 2 * plan.sensors)
    shape = (plan.part, plan.rows, plan.sources)
    if last:
        out_specs = [pl.BlockSpec(shape, lambda i: (0, 0, 0))] * 2
        out_shape = [jax.ShapeDtypeStruct(shape, BF16), jax.ShapeDtypeStruct(shape, F32)]
    else:
        out_specs = pl.BlockSpec((2,) + shape, lambda i: (0, 0, 0, 0))
        out_shape = jax.ShapeDtypeStruct((2,) + shape, BF16)
    return pl.pallas_call(
        kernel,
        grid=(1,),
        in_specs=[pl.BlockSpec(memory_space=pltpu.SMEM)] + [ANYWHERE] * 2
        + [pl.BlockSpec(size, lambda i: (0, 0, 0))] * 2 + [ANYWHERE] * len(wait),
        out_specs=out_specs,
        out_shape=out_shape,
        scratch_shapes=Parts.scratch(plan),
        cost_estimate=cost(plan.flops, 16 * plan.part * plan.sensors * plan.sources),
        compiler_params=pltpu.CompilerParams(vmem_limit_bytes=KERNEL_BYTES),
        name="adjoint",
    )(meta, near, far, *halves, *wait)


def split_call(plan, meta, keep, got, wait=()):
    piece, groups = plan.piece, plan.groups
    width = keep.shape[-1]

    def kernel(m, keep_ref, got_ref, *refs):
        mine_ref, *sends = refs[len(wait):]
        for d in range(groups):
            place = pl.ds(pl.multiple_of((m[3] ^ d) * piece, piece), piece)
            total = keep_ref[place].astype(F32) + got_ref[place].astype(F32)
            if d == 0:
                mine_ref[...] = total
            else:
                sends[d - 1][...] = total.astype(BF16)

    whole = pl.BlockSpec(memory_space=pltpu.VMEM)
    return pl.pallas_call(
        kernel,
        in_specs=[pl.BlockSpec(memory_space=pltpu.SMEM), whole, whole] + [ANYWHERE] * len(wait),
        out_specs=[whole] * groups,
        out_shape=[jax.ShapeDtypeStruct((piece, width), F32)]
        + [jax.ShapeDtypeStruct((piece, width), BF16)] * (groups - 1),
        cost_estimate=cost(groups * piece * width, groups * piece * width * 8),
        compiler_params=pltpu.CompilerParams(vmem_limit_bytes=KERNEL_BYTES),
        name="split",
    )(meta, keep.reshape(-1, width), got.reshape(-1, width), *wait)


def place_call(plan, meta, pieces, wait=()):
    piece, groups = plan.piece, plan.groups
    width = pieces[0].shape[-1]

    def kernel(m, *refs):
        for d in range(groups):
            place = pl.ds(pl.multiple_of((m[3] ^ d) * piece, piece), piece)
            refs[-1][place] = refs[d][...]

    whole = pl.BlockSpec(memory_space=pltpu.VMEM)
    out = pl.pallas_call(
        kernel,
        in_specs=[pl.BlockSpec(memory_space=pltpu.SMEM)] + [whole] * groups
        + [ANYWHERE] * len(wait),
        out_specs=whole,
        out_shape=jax.ShapeDtypeStruct((groups * piece, width), BF16),
        cost_estimate=cost(0, groups * piece * width * 4),
        compiler_params=pltpu.CompilerParams(vmem_limit_bytes=KERNEL_BYTES),
        name="place",
    )(meta, *pieces, *wait)
    return out.reshape(plan.part, plan.rows, width)


def ordered(array, *earlier):
    def kernel(*refs):
        del refs

    return pl.pallas_call(
        kernel,
        in_specs=[ANYWHERE] * (1 + len(earlier)),
        out_specs=ANYWHERE,
        out_shape=jax.ShapeDtypeStruct(array.shape, array.dtype),
        input_output_aliases={0: 0},
        cost_estimate=cost(0, 0),
        compiler_params=pltpu.CompilerParams(vmem_limit_bytes=KERNEL_BYTES),
        name="ordered",
    )(array, *earlier)


def lanes(array):
    total = jnp.sum(array.reshape(-1, 8, array.shape[-1]), axis=0)
    return sum(total[:, i:i + 128] for i in range(0, array.shape[-1], 128))


def sensor_call(
    plan, chunk, meta, weights, pieces, norms, alpha=None, damping=None, old=None, wait=()
):
    piece, rows, groups = plan.piece, plan.rows, plan.groups
    width = pieces[0].shape[-1]
    count = max(1, piece // rows)
    high = piece // count
    second = old is not None

    def kernel(m, *refs):
        if second:
            alpha_ref, damp_ref, old_ref, *refs = refs
        weights_ref, norms_ref, *refs = refs
        ins, (out_ref, *more) = refs[:groups], refs[groups + len(wait):]
        stats_ref = more[-1]
        square = cross = jnp.zeros((8, 128), F32)
        for c in range(count):
            at = pl.ds(c * high, high)
            freq = chunk * plan.part + (m[3] * piece + c * high) // rows
            field = ins[0][at]
            for ref in ins[1:]:
                field = field + ref[at].astype(F32)
            if second:
                factor = 1.0 - alpha_ref[0] * damp_ref[freq]
                field = factor * old_ref[at] - alpha_ref[0] * field
            scaled = weights_ref[pl.ds(freq, 1)] * field
            out_ref[at] = scaled.astype(BF16)
            square = square + lanes(scaled * field)
            if second:
                cross = cross + lanes(scaled * old_ref[at])
            else:
                more[0][at] = field
        stats_ref[0:8] = norms_ref[0:8]
        stats_ref[8:16] = norms_ref[8:16] + square
        stats_ref[16:24] = norms_ref[16:24] + cross

    whole = pl.BlockSpec(memory_space=pltpu.VMEM)
    scalars = pl.BlockSpec(memory_space=pltpu.SMEM)
    first_out = [] if second else [jax.ShapeDtypeStruct((piece, width), F32)]
    extra = (alpha, damping, old) if second else ()
    out_shape = [jax.ShapeDtypeStruct((piece, width), BF16)] + first_out
    out_shape = out_shape + [jax.ShapeDtypeStruct((24, 128), F32)]
    return pl.pallas_call(
        kernel,
        in_specs=[scalars] + ([scalars] * 2 + [whole] if second else []) + [whole] * (2 + groups)
        + [ANYWHERE] * len(wait),
        out_specs=[whole] * len(out_shape),
        out_shape=out_shape,
        cost_estimate=cost(8 * piece * width, 16 * piece * width),
        compiler_params=pltpu.CompilerParams(vmem_limit_bytes=KERNEL_BYTES),
        name="sensor",
    )(meta, *extra, weights, norms, *pieces, *wait)


def norms_call(plan, chunk, damping, start):
    block = (plan.part, plan.rows, plan.sources)

    def kernel(damp_ref, start_ref, stats_ref):
        plain = damped = jnp.zeros((8, 128), F32)
        for f in range(plan.part):
            term = lanes(start_ref[f] * start_ref[f])
            plain = plain + term
            damped = damped + damp_ref[chunk * plan.part + f] * term
        stats_ref[0:8] = plain
        stats_ref[8:16] = damped
        stats_ref[16:24] = jnp.zeros((8, 128), F32)

    return pl.pallas_call(
        kernel,
        grid=(1,),
        in_specs=[
            pl.BlockSpec(memory_space=pltpu.SMEM),
            pl.BlockSpec(block, lambda i: (chunk, 0, 0)),
        ],
        out_specs=pl.BlockSpec((24, 128), lambda i: (0, 0)),
        out_shape=jax.ShapeDtypeStruct((24, 128), F32),
        cost_estimate=cost(2 * start.size, 4 * start.size),
        compiler_params=pltpu.CompilerParams(vmem_limit_bytes=KERNEL_BYTES),
        name="norms",
    )(damping, start)


def residual_call(plan, chunk, alpha, damping, start, mine, got):
    part, rows, sources = plan.part, plan.rows, plan.sources

    def kernel(alpha_ref, damp_ref, start_ref, mine_ref, got_ref, image_ref, out_ref, stats_ref):
        plain = damped = mixed = jnp.zeros((8, 128), F32)
        for f in range(part):
            damp = damp_ref[chunk * part + f]
            begin = start_ref[f]
            image = mine_ref[f].astype(F32) + got_ref[f].astype(F32) + damp * begin
            residual = begin - alpha_ref[0] * image
            image_ref[f] = image
            out_ref[f] = residual
            term = lanes(residual * residual)
            plain = plain + term
            damped = damped + damp * term
            mixed = mixed + damp * lanes(residual * begin)
        stats_ref[0:8] = plain
        stats_ref[8:16] = damped
        stats_ref[16:24] = mixed

    block = (part, rows, sources)
    scalars = pl.BlockSpec(memory_space=pltpu.SMEM)
    out = jax.ShapeDtypeStruct(block, F32)
    return pl.pallas_call(
        kernel,
        grid=(1,),
        in_specs=[
            scalars,
            scalars,
            pl.BlockSpec(block, lambda i: (chunk, 0, 0)),
            pl.BlockSpec((None,) + block, lambda i: (0, 0, 0, 0)),
            pl.BlockSpec((None,) + block, lambda i: (1, 0, 0, 0)),
        ],
        out_specs=[
            pl.BlockSpec(block, lambda i: (0, 0, 0)),
            pl.BlockSpec(block, lambda i: (0, 0, 0)),
            pl.BlockSpec((24, 128), lambda i: (0, 0)),
        ],
        out_shape=[out, out, jax.ShapeDtypeStruct((24, 128), F32)],
        cost_estimate=cost(8 * part * rows * sources, 16 * part * rows * sources),
        compiler_params=pltpu.CompilerParams(vmem_limit_bytes=KERNEL_BYTES),
        name="residual",
    )(alpha, damping, start, mine, got)


def body(n_sens, n_src, operator, right_side, noise_weights, damping):
    plan = Plan(operator, right_side, n_sens, n_src, CHUNKS)
    sens, src = lax.axis_index("sens"), lax.axis_index("src")
    pair, core, half, group = sens // 2, sens % 2, src % 2, src // 2
    meta = jnp.stack([pair, core, half, group]).astype(jnp.int32)
    part, rows, block = plan.part, plan.rows, plan.block
    levels = range(n_src.bit_length() - 1)
    chunks = range(plan.chunks)

    def to_core(array):
        return lax.ppermute(array, "sens", [(i, i ^ 1) for i in range(n_sens)])

    def to_pair(array):
        return lax.ppermute(array, "sens", [(i, i ^ 2) for i in range(n_sens)])

    def to_src(array, step):
        return lax.ppermute(array, "src", [(j, j ^ step) for j in range(n_src)])

    def in_turn(arrays, move):
        moved = []
        for k, array in enumerate(arrays):
            if k > 0:
                array = arrays[k] = ordered(array, moved[-1])
            moved.append(move(array))
        return moved

    def total_near(sums, last):
        sums = sums + (to_src(sums, 1) if last else to_core(sums))
        sums = sums + to_pair(sums)
        return sums if last else sums + to_src(sums, 1)

    def total_far(sums, last):
        if last:
            sums = sums + to_core(sums)
        for level in levels[1:]:
            sums = sums + to_src(sums, 1 << level)
        return sums, jnp.sum(sums.reshape(-1, 8 * 128), axis=1)

    def double(table, level):
        other = to_src(table, 1 << level)
        low = (src >> level) % 2 == 0
        return jnp.concatenate([jnp.where(low, table, other), jnp.where(low, other, table)], axis=0)

    whole = operator.reshape(plan.pairs, 2, block * 2 * plan.sensors, plan.sources)
    start = right_side.reshape(block, rows, plan.sources)

    casts = [cast_call(plan, k, start) for k in chunks]
    cuts = [cut_call(plan, k, meta, whole) for k in chunks]
    got_b = in_turn(list(casts), to_pair)
    weights = noise_weights
    for level in levels[:2]:
        weights = double(weights, level)
    far, pairs = [to_core(cut) for cut in cuts], []
    for k in chunks:
        wait = tuple(casts[1:]) + tuple(cuts[1:]) + (weights,) if k == 0 else ()
        pairs.append(forward_call(plan, k, meta, whole, far[k], True, (start, got_b[k]), wait))

    for level in levels[2:]:
        weights = double(weights, level)
    weights = weights.reshape(plan.pairs, 2, block, plan.sensors)
    weights_near = lax.dynamic_index_in_dim(weights, core, 1, keepdims=False)
    weights_far = to_core(lax.dynamic_index_in_dim(weights, 1 - core, 1, keepdims=False))
    weights = jnp.concatenate([weights_near, weights_far], axis=-1)
    weights = lax.dynamic_index_in_dim(weights, pair ^ half, 0, keepdims=False)
    damping_row = jnp.where(half == 0, damping, to_pair(damping))
    steps = [2 * d for d in range(1, plan.groups)]

    def reduce_field(keep, got, wait=()):
        mine, *sends = split_call(plan, meta, keep, got, wait)
        return [mine] + [to_src(piece, step) for piece, step in zip(sends, steps)]

    def to_half(array):
        return to_src(array, 1)

    def both_products(scaled, near_sums, last, then):
        outs, wait, sums = [], (), None
        for k in chunks:
            pieces = [scaled[k]] + [to_src(scaled[k], step) for step in steps]
            own = place_call(plan, meta, pieces, wait)
            halves = (own, to_half(own))
            if k == 1:
                after = outs[0][1][0]
                far_sums, sums = total_far(near_sums if last else ordered(near_sums, after), last)
                wait = (after, far_sums)
            out = adjoint_call(plan, k, meta, near[k], far[k], halves, last, wait if k > 0 else ())
            outs.append((out, then(k, out)))
            wait = (out[0] if last else out, near_sums)
        return outs, total_far(near_sums, last)[1] if sums is None else sums

    sends, near = [each[0] for each in pairs], [each[2] for each in pairs]
    got = in_turn(sends, to_half)
    pieces = [reduce_field(pairs[k][1], got[k], tuple(sends[k + 1:k + 2])) for k in chunks]
    scaled, field, stats = zip(*[
        sensor_call(
            plan, k, meta, weights, pieces[k], norms_call(plan, k, damping, start),
            wait=tuple(got[k + 1:k + 2]),
        )
        for k in chunks
    ])
    near_0 = total_near(sum(stats), False)

    def go_on(k, back):
        got = to_pair(back)
        send, keep = forward_call(plan, k, meta, near[k], far[k], False, (back, got))
        return send, keep, got

    outs, sums = both_products(scaled, near_0, False, go_on)
    norm_0, curve_0 = sums[0], sums[1]
    alpha_0 = (norm_0 / curve_0)[None]
    back = [out for out, _ in outs]
    sends, keeps, got_back = zip(*[rest for _, rest in outs])
    got = in_turn(list(sends), to_half)
    image_0, residual, norms = zip(*[
        residual_call(plan, k, alpha_0, damping, start, back[k], got_back[k]) for k in chunks
    ])
    pieces = [reduce_field(keeps[k], got[k], (norms[k],)) for k in chunks]
    scaled, stats = zip(*[
        sensor_call(plan, k, meta, weights, pieces[k], norms[k], alpha_0, damping_row, field[k])
        for k in chunks
    ])
    near_1 = total_near(sum(stats), True)
    outs, sums = both_products(scaled, near_1, True, lambda k, out: (to_pair(out[0]),))
    norm_1 = sums[0]
    beta = norm_1 / norm_0
    curve_1 = sums[1] + 2.0 * beta * sums[2] + beta * beta * curve_0
    alpha_1 = norm_1 / curve_1

    final = [mine + rest[0].astype(F32) for (_, mine), rest in outs]
    residual, image_0 = jnp.concatenate(residual), jnp.concatenate(image_0)
    image_1 = jnp.concatenate(final) + damping[:, None, None] * residual + beta * image_0
    solution = alpha_0 * start + alpha_1 * (residual + beta * start)
    residual = residual - alpha_1 * image_1
    return solution.reshape(right_side.shape), residual.reshape(right_side.shape)


def solution(mesh):
    in_specs = (
        P(None, None, "sens", "src"),
        P("sens", None, None, "src"),
        P("src", "sens"),
        P("sens"),
    )
    out_specs = (P("sens", None, None, "src"), P("sens", None, None, "src"))
    shard = functools.partial(body, mesh.shape["sens"], mesh.shape["src"])
    return jax.shard_map(shard, mesh=mesh, in_specs=in_specs, out_specs=out_specs, check_vma=False)
```
